32 devices in a mesh: req: 4 (over x, core), exp: 8 (over z, y).
Axes of the slice: x: 2, y: 2, z: 4, core: 2. Of those that a mesh axis runs over, the one named last changes fastest.
Arguments:
- residual: bfloat16 [1024, 2048], P('exp'), may hold values from -6 to 6
- queries: bfloat16 [1024, 2048], P('exp', 'req'), may hold values from -128 to 128, as said below
- prefix_kv: bfloat16 [4, 2048, 256], P('req', 'exp'), may hold values from -4.5 to 4.5
- suffix_kv: bfloat16 [1024, 4, 256], P('exp', 'req'), may hold values from -6 to 6
- suffix_lengths: int32 [8, 4], P('exp'), may hold values from 1 to 96, 128 in all within a row
- out_proj: bfloat16 [2048, 2048], P('req'), may hold values from -0.5 to 0.5
- norm_gain: bfloat16 [2048], replicated, may hold values from 0.099609375 to 1.8984375
- routes: int32 [1024, 6], P('exp'), may hold values from 0 to 7, all different within a row; in each aligned block of 128 rows (0 to 127, 128 to 255, ...) at most 128 rows name the same one
- route_weights: float32 [1024, 6], P('exp'), may hold values from 0.1 to 0.5
- expert_gate: bfloat16 [8, 2048, 1408], P('exp', None, 'req'), may hold values from -0.125 to 0.125
- expert_up: bfloat16 [8, 2048, 1408], P('exp', None, 'req'), may hold values from -0.125 to 0.125
- expert_down: bfloat16 [8, 1408, 2048], P('exp', 'req'), may hold values from -0.15625 to 0.15625
- shared_gate: bfloat16 [2048, 1408], P(None, 'req'), may hold values from -0.125 to 0.125
- shared_up: bfloat16 [2048, 1408], P(None, 'req'), may hold values from -0.125 to 0.125
- shared_down: bfloat16 [1408, 2048], P('req'), may hold values from -0.15625 to 0.15625
Outputs:
- layer_out: bfloat16 [1024, 2048], P('exp')
The draws below stay inside these ranges and needn't reach their ends.
Inputs may be any that keep to these rules, and one draw needn't show every extreme that they name: In the hidden draw some queries are strong multiples of prefix keys. `suffix_lengths`: each row (the requests of one index of exp) sums to 128, and in every row one request has exactly 96 tokens. `routes`: the 6 experts of a token are different. Among the 128 tokens of one index of exp no expert is picked more than 128 times, and in every draw some expert is picked exactly 128 times by the tokens of some index of exp.
All inputs are finite; a program needn't handle non-finite values.
Results may differ from the reference program's by a relative error of at most 0.015.
Values may be sent and summed in bfloat16 or wider, within the bound.
No kernel may reach another device: no remote copies, remote signals or barrier semaphores. Data moves between devices by JAX's collectives and lax.ppermute only.
A program may use at most 128 MiB of HBM per device.

```python
import math
import jax
import jax.numpy as jnp
import numpy as np
from jax import lax

D = 2048
H = 16
KVH = 4
HD = 128
FF_EXP = 1408
TOP = 6
SHARED = 1408
TOK_DEV = 128
REQS_DEV = 4
EXPERTS = 8
LONGEST = 96
CAP = 128
TOKENS = 1024
PREFIX = 2048
N_REQ = 4
N_EXP = 8


def prefix_table(key):
    sample_base = jax.random.normal(jax.random.fold_in(key, 11), (KVH, PREFIX, 2 * HD), jnp.float32)
    sample_base = jnp.clip(sample_base, -4.5, 4.5)
    return sample_base


def draw_prefix_kv(key, part):
    return prefix_table(key).astype(jnp.bfloat16)


def draw_queries(key, part):
    sample_base = 2.5 * jax.random.normal(jax.random.fold_in(key, 12), (TOKENS, H * HD), jnp.float32)
    return jnp.clip(sample_base, -128.0, 128.0).astype(jnp.bfloat16)


def shard_levels(key, shape, shards, least, high):
    level = 1.0
    for dim, parts in shards:
        heights = jax.random.uniform(jax.random.fold_in(jax.random.fold_in(key, 6), dim), (parts,), jnp.float32, least / len(shards), high / len(shards))
        level = level * jnp.repeat(jnp.exp(heights), shape[dim] // parts).reshape((-1,) + (1,) * (len(shape) - 1 - dim))
    return level


def length_profile(amount, total, bound, skew):
    portions = [(1 << 20) // math.isqrt(rank ** skew) + 1 for rank in range(2, amount + 1)]
    surplus, holding = total - bound - (amount - 1), [1] * (amount - 1)
    while surplus > 0:
        candidates = [i for i in range(amount - 1) if holding[i] < bound]
        mass, left = sum([portions[i] for i in candidates]), surplus
        for i in candidates:
            extra = min(bound - holding[i], max(1, left * portions[i] // mass), surplus)
            holding[i] = holding[i] + extra
            surplus = surplus - extra
    return np.array([bound] + holding)


def uneven_parts(own_key, count, total, limit, skew):
    if count == 2:
        one = jax.random.randint(own_key, (), max(1, total - limit), min(limit, total - 1) + 1)
        return jnp.stack([one, total - one])
    tallies = jnp.asarray(length_profile(count, total, limit, skew), jnp.int32)
    twos = (count - 1) // 2
    donor, receiver = tallies[1:1 + 2 * twos:2], tallies[2:2 + 2 * twos:2]
    room = jnp.minimum(donor - 1, limit - receiver)
    shifted = jax.random.randint(jax.random.fold_in(own_key, 1), (twos,), 0, 1 << 20) % (room + 1)
    tallies = tallies.at[1:1 + 2 * twos:2].set(donor - shifted).at[2:2 + 2 * twos:2].set(receiver + shifted)
    return tallies[jax.random.permutation(jax.random.fold_in(own_key, 2), count)]


def routed_block(rng, own, number, rows, amount, top, reach, lean):
    order = jax.random.permutation(rng, amount)
    crowded, ordinary = portions_of(amount, rows * top, reach, lean, True), portions_of(amount, rows * top, reach, lean, False)
    places = jnp.arange(amount)

    def named(lengths, rotation):
        used = int((lengths > 0).sum())
        fixed = max(1, used // 4)
        shifted = fixed + (places - fixed + rotation * (used - fixed)) % max(1, amount - fixed)
        return jnp.zeros((amount,), jnp.int32).at[order[jnp.where(places < fixed, places, shifted)]].set(jnp.asarray(lengths, jnp.int32))

    lengths = jnp.where(number % 4 == 0, named(crowded, number // 4), named(ordinary, number - number // 4 - 1))
    mixed = jax.random.permutation(jax.random.fold_in(own, 3), amount)
    giver, receiver = mixed[0:amount // 2 * 2:2], mixed[1:amount // 2 * 2:2]
    slack = jnp.minimum(lengths[giver] - 1, reach - lengths[receiver]) // 2
    slack = jnp.where((giver == order[0]) | (receiver == order[0]) | (lengths[receiver] == 0), 0, jnp.maximum(slack, 0))
    shifted = jax.random.randint(jax.random.fold_in(own, 4), (amount // 2,), 0, 1 << 20) % (slack + 1)
    lengths = lengths.at[giver].add(-shifted).at[receiver].add(shifted)
    items = jnp.searchsorted(jnp.cumsum(lengths), jnp.arange(rows * top), side="right").astype(jnp.int32)
    listing = items.reshape(top, rows).T
    listing = listing[jax.random.permutation(jax.random.fold_in(own, 1), rows)]
    rotation = jax.random.randint(jax.random.fold_in(own, 2), (rows, 1), 0, top)
    return jnp.take_along_axis(listing, (jnp.arange(top)[None, :] + rotation) % top, axis=1)


def portions_of(count, total, limit, slope, full):
    portions = [(1 << 20) // math.isqrt(standing ** slope) + 1 for standing in range(1, count + 1)]
    largest = limit if full else min(limit, max(-(-total // count), total * portions[0] // sum(portions)))
    least = 1 if total - largest >= count - 1 else 0
    given, surplus = [largest] + [least] * (count - 1), total - largest - least * (count - 1)
    while surplus > 0:
        movable = [i for i in range(1, count) if given[i] < largest] or [i for i in range(1, count) if given[i] < limit]
        whole, left = sum([portions[i] for i in movable]), surplus
        for i in movable:
            extra = min(limit - given[i], max(1, left * portions[i] // whole), surplus)
            given[i] = given[i] + extra
            surplus = surplus - extra
    return np.array(given)


def bell_draw(own_key, extent, deviation, bound, pieces=(), kind=jnp.bfloat16):
    gain = shard_levels(own_key, extent, pieces, -0.22, 0.18) if pieces else 1.0
    values = jax.random.normal(own_key, extent, jnp.float32) * deviation * gain
    return jnp.minimum(jnp.maximum(values, -bound), bound).astype(kind)


def setup_inputs(seed: int = 0) -> dict:
    streams_of = jax.random.split(jax.random.key(seed), 16)
    residual = bell_draw(streams_of[0], (TOKENS, D), 1.0, 6.0, ((0, 8),))
    queries = draw_queries(jax.random.fold_in(streams_of[15], 71), 0)
    prefix_kv = draw_prefix_kv(jax.random.fold_in(streams_of[15], 71), 0)
    suffix_kv = bell_draw(streams_of[3], (TOKENS, KVH, 2 * HD), 1.0, 6.0, ((0, 8), (1, 4)))
    suffix_lengths = jax.vmap(lambda own: uneven_parts(own, REQS_DEV, TOK_DEV, LONGEST, 2))(jax.random.split(streams_of[4], N_EXP)).reshape((N_EXP, REQS_DEV)).astype(jnp.int32)
    out_proj = bell_draw(streams_of[5], (H * HD, D), HD ** -0.5, 0.5, ((0, 4),))
    norm_gain = jnp.clip(1.0 + 0.18 * jax.random.normal(streams_of[6], (D,), jnp.float32), 0.099609375, 1.8984375).astype(jnp.bfloat16)
    routes_keys = jax.random.split(jax.random.fold_in(streams_of[7], 1), TOKENS // TOK_DEV)
    routes_turns = jax.random.permutation(jax.random.fold_in(streams_of[7], 3), TOKENS // TOK_DEV)
    routes = jax.vmap(lambda own, number: routed_block(jax.random.fold_in(streams_of[7], 2), own, number, TOK_DEV, EXPERTS, TOP, CAP, 2))(routes_keys, routes_turns).reshape((TOKENS, TOP))
    route_weights = jnp.clip(0.1 + 0.4 * jax.random.uniform(streams_of[8], (TOKENS, TOP), jnp.float32) ** shard_levels(streams_of[8], (TOKENS, TOP), ((0, 8),), -0.2, 0.2), 0.1, 0.5)
    expert_gate = bell_draw(streams_of[9], (EXPERTS, D, FF_EXP), D ** -0.5, 0.125, ((0, 8), (2, 4)))
    expert_up = bell_draw(streams_of[10], (EXPERTS, D, FF_EXP), D ** -0.5, 0.125, ((0, 8), (2, 4)))
    expert_down = bell_draw(streams_of[11], (EXPERTS, FF_EXP, D), FF_EXP ** -0.5, 0.15625, ((0, 8), (1, 4)))
    shared_gate = bell_draw(streams_of[12], (D, SHARED), D ** -0.5, 0.125, ((1, 4),))
    shared_up = bell_draw(streams_of[13], (D, SHARED), D ** -0.5, 0.125, ((1, 4),))
    shared_down = bell_draw(streams_of[14], (SHARED, D), SHARED ** -0.5, 0.15625, ((0, 4),))
    return {"residual": residual, "queries": queries, "prefix_kv": prefix_kv, "suffix_kv": suffix_kv, "suffix_lengths": suffix_lengths, "out_proj": out_proj, "norm_gain": norm_gain, "routes": routes, "route_weights": route_weights, "expert_gate": expert_gate, "expert_up": expert_up, "expert_down": expert_down, "shared_gate": shared_gate, "shared_up": shared_up, "shared_down": shared_down}


neg_big = -1e+30
norm_eps = 1e-06

def reference(residual, queries, prefix_kv, suffix_kv, suffix_lengths, out_proj, norm_gain, routes, route_weights, expert_gate, expert_up, expert_down, shared_gate, shared_up, shared_down):
    group_size = H // KVH
    scaling = 1.0 / HD ** 0.5
    prefix_keys = prefix_kv[:, :, :HD].astype(jnp.float32)
    prefix_vals = prefix_kv[:, :, HD:].astype(jnp.float32)

    def column_attention(packed):
        query_col, suffix_col, length_col = packed
        query_heads = query_col.astype(jnp.float32).reshape(TOK_DEV, KVH, group_size, HD)
        suffix_keys = jnp.transpose(suffix_col[:, :, :HD].astype(jnp.float32), (1, 0, 2))
        suffix_vals = jnp.transpose(suffix_col[:, :, HD:].astype(jnp.float32), (1, 0, 2))
        keys_all = jnp.concatenate([prefix_keys, suffix_keys], axis=1)
        vals_all = jnp.concatenate([prefix_vals, suffix_vals], axis=1)
        scores = jnp.einsum('tgjd,gkd->gjtk', query_heads, keys_all) * scaling
        request_ends = jnp.cumsum(length_col)
        positions = jnp.arange(TOK_DEV, dtype=jnp.int32)
        request_ids = lax.optimization_barrier(jnp.sum((positions[:, None] >= request_ends[None, :]).astype(jnp.int32), axis=1))
        allowed = (request_ids[:, None] == request_ids[None, :]) & (positions[None, :] <= positions[:, None])
        allowed_all = jnp.concatenate([jnp.ones((TOK_DEV, PREFIX), dtype=bool), allowed], axis=1)
        scores = jnp.where(allowed_all[None, None], scores, neg_big)
        row_max = lax.optimization_barrier(jnp.max(scores, axis=-1, keepdims=True))
        exp_scores = jnp.exp(scores - row_max)
        row_sum = lax.optimization_barrier(jnp.sum(exp_scores, axis=-1))
        exp_weights = lax.optimization_barrier(exp_scores.astype(jnp.bfloat16)).astype(jnp.float32)
        attended = jnp.einsum('gjtk,gkd->tgjd', exp_weights, vals_all)
        attended = attended / jnp.transpose(row_sum, (2, 0, 1))[..., None]
        return attended.reshape(TOK_DEV, H * HD).astype(jnp.bfloat16)
    query_cols = queries.reshape(N_EXP, TOK_DEV, H * HD)
    suffix_cols = suffix_kv.reshape(N_EXP, TOK_DEV, KVH, 2 * HD)
    attention = lax.map(column_attention, (query_cols, suffix_cols, suffix_lengths)).reshape(TOKENS, H * HD)
    attn_out = jnp.dot(attention, out_proj, preferred_element_type=jnp.float32)
    hidden_state = (residual.astype(jnp.float32) + attn_out).astype(jnp.bfloat16)
    hidden_float = hidden_state.astype(jnp.float32)
    mean_square = lax.optimization_barrier(jnp.mean(hidden_float * hidden_float, axis=-1, keepdims=True))
    normed = (hidden_float * lax.rsqrt(mean_square + norm_eps) * norm_gain.astype(jnp.float32)).astype(jnp.bfloat16)
    shared_gate_act = jnp.dot(normed, shared_gate, preferred_element_type=jnp.float32)
    shared_up_act = jnp.dot(normed, shared_up, preferred_element_type=jnp.float32)
    shared_hidden = (jax.nn.silu(shared_gate_act) * shared_up_act).astype(jnp.bfloat16)
    shared_out = jnp.dot(shared_hidden, shared_down, preferred_element_type=jnp.float32)
    pick_ids = routes.reshape(-1).astype(jnp.int32)
    pick_tokens = (jnp.arange(TOKENS * TOP, dtype=jnp.int32) // TOP).astype(jnp.int32)
    pick_weights = route_weights.reshape(-1).astype(jnp.float32)
    one_hot = (pick_ids[:, None] == jnp.arange(EXPERTS, dtype=jnp.int32)[None, :]).astype(jnp.int32)
    pick_ranks = lax.optimization_barrier(jnp.sum((jnp.cumsum(one_hot, axis=0) - one_hot) * one_hot, axis=1)).astype(jnp.int32)
    slots_per = N_EXP * CAP
    token_table = jnp.full((EXPERTS, slots_per), TOKENS, dtype=jnp.int32).at[pick_ids, pick_ranks].set(pick_tokens)
    weight_table = jnp.zeros((EXPERTS, slots_per), jnp.float32).at[pick_ids, pick_ranks].set(pick_weights)
    normed_pad = jnp.concatenate([normed, jnp.zeros((1, D), normed.dtype)], axis=0)
    block_len = FF_EXP // N_REQ

    def expert_step(carried, packed):
        gate_w, up_w, down_w, token_ids, weight_ids = packed
        source_rows = normed_pad[token_ids]
        gate_act = jnp.dot(source_rows, gate_w, preferred_element_type=jnp.float32)
        up_act = jnp.dot(source_rows, up_w, preferred_element_type=jnp.float32)
        expert_hidden = (jax.nn.silu(gate_act) * up_act).astype(jnp.bfloat16)
        summed = jnp.zeros((slots_per, D), jnp.float32)
        for block_id in range(N_REQ):
            slice_out = jnp.dot(expert_hidden[:, block_id * block_len:(block_id + 1) * block_len], down_w[block_id * block_len:(block_id + 1) * block_len], preferred_element_type=jnp.float32).astype(jnp.bfloat16)
            summed = summed + slice_out.astype(jnp.float32)
        return (carried.at[token_ids].add(summed * weight_ids[:, None]), None)
    routed, unused = lax.scan(expert_step, jnp.zeros((TOKENS + 1, D), jnp.float32), (expert_gate, expert_up, expert_down, token_table, weight_table))
    return (hidden_float + shared_out + routed[:TOKENS]).astype(jnp.bfloat16)
```

```python
import functools
import math

import jax
import jax.numpy as jnp
from jax import lax
from jax.experimental import pallas as pl
from jax.experimental.pallas import tpu as pltpu
from jax.sharding import PartitionSpec as P

HD = 128
TOP = 6

neg_big = -1e30
norm_eps = 1e-06
f32 = jnp.float32
bf16 = jnp.bfloat16


def dot(a, b):
    return jnp.dot(a, b, preferred_element_type=f32)


def expert_capacity(tokens_here, experts):
    return min(tokens_here, 4 * ((tokens_here * TOP + 2 * experts - 1) // (2 * experts)))


def attend_kernel(heads, tokens, page_len, page_count, first, last, *refs):
    refs = list(refs)
    q_ref = refs.pop(0)
    if first:
        lengths_ref, suffix_ref = refs.pop(0), refs.pop(0)
    else:
        max_in, sum_in, acc_in = refs.pop(0), refs.pop(0), refs.pop(0)
    if last:
        core_ref = refs.pop(0)
    page_refs = [refs.pop(0) for _ in range(page_count)]
    scaling = 1.0 / math.sqrt(HD)
    q = jnp.concatenate([q_ref[:, h * HD : (h + 1) * HD] for h in range(heads)], axis=0)
    blocks = [(ref[:page_len, :HD], ref[:page_len, HD:]) for ref in page_refs]
    scores = [
        lax.dot_general(q, k, (((1,), (1,)), ((), ())), preferred_element_type=f32) * scaling
        for k, _ in blocks
    ]
    if first:
        ends, total = [], 0
        for i in range(lengths_ref.shape[1]):
            total = total + lengths_ref[0, i]
            ends.append(total)
        rows = lax.broadcasted_iota(jnp.int32, (tokens, tokens), 0)
        cols = lax.broadcasted_iota(jnp.int32, (tokens, tokens), 1)
        row_ids = sum((rows >= e).astype(jnp.int32) for e in ends)
        col_ids = sum((cols >= e).astype(jnp.int32) for e in ends)
        bias = jnp.where((row_ids == col_ids) & (cols <= rows), 0.0, neg_big).astype(f32)
        k, v = suffix_ref[:, :HD], suffix_ref[:, HD:]
        own = lax.dot_general(q, k, (((1,), (1,)), ((), ())), preferred_element_type=f32) * scaling
        own = jnp.where(jnp.concatenate([bias] * heads, axis=0) < 0.0, neg_big, own)
        scores.append(own)
        blocks.append((k, v))
    new_max = functools.reduce(
        jnp.maximum, [jnp.max(s, axis=-1, keepdims=True) for s in scores]
    )
    if not first:
        old_max = max_in[:, :1]
        new_max = jnp.maximum(new_max, old_max)
        factor = jnp.exp(old_max - new_max)
        total = sum_in[:, :1] * factor
        acc = acc_in[...] * factor
    else:
        total, acc = 0.0, 0.0
    for s, (_, v) in zip(scores, blocks):
        e = jnp.exp(s - new_max)
        total = total + jnp.sum(e, axis=-1, keepdims=True)
        acc = acc + jnp.dot(e.astype(bf16), v, preferred_element_type=f32)
    if last:
        keep_ref, send_ref = refs
        half = tokens // 2
        out = (acc / total).astype(bf16)
        second = core_ref[0] == 1
        for h in range(heads):
            low = out[h * tokens : h * tokens + half]
            high = out[h * tokens + half : (h + 1) * tokens]
            keep_ref[:, h * HD : (h + 1) * HD] = jnp.where(second, high, low)
            send_ref[:, h * HD : (h + 1) * HD] = jnp.where(second, low, high)
    else:
        max_out, sum_out, acc_out = refs
        max_out[...] = jnp.broadcast_to(new_max, max_out.shape)
        sum_out[...] = jnp.broadcast_to(total, sum_out.shape)
        acc_out[...] = acc


def attend(queries, pages, page_len, state=None, suffix=None, core=None):
    tokens, width = queries.shape
    heads = width // HD
    first, last = state is None, core is not None
    vmem, smem = pl.BlockSpec(memory_space=pltpu.VMEM), pl.BlockSpec(memory_space=pltpu.SMEM)
    args, specs = [queries], [vmem]
    if first:
        args += list(suffix)
        specs += [smem, vmem]
    else:
        args += list(state)
        specs += [vmem] * 3
    if last:
        args.append(core)
        specs.append(smem)
    args += pages
    specs += [vmem] * len(pages)
    if last:
        outs = [jax.ShapeDtypeStruct((tokens // 2, width), bf16)] * 2
    else:
        outs = [jax.ShapeDtypeStruct((heads * tokens, HD), f32)] * 3
    keys = sum(page_len for _ in pages) + (tokens if first else 0)
    return pl.pallas_call(
        functools.partial(attend_kernel, heads, tokens, page_len, len(pages), first, last),
        out_shape=outs,
        in_specs=specs,
        out_specs=[vmem] * len(outs),
        compiler_params=pltpu.CompilerParams(vmem_limit_bytes=32 << 20),
        cost_estimate=pl.CostEstimate(
            flops=4 * heads * tokens * keys * HD,
            bytes_accessed=4 * keys * HD + 2 * tokens * width,
            transcendentals=heads * tokens * keys,
        ),
    )(*args)


def on_device_ring(
    residual,
    queries,
    prefix_kv,
    suffix_kv,
    suffix_lengths,
    out_proj,
    norm_gain,
    routes,
    route_weights,
    expert_gate,
    expert_up,
    expert_down,
    shared_gate,
    shared_up,
    shared_down,
):
    tokens, width = residual.shape
    half = tokens // 2
    n = lax.axis_size("exp")
    steps = n // 2
    order = list(range(0, n, 2)) + list(range(n - 1, 0, -2))
    right = [(order[k], order[(k + 1) % n]) for k in range(n)]
    left = [(b, a) for a, b in right]
    req = lax.axis_size("req")
    sibling = [(i, i ^ 1) for i in range(req)]
    across = [(i, i ^ 2) for i in range(req)]
    core = lax.rem(lax.axis_index("req"), 2)
    me = lax.axis_index("exp")

    def half_of(x):
        return lax.dynamic_slice_in_dim(x, core * half, half, 0)

    slots = jnp.arange(n, dtype=jnp.int32)
    dense = jnp.sum(
        jnp.where(routes.T[None] == slots[:, None, None], route_weights.T[None], 0.0), axis=1
    )
    head = lax.reduce_precision(dense, 8, 7)
    rest = lax.reduce_precision(dense - head, 8, 7)
    gates = jnp.concatenate([head, rest], axis=1).astype(bf16)
    page_len = prefix_kv.shape[1]
    pad = -n % 16
    page = jnp.concatenate([prefix_kv[0], gates, jnp.zeros((pad, gates.shape[1]), bf16)], axis=0)

    out_proj_sib = lax.ppermute(out_proj, "req", sibling)
    shared_gate_sib = lax.ppermute(shared_gate, "req", sibling)
    shared_up_sib = lax.ppermute(shared_up, "req", sibling)
    shared_down_sib = lax.ppermute(shared_down, "req", sibling)
    gate_sib = lax.ppermute(expert_gate[0], "req", sibling)
    up_sib = lax.ppermute(expert_up[0], "req", sibling)
    down_sib = lax.ppermute(expert_down[0], "req", sibling)

    suffix = (suffix_lengths, suffix_kv[:, 0])
    core_arr = jnp.reshape(core, (1,)).astype(jnp.int32)
    gate_rows = {0: gates}
    from_left, from_right = page, page
    state = None
    arrived = [page]
    cut = (page_len // 2)
    for s in range(1, steps + 1):
        if s < steps:
            from_left = lax.ppermute(from_left, "exp", right)
            from_right = lax.ppermute(from_right, "exp", left)
            now = [from_left, from_right]
            gate_rows[s] = from_left[page_len : page_len + n]
            gate_rows[-s] = from_right[page_len : page_len + n]
        else:
            low = lax.ppermute(from_left[:cut], "exp", right)
            high = lax.ppermute(from_right[cut:], "exp", left)
            gate_rows[s] = high[page_len - cut : page_len - cut + n]
            now = [low, high[: page_len - cut]]
        if s == 1:
            arrived += now
            state = attend(queries, arrived, page_len, suffix=suffix)
        elif s < steps:
            state = attend(queries, now, page_len, state=state)
        else:
            keep, send = attend(queries, now, cut, state=state, core=core_arr)

    other = lax.ppermute(send, "req", sibling)
    terms = (dot(keep, out_proj) + dot(other, out_proj_sib)).astype(bf16)
    terms_across = lax.ppermute(terms, "req", across)
    hidden_state = (
        half_of(residual).astype(f32) + (terms.astype(f32) + terms_across.astype(f32))
    ).astype(bf16)
    hidden_float = hidden_state.astype(f32)
    mean_square = jnp.mean(hidden_float * hidden_float, axis=-1, keepdims=True)
    normed = (
        hidden_float * lax.rsqrt(mean_square + norm_eps) * norm_gain.astype(f32)
    ).astype(bf16)

    def glu(rows, weights, scale):
        total = 0.0
        for gate, up, down in weights:
            hidden = (jax.nn.silu(dot(rows, gate)) * dot(rows, up)).astype(bf16)
            total = total + dot(hidden, down)
        return total if scale is None else total * scale

    shared_weights = [
        (shared_gate, shared_up, shared_down),
        (shared_gate_sib, shared_up_sib, shared_down_sib),
    ]
    expert_weights = [
        (expert_gate[0], expert_up[0], expert_down[0]),
        (gate_sib, up_sib, down_sib),
    ]
    shared_part = glu(normed, shared_weights, None)

    def scale_of(distance):
        row = lax.dynamic_slice_in_dim(gate_rows[distance], me, 1, 0)[0].astype(f32)
        return half_of(row[:tokens] + row[tokens:])

    def experts(blocks):
        rows = jnp.concatenate([b for _, b in blocks], axis=0)
        scale = jnp.concatenate([scale_of(d) for d, _ in blocks])[:, None]
        out = glu(rows, expert_weights, scale).astype(bf16)
        return {d: out[i * half : (i + 1) * half] for i, (d, _) in enumerate(blocks)}

    parts = {}
    from_left, from_right = normed, normed
    quarter = half // 2
    for s in range(1, steps + 1):
        if s < steps:
            from_left = lax.ppermute(from_left, "exp", right)
            from_right = lax.ppermute(from_right, "exp", left)
            now = [(s, from_left), (-s, from_right)]
            if s == 1:
                now = [(0, normed)] + now
        else:
            low = lax.ppermute(from_left[:quarter], "exp", right)
            high = lax.ppermute(from_right[quarter:], "exp", left)
            now = [(s, jnp.concatenate([low, high], axis=0))]
        parts.update(experts(now))

    def add(a, b):
        return (a.astype(f32) + b.astype(f32)).astype(bf16)

    to_right = lax.ppermute(parts[steps][:quarter], "exp", right)
    to_left = lax.ppermute(parts[steps][quarter:], "exp", left)
    for k in range(steps - 1, 0, -1):
        a, b = parts[-k], parts[k]
        if k == steps - 1:
            a = jnp.concatenate([add(a[:quarter], to_right), a[quarter:]], axis=0)
            b = jnp.concatenate([b[:quarter], add(b[quarter:], to_left)], axis=0)
        else:
            a, b = add(a, to_right), add(b, to_left)
        to_right = lax.ppermute(a, "exp", right)
        to_left = lax.ppermute(b, "exp", left)
    routed = parts[0].astype(f32) + (to_right.astype(f32) + to_left.astype(f32))
    summed = (shared_part + routed).astype(bf16)
    summed_across = lax.ppermute(summed, "req", across)
    mine = (hidden_float + (summed.astype(f32) + summed_across.astype(f32))).astype(bf16)
    theirs = lax.ppermute(mine, "req", sibling)
    first = core == 0
    return jnp.concatenate(
        [jnp.where(first, mine, theirs), jnp.where(first, theirs, mine)], axis=0
    )


def on_device(
    residual,
    queries,
    prefix_kv,
    suffix_kv,
    suffix_lengths,
    out_proj,
    norm_gain,
    routes,
    route_weights,
    expert_gate,
    expert_up,
    expert_down,
    shared_gate,
    shared_up,
    shared_down,
):
    tokens_here = residual.shape[0]
    feat_width = residual.shape[1]
    head_count = queries.shape[1] // HD
    scaling = 1.0 / math.sqrt(HD)
    query_heads = jnp.transpose(queries.reshape(tokens_here, head_count, HD), (1, 0, 2))
    start_state = (
        jnp.full((head_count, tokens_here), neg_big, jnp.float32),
        jnp.zeros((head_count, tokens_here), jnp.float32),
        jnp.zeros((head_count, tokens_here, HD), jnp.float32),
    )

    def absorb(carried, key_rows, value_rows, allowed):
        running_max, running_sum, running_acc = carried
        scores = (
            jnp.einsum("htd,kd->htk", query_heads, key_rows, preferred_element_type=jnp.float32)
            * scaling
        )
        if allowed is not None:
            scores = jnp.where(allowed[None], scores, neg_big)
        new_max = jnp.maximum(running_max, jnp.max(scores, axis=-1))
        factor = jnp.exp(running_max - new_max)
        exp_scores = jnp.exp(scores - new_max[..., None])
        new_sum = running_sum * factor + jnp.sum(exp_scores, axis=-1)
        new_acc = running_acc * factor[..., None] + jnp.einsum(
            "htk,kd->htd",
            exp_scores.astype(jnp.bfloat16),
            value_rows,
            preferred_element_type=jnp.float32,
        )
        return (new_max, new_sum, new_acc)

    portion = lax.all_gather(prefix_kv, "exp", axis=1, tiled=True)
    key_count = portion.shape[1]
    window_len = math.gcd(key_count, 2048)

    def inner(position, inner_state):
        window = lax.dynamic_slice_in_dim(portion[0], position * window_len, window_len, 0)
        return absorb(inner_state, window[:, :HD], window[:, HD:], None)

    carried = lax.fori_loop(0, key_count // window_len, inner, start_state)
    request_ends = jnp.cumsum(suffix_lengths[0])
    positions = jnp.arange(tokens_here, dtype=jnp.int32)
    request_ids = jnp.sum((positions[:, None] >= request_ends[None, :]).astype(jnp.int32), axis=1)
    allowed = (request_ids[:, None] == request_ids[None, :]) & (
        positions[None, :] <= positions[:, None]
    )
    carried = absorb(carried, suffix_kv[:, 0, :HD], suffix_kv[:, 0, HD:], allowed)
    running_max, running_sum, running_acc = carried
    attention = (
        jnp.transpose(running_acc / running_sum[..., None], (1, 0, 2))
        .reshape(tokens_here, head_count * HD)
        .astype(jnp.bfloat16)
    )
    attn_terms = jnp.dot(attention, out_proj, preferred_element_type=jnp.float32)
    attn_out = lax.psum(attn_terms.astype(jnp.bfloat16), "req").astype(jnp.float32)
    hidden_state = (residual.astype(jnp.float32) + attn_out).astype(jnp.bfloat16)
    hidden_float = hidden_state.astype(jnp.float32)
    mean_square = jnp.mean(hidden_float * hidden_float, axis=-1, keepdims=True)
    normed = (
        hidden_float * lax.rsqrt(mean_square + norm_eps) * norm_gain.astype(jnp.float32)
    ).astype(jnp.bfloat16)
    shared_gate_act = jnp.dot(normed, shared_gate, preferred_element_type=jnp.float32)
    shared_up_act = jnp.dot(normed, shared_up, preferred_element_type=jnp.float32)
    shared_hidden = (jax.nn.silu(shared_gate_act) * shared_up_act).astype(jnp.bfloat16)
    shared_part = jnp.dot(shared_hidden, shared_down, preferred_element_type=jnp.float32)
    exp_count = lax.axis_size("exp")
    experts = exp_count * expert_gate.shape[0]
    capacity = expert_capacity(tokens_here, experts)
    pick_ids = routes.reshape(-1)
    one_hot = (pick_ids[:, None] == jnp.arange(experts, dtype=jnp.int32)[None, :]).astype(jnp.int32)
    pick_ranks = jnp.sum((jnp.cumsum(one_hot, axis=0) - one_hot) * one_hot, axis=1)
    pick_slots = (pick_ids * capacity + pick_ranks).reshape(tokens_here, TOP)
    slot_ids = jnp.arange(experts * capacity, dtype=jnp.int32)
    placement = jnp.any(pick_slots[None, :, :] == slot_ids[:, None, None], axis=2).astype(
        jnp.bfloat16
    )
    buffer = (
        jnp.dot(placement, normed, preferred_element_type=jnp.float32)
        .astype(jnp.bfloat16)
        .reshape(experts, capacity, feat_width)
    )
    source_rows = lax.all_to_all(buffer, "exp", split_axis=0, concat_axis=0, tiled=True)
    sources, slot_count, row_width = source_rows.shape
    flat_rows = source_rows.reshape(sources * slot_count, row_width)
    gate_act = jnp.dot(flat_rows, expert_gate[0], preferred_element_type=jnp.float32)
    up_act = jnp.dot(flat_rows, expert_up[0], preferred_element_type=jnp.float32)
    expert_hidden = (jax.nn.silu(gate_act) * up_act).astype(jnp.bfloat16)
    partial_out = jnp.dot(expert_hidden, expert_down[0], preferred_element_type=jnp.float32).astype(
        jnp.bfloat16
    )
    finish_partial_out = partial_out.reshape(sources, slot_count, row_width)
    returned = lax.all_to_all(finish_partial_out, "exp", split_axis=0, concat_axis=0, tiled=True)
    flat_back = returned.reshape(experts * capacity, feat_width)
    picked_rows = (
        flat_back[pick_slots.reshape(-1)].astype(jnp.float32).reshape(tokens_here, TOP, feat_width)
    )
    routed = jnp.sum(picked_rows * route_weights[:, :, None], axis=1)
    summed = lax.psum((shared_part + routed).astype(jnp.bfloat16), "req").astype(jnp.float32)
    return (hidden_float + summed).astype(jnp.bfloat16)


def solution(mesh):
    placed = (
        P("exp", None),
        P("exp", "req"),
        P("req", "exp", None),
        P("exp", "req", None),
        P("exp", None),
        P("req", None),
        P(),
        P("exp", None),
        P("exp", None),
        P("exp", None, "req"),
        P("exp", None, "req"),
        P("exp", "req", None),
        P(None, "req"),
        P(None, "req"),
        P("req", None),
    )

    def program(residual, *rest):
        n_exp, n_req = mesh.shape["exp"], mesh.shape["req"]
        tokens_here = residual.shape[0] // n_exp
        experts = rest[8].shape[0]
        every_row = expert_capacity(tokens_here, experts) == tokens_here
        ring = every_row and experts == n_exp and n_req == 4 and n_exp % 2 == 0 and n_exp >= 4
        return jax.shard_map(
            on_device_ring if ring else on_device,
            mesh=mesh,
            in_specs=placed,
            out_specs=P("exp", None),
            check_vma=False,
        )(residual, *rest)

    return program
```

```python
import functools
import math

import jax
import jax.numpy as jnp
from jax import lax
from jax.experimental import pallas as pl
from jax.experimental.pallas import tpu as pltpu
from jax.sharding import PartitionSpec as P

HD = 128
TOP = 6

neg_big = -1e30
norm_eps = 1e-06
f32 = jnp.float32
bf16 = jnp.bfloat16
STAGE_VMEM = 1 << 20
SHARED_VMEM = 8 << 20
EXPERT_VMEM = 5 << 20
COLUMNS = 512


def dot(a, b):
    return jnp.dot(a, b, preferred_element_type=f32)


def expert_capacity(tokens_here, experts):
    return min(tokens_here, 4 * ((tokens_here * TOP + 2 * experts - 1) // (2 * experts)))


def attend_kernel(heads, tokens, page_len, page_count, first, last, *refs):
    refs = list(refs)
    q_ref = refs.pop(0)
    if first:
        lengths_ref, suffix_ref = refs.pop(0), refs.pop(0)
    else:
        max_in, sum_in, acc_in = refs.pop(0), refs.pop(0), refs.pop(0)
    if last:
        core_ref, proj_ref = refs.pop(0), refs.pop(0)
    page_refs = [refs.pop(0) for _ in range(page_count)]
    if last:
        keep_ref, send_ref, proj_buf, proj_sem = refs
        fetch = pltpu.make_async_copy(proj_ref, proj_buf, proj_sem)
        fetch.start()
    scaling = 1.0 / math.sqrt(HD)
    q = jnp.concatenate([q_ref[:, h * HD : (h + 1) * HD] for h in range(heads)], axis=0)
    blocks = [(ref[:page_len, :HD], ref[:page_len, HD:]) for ref in page_refs]
    scores = [
        lax.dot_general(q, k, (((1,), (1,)), ((), ())), preferred_element_type=f32) * scaling
        for k, _ in blocks
    ]
    if first:
        ends, total = [], 0
        for i in range(lengths_ref.shape[1]):
            total = total + lengths_ref[0, i]
            ends.append(total)
        rows = lax.broadcasted_iota(jnp.int32, (tokens, tokens), 0)
        cols = lax.broadcasted_iota(jnp.int32, (tokens, tokens), 1)
        row_ids = sum((rows >= e).astype(jnp.int32) for e in ends)
        col_ids = sum((cols >= e).astype(jnp.int32) for e in ends)
        bias = jnp.where((row_ids == col_ids) & (cols <= rows), 0.0, neg_big).astype(f32)
        k, v = suffix_ref[:, :HD], suffix_ref[:, HD:]
        own = lax.dot_general(q, k, (((1,), (1,)), ((), ())), preferred_element_type=f32) * scaling
        own = jnp.where(jnp.concatenate([bias] * heads, axis=0) < 0.0, neg_big, own)
        scores.append(own)
        blocks.append((k, v))
    new_max = functools.reduce(
        jnp.maximum, [jnp.max(s, axis=-1, keepdims=True) for s in scores]
    )
    if not first:
        old_max = max_in[:, :1]
        new_max = jnp.maximum(new_max, old_max)
        factor = jnp.exp(old_max - new_max)
        total = sum_in[:, :1] * factor
        acc = acc_in[...] * factor
    else:
        total, acc = 0.0, 0.0
    for s, (_, v) in zip(scores, blocks):
        e = jnp.exp(s - new_max)
        total = total + jnp.sum(e, axis=-1, keepdims=True)
        acc = acc + jnp.dot(e.astype(bf16), v, preferred_element_type=f32)
    if last:
        out = (acc / total).astype(bf16)
        rows = jnp.concatenate([out[h * tokens : (h + 1) * tokens] for h in range(heads)], axis=1)
        half = tokens // 2
        second = core_ref[0] == 1
        fetch.wait()
        for c in range(0, proj_buf.shape[1], COLUMNS):
            cols = slice(c, c + COLUMNS)
            terms = jnp.dot(rows, proj_buf[:, cols], preferred_element_type=f32).astype(bf16)
            low, high = terms[:half], terms[half:]
            keep_ref[:, cols] = jnp.where(second, high, low)
            send_ref[:, cols] = jnp.where(second, low, high)
    else:
        max_out, sum_out, acc_out = refs
        max_out[...] = jnp.broadcast_to(new_max, max_out.shape)
        sum_out[...] = jnp.broadcast_to(total, sum_out.shape)
        acc_out[...] = acc


def attend(queries, pages, page_len, state=None, suffix=None, core=None, out_proj=None):
    tokens, width = queries.shape
    heads = width // HD
    first, last = state is None, core is not None
    vmem, smem = pl.BlockSpec(memory_space=pltpu.VMEM), pl.BlockSpec(memory_space=pltpu.SMEM)
    args, specs = [queries], [vmem]
    if first:
        args += list(suffix)
        specs += [smem, vmem]
    else:
        args += list(state)
        specs += [vmem] * 3
    if last:
        args += [core, pltpu.with_memory_space_constraint(out_proj, pltpu.HBM)]
        specs += [smem, pl.BlockSpec(memory_space=pl.ANY)]
    args += pages
    specs += [vmem] * len(pages)
    if last:
        outs = [jax.ShapeDtypeStruct((tokens // 2, out_proj.shape[1]), bf16)] * 2
        scratch = [pltpu.VMEM(out_proj.shape, bf16), pltpu.SemaphoreType.DMA(())]
    else:
        outs = [jax.ShapeDtypeStruct((heads * tokens, HD), f32)] * 3
        scratch = []
    keys = sum(page_len for _ in pages) + (tokens if first else 0)
    return pl.pallas_call(
        functools.partial(attend_kernel, heads, tokens, page_len, len(pages), first, last),
        out_shape=outs,
        in_specs=specs,
        out_specs=[vmem] * len(outs),
        scratch_shapes=scratch,
        compiler_params=pltpu.CompilerParams(vmem_limit_bytes=12 << 20),
        cost_estimate=pl.CostEstimate(
            flops=4 * heads * tokens * keys * HD,
            bytes_accessed=4 * keys * HD + 2 * tokens * width,
            transcendentals=heads * tokens * keys,
        ),
    )(*args)


def stage_kernel(*refs):
    sources, outs, sems = refs[:6], refs[6:9], refs[9]
    block = sources[0].shape[0]
    copies = [
        pltpu.make_async_copy(
            sources[i], outs[i // 2].at[pl.ds(i % 2 * block, block)], sems.at[i]
        )
        for i in range(6)
    ]
    for copy in copies:
        copy.start()
    for copy in copies:
        copy.wait()


def stage(weights):
    block, width = weights[0].shape
    return pl.pallas_call(
        stage_kernel,
        out_shape=[pltpu.VMEM((2 * block, width), bf16)] * 3,
        in_specs=[pl.BlockSpec(memory_space=pl.ANY)] * 6,
        out_specs=[pl.BlockSpec(memory_space=pltpu.VMEM)] * 3,
        scratch_shapes=[pltpu.SemaphoreType.DMA((6,))],
        compiler_params=pltpu.CompilerParams(vmem_limit_bytes=STAGE_VMEM),
        cost_estimate=pl.CostEstimate(
            flops=0, bytes_accessed=12 * block * width, transcendentals=0
        ),
    )(*[pltpu.with_memory_space_constraint(w, pltpu.HBM) for w in weights])


def fetches(sources, bufs, sems):
    block = sources[0].shape[0]
    return [
        pltpu.make_async_copy(
            sources[i], bufs[i // 2 % 2].at[pl.ds(i % 2 * block, block)], sems.at[i]
        )
        for i in range(6)
    ]


def hidden_units(x, copies, bufs):
    contract = (((1,), (1,)), ((), ()))
    for copy in copies[:4]:
        copy.start()
    for copy in copies[:2]:
        copy.wait()
    gate = lax.dot_general(x, bufs[0][...], contract, preferred_element_type=f32)
    for copy in copies[4:]:
        copy.start()
    for copy in copies[2:4]:
        copy.wait()
    up = lax.dot_general(x, bufs[1][...], contract, preferred_element_type=f32)
    hidden = (gate / (1.0 + jnp.exp(-gate)) * up).astype(bf16)
    for copy in copies[4:]:
        copy.wait()
    return hidden


def glu_call(kernel, args, specs, weights, outs, rows):
    block, width = weights[0].shape
    vmem = pl.BlockSpec(memory_space=pltpu.VMEM)
    return pl.pallas_call(
        kernel,
        out_shape=outs,
        in_specs=specs + [pl.BlockSpec(memory_space=pl.ANY)] * 6,
        out_specs=[vmem] * len(outs),
        scratch_shapes=[pltpu.VMEM((2 * block, width), bf16)] * 2
        + [pltpu.SemaphoreType.DMA((6,))],
        compiler_params=pltpu.CompilerParams(vmem_limit_bytes=SHARED_VMEM),
        cost_estimate=pl.CostEstimate(
            flops=12 * rows * width * block,
            bytes_accessed=12 * block * width,
            transcendentals=2 * rows * block,
        ),
    )(*args, *[pltpu.with_memory_space_constraint(w, pltpu.HBM) for w in weights])


def shared_kernel(x_ref, *refs):
    sources, out_ref, bufs, sems = refs[:6], refs[6], refs[7:9], refs[9]
    width = out_ref.shape[1]
    hidden = hidden_units(x_ref[:, :width], fetches(sources, bufs, sems), bufs)
    for c in range(0, width, COLUMNS):
        cols = slice(c, c + COLUMNS)
        out_ref[:, cols] = jnp.dot(hidden, bufs[0][:, cols], preferred_element_type=f32)


def shared_expert(rows, weights):
    width = weights[0].shape[1]
    outs = [jax.ShapeDtypeStruct((rows.shape[0], width), f32)]
    specs = [pl.BlockSpec(memory_space=pltpu.VMEM)]
    return glu_call(shared_kernel, [rows], specs, weights, outs, rows.shape[0])[0]


def expert_kernel(n_experts, counts, plus, *refs):
    refs = list(refs)
    place_ref = refs.pop(0)
    sources = [refs.pop(0) for _ in range(sum(counts))]
    shared_ref = refs.pop(0) if plus else None
    gate_ref, up_ref, down_ref = refs[:3]
    keeps, send_ref = refs[3:-1], refs[-1]
    width = send_ref.shape[1]
    x = jnp.concatenate([ref[:, :width] for ref in sources], axis=0)
    contract = (((1,), (1,)), ((), ()))
    gate = lax.dot_general(x, gate_ref[...], contract, preferred_element_type=f32)
    up = lax.dot_general(x, up_ref[...], contract, preferred_element_type=f32)
    hidden = (gate / (1.0 + jnp.exp(-gate)) * up).astype(bf16)
    lanes = jnp.concatenate([ref[:, width:] for ref in sources], axis=0).astype(f32)
    lane = lax.broadcasted_iota(jnp.int32, lanes.shape, 1)
    e, second = place_ref[0], place_ref[1] == 1
    scale = jnp.sum(
        jnp.where((lane == e) | (lane == e + n_experts), lanes, 0.0), axis=1, keepdims=True
    )
    part = keeps[0].shape[0]
    for c in range(0, width, COLUMNS):
        cols = slice(c, c + COLUMNS)
        out = jnp.dot(hidden, down_ref[:, cols], preferred_element_type=f32) * scale
        for i, keep_ref in enumerate(keeps):
            low = out[2 * part * i : 2 * part * i + part]
            high = out[2 * part * i + part : 2 * part * (i + 1)]
            if plus and i == 0:
                low = low + shared_ref[:part, cols]
                high = high + shared_ref[part:, cols]
            low, high = low.astype(bf16), high.astype(bf16)
            keep_ref[:, cols] = jnp.where(second, high, low)
            send_ref[part * i : part * (i + 1), cols] = jnp.where(second, low, high)


def expert(blocks, weights, n_experts, place, shared=None):
    counts = [len(b) for b in blocks]
    rows = sum(a.shape[0] for b in blocks for a in b)
    part = rows // len(blocks) // 2
    hidden, width = weights[0].shape
    vmem, smem = pl.BlockSpec(memory_space=pltpu.VMEM), pl.BlockSpec(memory_space=pltpu.SMEM)
    args = [place] + [a for b in blocks for a in b] + ([] if shared is None else [shared])
    outs = pl.pallas_call(
        functools.partial(expert_kernel, n_experts, counts, shared is not None),
        out_shape=[jax.ShapeDtypeStruct((part, width), bf16)] * len(blocks)
        + [jax.ShapeDtypeStruct((part * len(blocks), width), bf16)],
        in_specs=[smem] + [vmem] * (len(args) - 1 + 3),
        out_specs=[vmem] * (len(blocks) + 1),
        compiler_params=pltpu.CompilerParams(vmem_limit_bytes=EXPERT_VMEM),
        cost_estimate=pl.CostEstimate(
            flops=6 * rows * width * hidden,
            bytes_accessed=4 * rows * width,
            transcendentals=rows * hidden,
        ),
    )(*args, *[pltpu.with_memory_space_constraint(w, pltpu.VMEM) for w in weights])
    return outs[:-1], outs[-1]


def on_device_ring(
    residual,
    queries,
    prefix_kv,
    suffix_kv,
    suffix_lengths,
    out_proj,
    norm_gain,
    routes,
    route_weights,
    expert_gate,
    expert_up,
    expert_down,
    shared_gate,
    shared_up,
    shared_down,
):
    tokens, width = residual.shape
    half = tokens // 2
    n = lax.axis_size("exp")
    steps = n // 2
    order = list(range(0, n, 2)) + list(range(n - 1, 0, -2))
    right = [(order[k], order[(k + 1) % n]) for k in range(n)]
    left = [(b, a) for a, b in right]
    req = lax.axis_size("req")
    sibling = [(i, i ^ 1) for i in range(req)]
    across = [(i, i ^ 2) for i in range(req)]
    core = lax.rem(lax.axis_index("req"), 2)
    plane = lax.div(lax.axis_index("req"), 2)
    me = lax.axis_index("exp")

    def half_of(x):
        return lax.dynamic_slice_in_dim(x, core * half, half, 0)

    slots = jnp.arange(n, dtype=jnp.int32)
    dense = jnp.sum(
        jnp.where(half_of(routes)[:, :, None] == slots, half_of(route_weights)[:, :, None], 0.0),
        axis=1,
    )
    head = lax.reduce_precision(dense, 8, 7)
    rest = lax.reduce_precision(dense - head, 8, 7)
    gates = jnp.concatenate(
        [head, rest, jnp.zeros((half, -2 * n % HD), f32)], axis=1
    ).astype(bf16)
    page = prefix_kv[0]
    page_len = page.shape[0]

    shared_weights = (shared_gate.T, shared_up.T, shared_down)
    expert_weights = (expert_gate[0].T, expert_up[0].T, expert_down[0])

    def with_sibling(weights):
        return [w for own in weights for w in (own, lax.ppermute(own, "req", sibling))]

    shared_weights = with_sibling(shared_weights)
    expert_weights = with_sibling(expert_weights)

    suffix = (suffix_lengths, suffix_kv[:, 0])
    core_arr = jnp.reshape(core, (1,)).astype(jnp.int32)
    from_left, from_right = page, page
    cut = page_len // 2
    state = attend(queries, [page], page_len, suffix=suffix)
    for s in range(1, steps):
        from_left = lax.ppermute(from_left, "exp", right)
        from_right = lax.ppermute(from_right, "exp", left)
        from_left, state = lax.optimization_barrier((from_left, state))
        state = attend(queries, [from_left, from_right], page_len, state=state)
    low = lax.ppermute(from_left[:cut], "exp", right)
    high = lax.ppermute(from_right[cut:], "exp", left)
    low, state = lax.optimization_barrier((low, state))
    keep, send = attend(
        queries, [low, high], cut, state=state, core=core_arr, out_proj=out_proj
    )

    other = lax.ppermute(send, "req", sibling)
    terms = (keep.astype(f32) + other.astype(f32)).astype(bf16)
    terms_across = lax.ppermute(terms, "req", across)
    terms_across, staged = lax.optimization_barrier((terms_across, stage(expert_weights)))
    hidden_state = (
        half_of(residual).astype(f32) + (terms.astype(f32) + terms_across.astype(f32))
    ).astype(bf16)
    hidden_float = hidden_state.astype(f32)
    mean_square = jnp.mean(hidden_float * hidden_float, axis=-1, keepdims=True)
    normed = (
        hidden_float * lax.rsqrt(mean_square + norm_eps) * norm_gain.astype(f32)
    ).astype(bf16)

    normed = jnp.concatenate([normed, gates], axis=1)
    place = jnp.stack([me, plane]).astype(jnp.int32)

    own, summand = {}, {}
    quarter = half // 2

    def work(blocks, shared=None):
        keeps, send = expert([b for _, b in blocks], staged, n, place, shared)
        for (d, _), keep in zip(blocks, keeps):
            own[d] = keep
        got = lax.ppermute(send, "req", across)
        for i, (d, _) in enumerate(blocks):
            summand[d] = got[i * quarter : (i + 1) * quarter]
        return keeps, got

    from_left, from_right = normed, normed
    before = shared_part = shared_expert(normed, shared_weights)
    on_way, next_on_way = (), ()
    for s in range(1, steps):
        from_left = lax.ppermute(from_left, "exp", right)
        from_right = lax.ppermute(from_right, "exp", left)
        from_left, before, on_way = lax.optimization_barrier((from_left, before, on_way))
        blocks = [(s, [from_left]), (-s, [from_right])]
        on_way = next_on_way
        if s == 1:
            before, next_on_way = work([(0, [normed])] + blocks, shared_part)
        else:
            before, next_on_way = work(blocks)
    low = lax.ppermute(from_left[:quarter], "exp", right)
    high = lax.ppermute(from_right[quarter:], "exp", left)
    low, before, on_way = lax.optimization_barrier((low, before, on_way))
    work([(steps, [low, high])])

    def part(d):
        return own[d].astype(f32) + summand[d].astype(f32)

    eighth = quarter // 2
    far = part(steps).astype(bf16)
    to_right = lax.ppermute(far[:eighth], "exp", right)
    to_left = lax.ppermute(far[eighth:], "exp", left)
    for k in range(steps - 1, 0, -1):
        a, b = part(-k), part(k)
        if k == steps - 1:
            a = jnp.concatenate([a[:eighth] + to_right.astype(f32), a[eighth:]], axis=0)
            b = jnp.concatenate([b[:eighth], b[eighth:] + to_left.astype(f32)], axis=0)
        else:
            a, b = a + to_right.astype(f32), b + to_left.astype(f32)
        to_right = lax.ppermute(a.astype(bf16), "exp", right)
        to_left = lax.ppermute(b.astype(bf16), "exp", left)
    total = part(0) + (to_right.astype(f32) + to_left.astype(f32))
    hidden_here = lax.dynamic_slice_in_dim(hidden_state, plane * quarter, quarter, 0)
    mine = (hidden_here.astype(f32) + total).astype(bf16)

    def joined(index, here, there):
        first = index == 0
        return jnp.concatenate(
            [jnp.where(first, here, there), jnp.where(first, there, here)], axis=0
        )

    mine = joined(plane, mine, lax.ppermute(mine, "req", across))
    return joined(core, mine, lax.ppermute(mine, "req", sibling))


def on_device(
    residual,
    queries,
    prefix_kv,
    suffix_kv,
    suffix_lengths,
    out_proj,
    norm_gain,
    routes,
    route_weights,
    expert_gate,
    expert_up,
    expert_down,
    shared_gate,
    shared_up,
    shared_down,
):
    tokens_here = residual.shape[0]
    feat_width = residual.shape[1]
    head_count = queries.shape[1] // HD
    scaling = 1.0 / math.sqrt(HD)
    query_heads = jnp.transpose(queries.reshape(tokens_here, head_count, HD), (1, 0, 2))
    start_state = (
        jnp.full((head_count, tokens_here), neg_big, jnp.float32),
        jnp.zeros((head_count, tokens_here), jnp.float32),
        jnp.zeros((head_count, tokens_here, HD), jnp.float32),
    )

    def absorb(carried, key_rows, value_rows, allowed):
        running_max, running_sum, running_acc = carried
        scores = (
            jnp.einsum("htd,kd->htk", query_heads, key_rows, preferred_element_type=jnp.float32)
            * scaling
        )
        if allowed is not None:
            scores = jnp.where(allowed[None], scores, neg_big)
        new_max = jnp.maximum(running_max, jnp.max(scores, axis=-1))
        factor = jnp.exp(running_max - new_max)
        exp_scores = jnp.exp(scores - new_max[..., None])
        new_sum = running_sum * factor + jnp.sum(exp_scores, axis=-1)
        new_acc = running_acc * factor[..., None] + jnp.einsum(
            "htk,kd->htd",
            exp_scores.astype(jnp.bfloat16),
            value_rows,
            preferred_element_type=jnp.float32,
        )
        return (new_max, new_sum, new_acc)

    portion = lax.all_gather(prefix_kv, "exp", axis=1, tiled=True)
    key_count = portion.shape[1]
    window_len = math.gcd(key_count, 2048)

    def inner(position, inner_state):
        window = lax.dynamic_slice_in_dim(portion[0], position * window_len, window_len, 0)
        return absorb(inner_state, window[:, :HD], window[:, HD:], None)

    carried = lax.fori_loop(0, key_count // window_len, inner, start_state)
    request_ends = jnp.cumsum(suffix_lengths[0])
    positions = jnp.arange(tokens_here, dtype=jnp.int32)
    request_ids = jnp.sum((positions[:, None] >= request_ends[None, :]).astype(jnp.int32), axis=1)
    allowed = (request_ids[:, None] == request_ids[None, :]) & (
        positions[None, :] <= positions[:, None]
    )
    carried = absorb(carried, suffix_kv[:, 0, :HD], suffix_kv[:, 0, HD:], allowed)
    running_max, running_sum, running_acc = carried
    attention = (
        jnp.transpose(running_acc / running_sum[..., None], (1, 0, 2))
        .reshape(tokens_here, head_count * HD)
        .astype(jnp.bfloat16)
    )
    attn_terms = jnp.dot(attention, out_proj, preferred_element_type=jnp.float32)
    attn_out = lax.psum(attn_terms.astype(jnp.bfloat16), "req").astype(jnp.float32)
    hidden_state = (residual.astype(jnp.float32) + attn_out).astype(jnp.bfloat16)
    hidden_float = hidden_state.astype(jnp.float32)
    mean_square = jnp.mean(hidden_float * hidden_float, axis=-1, keepdims=True)
    normed = (
        hidden_float * lax.rsqrt(mean_square + norm_eps) * norm_gain.astype(jnp.float32)
    ).astype(jnp.bfloat16)
    shared_gate_act = jnp.dot(normed, shared_gate, preferred_element_type=jnp.float32)
    shared_up_act = jnp.dot(normed, shared_up, preferred_element_type=jnp.float32)
    shared_hidden = (jax.nn.silu(shared_gate_act) * shared_up_act).astype(jnp.bfloat16)
    shared_part = jnp.dot(shared_hidden, shared_down, preferred_element_type=jnp.float32)
    exp_count = lax.axis_size("exp")
    experts = exp_count * expert_gate.shape[0]
    capacity = expert_capacity(tokens_here, experts)
    pick_ids = routes.reshape(-1)
    one_hot = (pick_ids[:, None] == jnp.arange(experts, dtype=jnp.int32)[None, :]).astype(jnp.int32)
    pick_ranks = jnp.sum((jnp.cumsum(one_hot, axis=0) - one_hot) * one_hot, axis=1)
    pick_slots = (pick_ids * capacity + pick_ranks).reshape(tokens_here, TOP)
    slot_ids = jnp.arange(experts * capacity, dtype=jnp.int32)
    placement = jnp.any(pick_slots[None, :, :] == slot_ids[:, None, None], axis=2).astype(
        jnp.bfloat16
    )
    buffer = (
        jnp.dot(placement, normed, preferred_element_type=jnp.float32)
        .astype(jnp.bfloat16)
        .reshape(experts, capacity, feat_width)
    )
    source_rows = lax.all_to_all(buffer, "exp", split_axis=0, concat_axis=0, tiled=True)
    sources, slot_count, row_width = source_rows.shape
    flat_rows = source_rows.reshape(sources * slot_count, row_width)
    gate_act = jnp.dot(flat_rows, expert_gate[0], preferred_element_type=jnp.float32)
    up_act = jnp.dot(flat_rows, expert_up[0], preferred_element_type=jnp.float32)
    expert_hidden = (jax.nn.silu(gate_act) * up_act).astype(jnp.bfloat16)
    partial_out = jnp.dot(expert_hidden, expert_down[0], preferred_element_type=jnp.float32).astype(
        jnp.bfloat16
    )
    finish_partial_out = partial_out.reshape(sources, slot_count, row_width)
    returned = lax.all_to_all(finish_partial_out, "exp", split_axis=0, concat_axis=0, tiled=True)
    flat_back = returned.reshape(experts * capacity, feat_width)
    picked_rows = (
        flat_back[pick_slots.reshape(-1)].astype(jnp.float32).reshape(tokens_here, TOP, feat_width)
    )
    routed = jnp.sum(picked_rows * route_weights[:, :, None], axis=1)
    summed = lax.psum((shared_part + routed).astype(jnp.bfloat16), "req").astype(jnp.float32)
    return (hidden_float + summed).astype(jnp.bfloat16)


def solution(mesh):
    placed = (
        P("exp", None),
        P("exp", "req"),
        P("req", "exp", None),
        P("exp", "req", None),
        P("exp", None),
        P("req", None),
        P(),
        P("exp", None),
        P("exp", None),
        P("exp", None, "req"),
        P("exp", None, "req"),
        P("exp", "req", None),
        P(None, "req"),
        P(None, "req"),
        P("req", None),
    )

    def program(residual, *rest):
        n_exp, n_req = mesh.shape["exp"], mesh.shape["req"]
        tokens_here = residual.shape[0] // n_exp
        experts = rest[8].shape[0]
        every_row = expert_capacity(tokens_here, experts) == tokens_here
        ring = every_row and experts == n_exp and n_req == 4 and n_exp % 2 == 0 and n_exp >= 4
        return jax.shard_map(
            on_device_ring if ring else on_device,
            mesh=mesh,
            in_specs=placed,
            out_specs=P("exp", None),
            check_vma=False,
        )(residual, *rest)

    return program
```

```python
import functools
import math

import jax
import jax.numpy as jnp
from jax import lax
from jax.experimental import pallas as pl
from jax.experimental.pallas import tpu as pltpu
from jax.sharding import PartitionSpec as P

HD = 128
TOP = 6

neg_big = -1e30
norm_eps = 1e-06
f32 = jnp.float32
bf16 = jnp.bfloat16
STAGE_VMEM = 1 << 20
SHARED_VMEM = 5 << 20
EXPERT_VMEM = 4 << 20
COLUMNS = 512
SLOTS = 6
EFFORT = 50


def expert_capacity(tokens_here, experts):
    return min(tokens_here, 4 * ((tokens_here * TOP + 2 * experts - 1) // (2 * experts)))


def attend_kernel(heads, tokens, page_len, page_count, first, last, *refs):
    refs = list(refs)
    q_ref = refs.pop(0)
    if first:
        lengths_ref, suffix_ref = refs.pop(0), refs.pop(0)
    else:
        max_in, sum_in, acc_in = refs.pop(0), refs.pop(0), refs.pop(0)
    if last:
        core_ref, proj_ref = refs.pop(0), refs.pop(0)
    page_refs = [refs.pop(0) for _ in range(page_count)]
    if last:
        keep_ref, send_ref, proj_buf, proj_sem = refs
        fetch = pltpu.make_async_copy(proj_ref, proj_buf, proj_sem)
        fetch.start()
    scaling = 1.0 / math.sqrt(HD)
    q = jnp.concatenate([q_ref[:, h * HD : (h + 1) * HD] for h in range(heads)], axis=0)
    blocks = [(ref[:page_len, :HD], ref[:page_len, HD:]) for ref in page_refs]
    scores = [
        lax.dot_general(q, k, (((1,), (1,)), ((), ())), preferred_element_type=f32) * scaling
        for k, _ in blocks
    ]
    if first:
        ends, total = [], 0
        for i in range(lengths_ref.shape[1]):
            total = total + lengths_ref[0, i]
            ends.append(total)
        rows = lax.broadcasted_iota(jnp.int32, (tokens, tokens), 0)
        cols = lax.broadcasted_iota(jnp.int32, (tokens, tokens), 1)
        row_ids = sum((rows >= e).astype(jnp.int32) for e in ends)
        col_ids = sum((cols >= e).astype(jnp.int32) for e in ends)
        bias = jnp.where((row_ids == col_ids) & (cols <= rows), 0.0, neg_big).astype(f32)
        k, v = suffix_ref[:, :HD], suffix_ref[:, HD:]
        own = lax.dot_general(q, k, (((1,), (1,)), ((), ())), preferred_element_type=f32) * scaling
        own = jnp.where(jnp.concatenate([bias] * heads, axis=0) < 0.0, neg_big, own)
        scores.append(own)
        blocks.append((k, v))
    new_max = functools.reduce(
        jnp.maximum, [jnp.max(s, axis=-1, keepdims=True) for s in scores]
    )
    if not first:
        old_max = max_in[:, :1]
        new_max = jnp.maximum(new_max, old_max)
        factor = jnp.exp(old_max - new_max)
        total = sum_in[:, :1] * factor
        acc = acc_in[...] * factor
    else:
        total, acc = 0.0, 0.0
    for s, (_, v) in zip(scores, blocks):
        e = jnp.exp(s - new_max)
        total = total + jnp.sum(e, axis=-1, keepdims=True)
        acc = acc + jnp.dot(e.astype(bf16), v, preferred_element_type=f32)
    if last:
        out = (acc / total).astype(bf16)
        rows = jnp.concatenate([out[h * tokens : (h + 1) * tokens] for h in range(heads)], axis=1)
        half = tokens // 2
        second = core_ref[0] == 1
        fetch.wait()
        for c in range(0, proj_buf.shape[1], COLUMNS):
            cols = slice(c, c + COLUMNS)
            terms = jnp.dot(rows, proj_buf[:, cols], preferred_element_type=f32).astype(bf16)
            low, high = terms[:half], terms[half:]
            keep_ref[:, cols] = jnp.where(second, high, low)
            send_ref[:, cols] = jnp.where(second, low, high)
    else:
        max_out, sum_out, acc_out = refs
        max_out[...] = jnp.broadcast_to(new_max, max_out.shape)
        sum_out[...] = jnp.broadcast_to(total, sum_out.shape)
        acc_out[...] = acc


def attend(queries, pages, page_len, state=None, suffix=None, core=None, out_proj=None):
    tokens, width = queries.shape
    heads = width // HD
    first, last = state is None, core is not None
    vmem, smem = pl.BlockSpec(memory_space=pltpu.VMEM), pl.BlockSpec(memory_space=pltpu.SMEM)
    args, specs = [queries], [vmem]
    if first:
        args += list(suffix)
        specs += [smem, vmem]
    else:
        args += list(state)
        specs += [vmem] * 3
    if last:
        args += [core, pltpu.with_memory_space_constraint(out_proj, pltpu.HBM)]
        specs += [smem, pl.BlockSpec(memory_space=pl.ANY)]
    args += pages
    specs += [vmem] * len(pages)
    if last:
        outs = [jax.ShapeDtypeStruct((tokens // 2, out_proj.shape[1]), bf16)] * 2
        scratch = [pltpu.VMEM(out_proj.shape, bf16), pltpu.SemaphoreType.DMA(())]
    else:
        outs = [jax.ShapeDtypeStruct((heads * tokens, HD), f32)] * 3
        scratch = []
    keys = sum(page_len for _ in pages) + (tokens if first else 0)
    return pl.pallas_call(
        functools.partial(attend_kernel, heads, tokens, page_len, len(pages), first, last),
        out_shape=outs,
        in_specs=specs,
        out_specs=[vmem] * len(outs),
        scratch_shapes=scratch,
        compiler_params=pltpu.CompilerParams(vmem_limit_bytes=12 << 20),
        cost_estimate=pl.CostEstimate(
            flops=4 * heads * tokens * keys * HD,
            bytes_accessed=4 * keys * HD + 2 * tokens * width,
            transcendentals=heads * tokens * keys,
        ),
    )(*args)


def in_vmem(arrays):
    return [pltpu.with_memory_space_constraint(a, pltpu.VMEM) for a in arrays]


def in_hbm(arrays):
    return [pltpu.with_memory_space_constraint(a, pltpu.HBM) for a in arrays]


def norm_kernel(
    plane_ref, here_ref, there_ref, residual_ref, gain_ref, gates_ref, hidden_ref, out_ref
):
    width = hidden_ref.shape[1]
    attn_out = here_ref[...].astype(f32) + there_ref[...].astype(f32)
    hidden = (residual_ref[...].astype(f32) + attn_out).astype(bf16)
    part = hidden_ref.shape[0]
    hidden_ref[...] = jnp.where(plane_ref[0] == 1, hidden[part:], hidden[:part])
    hidden = hidden.astype(f32)
    mean_square = jnp.mean(hidden * hidden, axis=-1, keepdims=True)
    normed = hidden * lax.rsqrt(mean_square + norm_eps) * gain_ref[...].astype(f32)
    out_ref[:, :width] = normed.astype(bf16)
    out_ref[:, width:] = gates_ref[...]


def norm(plane, here, there, residual, gain, gates):
    rows, width = here.shape
    vmem = pl.BlockSpec(memory_space=pltpu.VMEM)
    return pl.pallas_call(
        norm_kernel,
        out_shape=[
            jax.ShapeDtypeStruct((rows // 2, width), bf16),
            jax.ShapeDtypeStruct((rows, width + gates.shape[1]), bf16),
        ],
        in_specs=[pl.BlockSpec(memory_space=pltpu.SMEM)] + [vmem] * 5,
        out_specs=[vmem] * 2,
        compiler_params=pltpu.CompilerParams(vmem_limit_bytes=2 << 20),
        cost_estimate=pl.CostEstimate(
            flops=8 * rows * width, bytes_accessed=10 * rows * width, transcendentals=rows
        ),
    )(plane, here, there, residual, gain.reshape(1, width), gates)


def joining(sources, outs, sems):
    block = sources[0].shape[0]
    return [
        pltpu.make_async_copy(
            source, outs[i // 2].at[pl.ds(i % 2 * block, block)], sems.at[i]
        )
        for i, source in enumerate(sources)
    ]


def stage_kernel(*refs):
    copies = joining(refs[:4], refs[4:6], refs[6])
    for copy in copies:
        copy.start()
    for copy in copies:
        copy.wait()


def stage(weights):
    block, width = weights[0].shape
    return pl.pallas_call(
        stage_kernel,
        out_shape=[pltpu.VMEM((2 * block, width), bf16)] * 2,
        in_specs=[pl.BlockSpec(memory_space=pl.ANY)] * 4,
        out_specs=[pl.BlockSpec(memory_space=pltpu.VMEM)] * 2,
        scratch_shapes=[pltpu.SemaphoreType.DMA((4,))],
        compiler_params=pltpu.CompilerParams(vmem_limit_bytes=STAGE_VMEM),
        cost_estimate=pl.CostEstimate(
            flops=0, bytes_accessed=8 * block * width, transcendentals=0
        ),
    )(*in_hbm(weights))


def hidden_units(x, gate_weights, up_weights):
    contract = (((1,), (1,)), ((), ()))
    gate = lax.dot_general(x, gate_weights, contract, preferred_element_type=f32)
    up = lax.dot_general(x, up_weights, contract, preferred_element_type=f32)
    return (gate / (1.0 + jnp.exp(-gate)) * up).astype(bf16)


def shared_kernel(count, *refs):
    rows, sources = refs[:count], refs[count : count + 6]
    out_ref, buf, sems = refs[-3:]
    block, width = sources[0].shape
    slots, units = buf.shape[:2]
    pieces = 2 * block // units

    def fetch(k):
        core, row = divmod(k // 3 * units, block)
        return pltpu.make_async_copy(
            sources[2 * (k % 3) + core].at[pl.ds(row, units)], buf.at[k % slots], sems.at[k % slots]
        )

    def free(k):
        if k + slots < 3 * pieces:
            fetch(k + slots).start()

    for k in range(slots):
        fetch(k).start()
    x = jnp.concatenate([ref[:, :width] for ref in rows], axis=0)
    for piece in range(pieces):
        k = 3 * piece
        fetch(k).wait()
        fetch(k + 1).wait()
        hidden = hidden_units(x, buf[k % slots], buf[(k + 1) % slots])
        free(k)
        free(k + 1)
        fetch(k + 2).wait()
        for c in range(0, width, COLUMNS):
            cols = slice(c, c + COLUMNS)
            out = jnp.dot(hidden, buf[(k + 2) % slots, :, cols], preferred_element_type=f32)
            out_ref[:, cols] = out if piece == 0 else out_ref[:, cols] + out
        free(k + 2)


def shared_expert(rows, weights):
    block, width = weights[0].shape
    units = block // 2
    count = sum(a.shape[0] for a in rows)
    vmem = pl.BlockSpec(memory_space=pltpu.VMEM)
    return pl.pallas_call(
        functools.partial(shared_kernel, len(rows)),
        out_shape=jax.ShapeDtypeStruct((count, width), f32),
        in_specs=[vmem] * len(rows) + [pl.BlockSpec(memory_space=pl.ANY)] * 6,
        out_specs=vmem,
        scratch_shapes=[
            pltpu.VMEM((SLOTS, units, width), bf16),
            pltpu.SemaphoreType.DMA((SLOTS,)),
        ],
        compiler_params=pltpu.CompilerParams(vmem_limit_bytes=SHARED_VMEM),
        cost_estimate=pl.CostEstimate(
            flops=12 * count * width * block,
            bytes_accessed=12 * block * width,
            transcendentals=2 * count * block,
        ),
    )(*rows, *in_hbm(weights))


def expert_kernel(n_experts, counts, plus, staging, *refs):
    refs = list(refs)
    place_ref = refs.pop(0)
    sources = [refs.pop(0) for _ in range(sum(counts))]
    shared_ref = refs.pop(0) if plus else None
    gate_ref, up_ref = refs[:2]
    if staging:
        down_ref, sems = refs[-2:]
        copies = joining(refs[2:4], [down_ref], sems)
        for copy in copies:
            copy.start()
        keeps, send_ref = refs[4:-3], refs[-3]
    else:
        down_ref = refs[2]
        keeps, send_ref = refs[3:-1], refs[-1]
    width = send_ref.shape[1]
    x = jnp.concatenate([ref[:, :width] for ref in sources], axis=0)
    hidden = hidden_units(x, gate_ref[...], up_ref[...])
    lanes = jnp.concatenate([ref[:, width:] for ref in sources], axis=0).astype(f32)
    lane = lax.broadcasted_iota(jnp.int32, lanes.shape, 1)
    e, second = place_ref[0], place_ref[1] == 1
    scale = jnp.sum(
        jnp.where((lane == e) | (lane == e + n_experts), lanes, 0.0), axis=1, keepdims=True
    )
    part = keeps[0].shape[0]
    if staging:
        for copy in copies:
            copy.wait()
    for c in range(0, width, COLUMNS):
        cols = slice(c, c + COLUMNS)
        out = jnp.dot(hidden, down_ref[:, cols], preferred_element_type=f32) * scale
        for i, keep_ref in enumerate(keeps):
            low = out[2 * part * i : 2 * part * i + part]
            high = out[2 * part * i + part : 2 * part * (i + 1)]
            if plus and i == 0:
                low = low + shared_ref[:part, cols]
                high = high + shared_ref[part:, cols]
            low, high = low.astype(bf16), high.astype(bf16)
            keep_ref[:, cols] = jnp.where(second, high, low)
            send_ref[part * i : part * (i + 1), cols] = jnp.where(second, low, high)


def expert(blocks, weights, n_experts, place, shared=None):
    counts = [len(b) for b in blocks]
    rows = sum(a.shape[0] for b in blocks for a in b)
    part = rows // len(blocks) // 2
    hidden, width = weights[0].shape
    staging = len(weights) == 4
    vmem, smem = pl.BlockSpec(memory_space=pltpu.VMEM), pl.BlockSpec(memory_space=pltpu.SMEM)
    args = [place] + [a for b in blocks for a in b] + ([] if shared is None else [shared])
    specs = [smem] + [vmem] * (len(args) + 1)
    outs = [jax.ShapeDtypeStruct((part, width), bf16)] * len(blocks)
    outs.append(jax.ShapeDtypeStruct((part * len(blocks), width), bf16))
    if staging:
        args += in_vmem(weights[:2]) + in_hbm(weights[2:])
        specs += [pl.BlockSpec(memory_space=pl.ANY)] * 2
        outs.append(pltpu.VMEM((hidden, width), bf16))
    else:
        args += in_vmem(weights)
        specs += [vmem]
    outs = pl.pallas_call(
        functools.partial(expert_kernel, n_experts, counts, shared is not None, staging),
        out_shape=outs,
        in_specs=specs,
        out_specs=[vmem] * len(outs),
        scratch_shapes=[pltpu.SemaphoreType.DMA((2,))] if staging else [],
        compiler_params=pltpu.CompilerParams(vmem_limit_bytes=EXPERT_VMEM),
        cost_estimate=pl.CostEstimate(
            flops=EFFORT * 6 * rows * width * hidden,
            bytes_accessed=4 * rows * width,
            transcendentals=rows * hidden,
        ),
    )(*args)
    if staging:
        weights = [weights[0], weights[1], outs[-1]]
        outs = outs[:-1]
    return outs[:-1], outs[-1], weights


def on_device_ring(
    residual,
    queries,
    prefix_kv,
    suffix_kv,
    suffix_lengths,
    out_proj,
    norm_gain,
    routes,
    route_weights,
    expert_gate,
    expert_up,
    expert_down,
    shared_gate,
    shared_up,
    shared_down,
):
    tokens, width = residual.shape
    half = tokens // 2
    n = lax.axis_size("exp")
    steps = n // 2
    order = list(range(0, n, 2)) + list(range(n - 1, 0, -2))
    right = [(order[k], order[(k + 1) % n]) for k in range(n)]
    left = [(b, a) for a, b in right]
    req = lax.axis_size("req")
    sibling = [(i, i ^ 1) for i in range(req)]
    across = [(i, i ^ 2) for i in range(req)]
    core = lax.rem(lax.axis_index("req"), 2)
    plane = lax.div(lax.axis_index("req"), 2)
    me = lax.axis_index("exp")

    def half_of(x):
        return lax.dynamic_slice_in_dim(x, core * half, half, 0)

    slots = jnp.arange(n, dtype=jnp.int32)
    dense = jnp.sum(
        jnp.where(half_of(routes)[:, :, None] == slots, half_of(route_weights)[:, :, None], 0.0),
        axis=1,
    )
    head = lax.reduce_precision(dense, 8, 7)
    rest = lax.reduce_precision(dense - head, 8, 7)
    gates = jnp.concatenate(
        [head, rest, jnp.zeros((half, -2 * n % HD), f32)], axis=1
    ).astype(bf16)
    page = prefix_kv[0]
    page_len = page.shape[0]

    shared_weights = (shared_gate.T, shared_up.T, shared_down)
    expert_weights = (expert_gate[0].T, expert_up[0].T, expert_down[0])

    def with_sibling(weights):
        return [w for own in weights for w in (own, lax.ppermute(own, "req", sibling))]

    shared_weights = with_sibling(shared_weights)
    expert_weights = with_sibling(expert_weights)

    suffix = (suffix_lengths, suffix_kv[:, 0])
    core_arr = jnp.reshape(core, (1,)).astype(jnp.int32)
    from_left, from_right = page, page
    cut = page_len // 2
    state = attend(queries, [page], page_len, suffix=suffix)
    for s in range(1, steps):
        from_left = lax.ppermute(from_left, "exp", right)
        from_right = lax.ppermute(from_right, "exp", left)
        from_left, state = lax.optimization_barrier((from_left, state))
        state = attend(queries, [from_left, from_right], page_len, state=state)
    low = lax.ppermute(from_left[:cut], "exp", right)
    high = lax.ppermute(from_right[cut:], "exp", left)
    low, state = lax.optimization_barrier((low, state))
    keep, send = attend(
        queries, [low, high], cut, state=state, core=core_arr, out_proj=out_proj
    )

    other = lax.ppermute(send, "req", sibling)
    terms = (keep.astype(f32) + other.astype(f32)).astype(bf16)
    quarter = half // 2
    terms_across = lax.ppermute(terms, "req", across)
    terms_across, staged = lax.optimization_barrier((terms_across, stage(expert_weights[:4])))
    staged = list(staged) + expert_weights[4:]
    hidden_here, normed = norm(
        plane.reshape(1), terms, terms_across, half_of(residual), norm_gain, gates
    )
    place = jnp.stack([me, plane]).astype(jnp.int32)

    own, summand = {}, {}

    def work(blocks, shared=None):
        nonlocal staged
        keeps, send, staged = expert([b for _, b in blocks], staged, n, place, shared)
        got = lax.ppermute(send, "req", across)
        for (d, _), keep in zip(blocks, keeps):
            own[d] = keep
        return keeps, ([d for d, _ in blocks], got)

    def landed(step, *others):
        due = [k for k in on_way if k < steps and max(k + 2, steps) == step]
        out = lax.optimization_barrier(others + tuple(on_way[k][1] for k in due))
        for k, got in zip(due, out[len(others) :]):
            for i, d in enumerate(on_way[k][0]):
                summand[d] = got[i * quarter : (i + 1) * quarter]
        return out[: len(others)]

    from_left, from_right = normed, normed
    before = shared_part = shared_expert([normed], shared_weights)
    on_way = {}
    for s in range(1, steps):
        from_left = lax.ppermute(from_left, "exp", right)
        from_right = lax.ppermute(from_right, "exp", left)
        from_left, before = landed(s, from_left, before)
        blocks = [(s, [from_left]), (-s, [from_right])]
        before, on_way[s] = work(blocks)
    low = lax.ppermute(from_left[:quarter], "exp", right)
    high = lax.ppermute(from_right[quarter:], "exp", left)
    low, before = landed(steps, low, before)
    last, on_way[steps] = work([(0, [normed]), (steps, [low, high])], shared_part)
    (last,) = landed(steps + 1, last)
    for i, d in enumerate(on_way[steps][0]):
        summand[d] = on_way[steps][1][i * quarter : (i + 1) * quarter]

    def part(d):
        return own[d].astype(f32) + summand[d].astype(f32)

    def along(hops):
        return [(order[i], order[(i + hops) % n]) for i in range(n)]

    total = hidden_here.astype(f32) + part(0)
    near = steps // 2
    arrived = []
    for d in range(steps, near, -1):
        for sign in (1, -1) if 2 * d != n else (1,):
            block = d if 2 * d == n else -sign * d
            arrived.append(lax.ppermute(part(block).astype(bf16), "exp", along(sign * d)))
    to_right = to_left = None
    for k in range(near, 0, -1):
        a, b = part(-k), part(k)
        if to_right is not None:
            a, b = a + to_right.astype(f32), b + to_left.astype(f32)
        to_right = lax.ppermute(a.astype(bf16), "exp", right)
        to_left = lax.ppermute(b.astype(bf16), "exp", left)
    for terms_there in [to_right, to_left] + arrived:
        total = total + terms_there.astype(f32)
    mine = total.astype(bf16)

    def joined(index, here, there):
        first = index == 0
        return jnp.concatenate(
            [jnp.where(first, here, there), jnp.where(first, there, here)], axis=0
        )

    mine = joined(plane, mine, lax.ppermute(mine, "req", across))
    return joined(core, mine, lax.ppermute(mine, "req", sibling))


def on_device(
    residual,
    queries,
    prefix_kv,
    suffix_kv,
    suffix_lengths,
    out_proj,
    norm_gain,
    routes,
    route_weights,
    expert_gate,
    expert_up,
    expert_down,
    shared_gate,
    shared_up,
    shared_down,
):
    tokens_here = residual.shape[0]
    feat_width = residual.shape[1]
    head_count = queries.shape[1] // HD
    scaling = 1.0 / math.sqrt(HD)
    query_heads = jnp.transpose(queries.reshape(tokens_here, head_count, HD), (1, 0, 2))
    start_state = (
        jnp.full((head_count, tokens_here), neg_big, jnp.float32),
        jnp.zeros((head_count, tokens_here), jnp.float32),
        jnp.zeros((head_count, tokens_here, HD), jnp.float32),
    )

    def absorb(carried, key_rows, value_rows, allowed):
        running_max, running_sum, running_acc = carried
        scores = (
            jnp.einsum("htd,kd->htk", query_heads, key_rows, preferred_element_type=jnp.float32)
            * scaling
        )
        if allowed is not None:
            scores = jnp.where(allowed[None], scores, neg_big)
        new_max = jnp.maximum(running_max, jnp.max(scores, axis=-1))
        factor = jnp.exp(running_max - new_max)
        exp_scores = jnp.exp(scores - new_max[..., None])
        new_sum = running_sum * factor + jnp.sum(exp_scores, axis=-1)
        new_acc = running_acc * factor[..., None] + jnp.einsum(
            "htk,kd->htd",
            exp_scores.astype(jnp.bfloat16),
            value_rows,
            preferred_element_type=jnp.float32,
        )
        return (new_max, new_sum, new_acc)

    portion = lax.all_gather(prefix_kv, "exp", axis=1, tiled=True)
    key_count = portion.shape[1]
    window_len = math.gcd(key_count, 2048)

    def inner(position, inner_state):
        window = lax.dynamic_slice_in_dim(portion[0], position * window_len, window_len, 0)
        return absorb(inner_state, window[:, :HD], window[:, HD:], None)

    carried = lax.fori_loop(0, key_count // window_len, inner, start_state)
    request_ends = jnp.cumsum(suffix_lengths[0])
    positions = jnp.arange(tokens_here, dtype=jnp.int32)
    request_ids = jnp.sum((positions[:, None] >= request_ends[None, :]).astype(jnp.int32), axis=1)
    allowed = (request_ids[:, None] == request_ids[None, :]) & (
        positions[None, :] <= positions[:, None]
    )
    carried = absorb(carried, suffix_kv[:, 0, :HD], suffix_kv[:, 0, HD:], allowed)
    running_max, running_sum, running_acc = carried
    attention = (
        jnp.transpose(running_acc / running_sum[..., None], (1, 0, 2))
        .reshape(tokens_here, head_count * HD)
        .astype(jnp.bfloat16)
    )
    attn_terms = jnp.dot(attention, out_proj, preferred_element_type=jnp.float32)
    attn_out = lax.psum(attn_terms.astype(jnp.bfloat16), "req").astype(jnp.float32)
    hidden_state = (residual.astype(jnp.float32) + attn_out).astype(jnp.bfloat16)
    hidden_float = hidden_state.astype(jnp.float32)
    mean_square = jnp.mean(hidden_float * hidden_float, axis=-1, keepdims=True)
    normed = (
        hidden_float * lax.rsqrt(mean_square + norm_eps) * norm_gain.astype(jnp.float32)
    ).astype(jnp.bfloat16)
    shared_gate_act = jnp.dot(normed, shared_gate, preferred_element_type=jnp.float32)
    shared_up_act = jnp.dot(normed, shared_up, preferred_element_type=jnp.float32)
    shared_hidden = (jax.nn.silu(shared_gate_act) * shared_up_act).astype(jnp.bfloat16)
    shared_part = jnp.dot(shared_hidden, shared_down, preferred_element_type=jnp.float32)
    exp_count = lax.axis_size("exp")
    experts = exp_count * expert_gate.shape[0]
    capacity = expert_capacity(tokens_here, experts)
    pick_ids = routes.reshape(-1)
    one_hot = (pick_ids[:, None] == jnp.arange(experts, dtype=jnp.int32)[None, :]).astype(jnp.int32)
    pick_ranks = jnp.sum((jnp.cumsum(one_hot, axis=0) - one_hot) * one_hot, axis=1)
    pick_slots = (pick_ids * capacity + pick_ranks).reshape(tokens_here, TOP)
    slot_ids = jnp.arange(experts * capacity, dtype=jnp.int32)
    placement = jnp.any(pick_slots[None, :, :] == slot_ids[:, None, None], axis=2).astype(
        jnp.bfloat16
    )
    buffer = (
        jnp.dot(placement, normed, preferred_element_type=jnp.float32)
        .astype(jnp.bfloat16)
        .reshape(experts, capacity, feat_width)
    )
    source_rows = lax.all_to_all(buffer, "exp", split_axis=0, concat_axis=0, tiled=True)
    sources, slot_count, row_width = source_rows.shape
    flat_rows = source_rows.reshape(sources * slot_count, row_width)
    gate_act = jnp.dot(flat_rows, expert_gate[0], preferred_element_type=jnp.float32)
    up_act = jnp.dot(flat_rows, expert_up[0], preferred_element_type=jnp.float32)
    expert_hidden = (jax.nn.silu(gate_act) * up_act).astype(jnp.bfloat16)
    partial_out = jnp.dot(expert_hidden, expert_down[0], preferred_element_type=jnp.float32).astype(
        jnp.bfloat16
    )
    finish_partial_out = partial_out.reshape(sources, slot_count, row_width)
    returned = lax.all_to_all(finish_partial_out, "exp", split_axis=0, concat_axis=0, tiled=True)
    flat_back = returned.reshape(experts * capacity, feat_width)
    picked_rows = (
        flat_back[pick_slots.reshape(-1)].astype(jnp.float32).reshape(tokens_here, TOP, feat_width)
    )
    routed = jnp.sum(picked_rows * route_weights[:, :, None], axis=1)
    summed = lax.psum((shared_part + routed).astype(jnp.bfloat16), "req").astype(jnp.float32)
    return (hidden_float + summed).astype(jnp.bfloat16)


def solution(mesh):
    placed = (
        P("exp", None),
        P("exp", "req"),
        P("req", "exp", None),
        P("exp", "req", None),
        P("exp", None),
        P("req", None),
        P(),
        P("exp", None),
        P("exp", None),
        P("exp", None, "req"),
        P("exp", None, "req"),
        P("exp", "req", None),
        P(None, "req"),
        P(None, "req"),
        P("req", None),
    )

    def program(residual, *rest):
        n_exp, n_req = mesh.shape["exp"], mesh.shape["req"]
        tokens_here = residual.shape[0] // n_exp
        experts = rest[8].shape[0]
        every_row = expert_capacity(tokens_here, experts) == tokens_here
        ring = every_row and experts == n_exp and n_req == 4 and n_exp % 2 == 0 and n_exp >= 4
        return jax.shard_map(
            on_device_ring if ring else on_device,
            mesh=mesh,
            in_specs=placed,
            out_specs=P("exp", None),
            check_vma=False,
        )(residual, *rest)

    return program
```

```python
import functools
import math

import jax
import jax.numpy as jnp
from jax import lax
from jax.experimental import pallas as pl
from jax.experimental.pallas import tpu as pltpu
from jax.sharding import PartitionSpec as P

HD = 128
TOP = 6

neg_big = -1e30
norm_eps = 1e-06
f32 = jnp.float32
bf16 = jnp.bfloat16
STAGE_VMEM = 1 << 20
SHARED_VMEM = 5 << 20
EXPERT_VMEM = 4 << 20
COLUMNS = 512
SLOTS = 6
PIECES = 4
FETCH = 1
EFFORT = 50


def expert_capacity(tokens_here, experts):
    return min(tokens_here, 4 * ((tokens_here * TOP + 2 * experts - 1) // (2 * experts)))


def in_vmem(arrays):
    return [pltpu.with_memory_space_constraint(a, pltpu.VMEM) for a in arrays]


def in_hbm(arrays):
    return [pltpu.with_memory_space_constraint(a, pltpu.HBM) for a in arrays]


def in_pieces(source, target, sems):
    rows = source.shape[0] // PIECES
    return [
        pltpu.make_async_copy(
            source.at[pl.ds(i * rows, rows)], target.at[pl.ds(i * rows, rows)], sems.at[i]
        )
        for i in range(PIECES)
    ]


def attend_kernel(heads, tokens, page_len, page_count, first, fetching, last, *refs):
    refs = list(refs)
    q_ref = refs.pop(0)
    if first:
        lengths_ref, suffix_ref = refs.pop(0), refs.pop(0)
    else:
        max_in, sum_in, acc_in = refs.pop(0), refs.pop(0), refs.pop(0)
    if last:
        core_ref, proj_ref = refs.pop(0), refs.pop(0)
        keep_ref, send_ref = refs[-2:]
    if fetching:
        fetches = in_pieces(refs.pop(0), refs[-2], refs[-1])
        for fetch in fetches:
            fetch.start()
    page_refs = [refs.pop(0) for _ in range(page_count)]
    scaling = 1.0 / math.sqrt(HD)
    if first:
        q = jnp.concatenate([q_ref[:, h * HD : (h + 1) * HD] for h in range(heads)], axis=0)
    else:
        q = q_ref[...]
    blocks = [(ref[:page_len, :HD], ref[:page_len, HD:]) for ref in page_refs]
    scores = [
        lax.dot_general(q, k, (((1,), (1,)), ((), ())), preferred_element_type=f32) * scaling
        for k, _ in blocks
    ]
    if first:
        ends, total = [], 0
        for i in range(lengths_ref.shape[1]):
            total = total + lengths_ref[0, i]
            ends.append(total)
        rows = lax.broadcasted_iota(jnp.int32, (tokens, tokens), 0)
        cols = lax.broadcasted_iota(jnp.int32, (tokens, tokens), 1)
        row_ids = sum((rows >= e).astype(jnp.int32) for e in ends)
        col_ids = sum((cols >= e).astype(jnp.int32) for e in ends)
        bias = jnp.where((row_ids == col_ids) & (cols <= rows), 0.0, neg_big).astype(f32)
        k, v = suffix_ref[:, :HD], suffix_ref[:, HD:]
        own = lax.dot_general(q, k, (((1,), (1,)), ((), ())), preferred_element_type=f32) * scaling
        own = jnp.where(jnp.concatenate([bias] * heads, axis=0) < 0.0, neg_big, own)
        scores.append(own)
        blocks.append((k, v))
    new_max = functools.reduce(
        jnp.maximum, [jnp.max(s, axis=-1, keepdims=True) for s in scores]
    )
    if not first:
        old_max = max_in[:, :1]
        new_max = jnp.maximum(new_max, old_max)
        factor = jnp.exp(old_max - new_max)
        total = sum_in[:, :1] * factor
        acc = acc_in[...] * factor
    else:
        total, acc = 0.0, 0.0
    for s, (_, v) in zip(scores, blocks):
        e = jnp.exp(s - new_max)
        total = total + jnp.sum(e, axis=-1, keepdims=True)
        acc = acc + jnp.dot(e.astype(bf16), v, preferred_element_type=f32)
    if last:
        out = (acc / total).astype(bf16)
        rows = jnp.concatenate([out[h * tokens : (h + 1) * tokens] for h in range(heads)], axis=1)
        half = tokens // 2
        second = core_ref[0] == 1
        for c in range(0, proj_ref.shape[1], COLUMNS):
            cols = slice(c, c + COLUMNS)
            terms = jnp.dot(rows, proj_ref[:, cols], preferred_element_type=f32).astype(bf16)
            low, high = terms[:half], terms[half:]
            keep_ref[:, cols] = jnp.where(second, high, low)
            send_ref[:, cols] = jnp.where(second, low, high)
    else:
        max_out, sum_out, acc_out = refs[:3]
        max_out[...] = jnp.broadcast_to(new_max, max_out.shape)
        sum_out[...] = jnp.broadcast_to(total, sum_out.shape)
        acc_out[...] = acc
        if first:
            refs[3][...] = q
        if fetching:
            for fetch in fetches:
                fetch.wait()


def attend(queries, pages, page_len, tokens, state=None, suffix=None, fetch=None, core=None, proj=None):
    first, last = state is None, core is not None
    heads = queries.shape[1] // HD if first else queries.shape[0] // tokens
    vmem, smem = pl.BlockSpec(memory_space=pltpu.VMEM), pl.BlockSpec(memory_space=pltpu.SMEM)
    outs = [jax.ShapeDtypeStruct((heads * tokens, HD), f32)] * 3
    scratch = []
    if first:
        lengths, suffix = suffix
        args = in_hbm([queries]) + [lengths] + in_hbm([suffix])
        pages = in_hbm(pages)
        specs = [vmem, smem, vmem]
        outs.append(jax.ShapeDtypeStruct((heads * tokens, HD), bf16))
    else:
        args = [queries] + list(state)
        specs = [vmem] * 4
    if last:
        args += [core] + in_vmem([proj])
        specs += [smem, vmem]
        outs = [jax.ShapeDtypeStruct((tokens // 2, proj.shape[1]), bf16)] * 2
    if fetch is not None:
        args += in_hbm([fetch])
        specs.append(pl.BlockSpec(memory_space=pl.ANY))
        outs.append(pltpu.VMEM(fetch.shape, fetch.dtype))
        scratch.append(pltpu.SemaphoreType.DMA((PIECES,)))
    keys = page_len * len(pages) + (tokens if first else 0)
    return pl.pallas_call(
        functools.partial(
            attend_kernel, heads, tokens, page_len, len(pages), first, fetch is not None, last
        ),
        out_shape=outs,
        in_specs=specs + [vmem] * len(pages),
        out_specs=[vmem] * len(outs),
        scratch_shapes=scratch,
        compiler_params=pltpu.CompilerParams(vmem_limit_bytes=12 << 20),
        cost_estimate=pl.CostEstimate(
            flops=(1 if last or fetch is not None else EFFORT) * 4 * heads * tokens * keys * HD,
            bytes_accessed=4 * keys * HD + 2 * heads * tokens * HD,
            transcendentals=heads * tokens * keys,
        ),
    )(*args, *pages)


def norm_kernel(
    plane_ref, here_ref, there_ref, residual_ref, gain_ref, gates_ref, hidden_ref, out_ref
):
    width = hidden_ref.shape[1]
    attn_out = here_ref[...].astype(f32) + there_ref[...].astype(f32)
    hidden = (residual_ref[...].astype(f32) + attn_out).astype(bf16)
    part = hidden_ref.shape[0]
    hidden_ref[...] = jnp.where(plane_ref[0] == 1, hidden[part:], hidden[:part])
    hidden = hidden.astype(f32)
    mean_square = jnp.mean(hidden * hidden, axis=-1, keepdims=True)
    normed = hidden * lax.rsqrt(mean_square + norm_eps) * gain_ref[...].astype(f32)
    out_ref[:, :width] = normed.astype(bf16)
    out_ref[:, width:] = gates_ref[...]


def norm(plane, here, there, residual, gain, gates):
    rows, width = here.shape
    vmem = pl.BlockSpec(memory_space=pltpu.VMEM)
    return pl.pallas_call(
        norm_kernel,
        out_shape=[
            jax.ShapeDtypeStruct((rows // 2, width), bf16),
            jax.ShapeDtypeStruct((rows, width + gates.shape[1]), bf16),
        ],
        in_specs=[pl.BlockSpec(memory_space=pltpu.SMEM)] + [vmem] * 5,
        out_specs=[vmem] * 2,
        compiler_params=pltpu.CompilerParams(vmem_limit_bytes=2 << 20),
        cost_estimate=pl.CostEstimate(
            flops=8 * rows * width, bytes_accessed=10 * rows * width, transcendentals=rows
        ),
    )(plane, here, there, residual, gain.reshape(1, width), gates)


def joining(sources, outs, sems):
    block = sources[0].shape[0]
    return [
        pltpu.make_async_copy(
            source, outs[i // 2].at[pl.ds(i % 2 * block, block)], sems.at[i]
        )
        for i, source in enumerate(sources)
    ]


def stage_kernel(*refs):
    copies = joining(refs[:4], refs[4:6], refs[6])
    for copy in copies:
        copy.start()
    for copy in copies:
        copy.wait()


def stage(weights):
    block, width = weights[0].shape
    return pl.pallas_call(
        stage_kernel,
        out_shape=[pltpu.VMEM((2 * block, width), bf16)] * 2,
        in_specs=[pl.BlockSpec(memory_space=pl.ANY)] * 4,
        out_specs=[pl.BlockSpec(memory_space=pltpu.VMEM)] * 2,
        scratch_shapes=[pltpu.SemaphoreType.DMA((4,))],
        compiler_params=pltpu.CompilerParams(vmem_limit_bytes=STAGE_VMEM),
        cost_estimate=pl.CostEstimate(
            flops=0, bytes_accessed=8 * block * width, transcendentals=0
        ),
    )(*in_hbm(weights))


def hidden_units(x, gate_weights, up_weights):
    contract = (((1,), (1,)), ((), ()))
    gate = lax.dot_general(x, gate_weights, contract, preferred_element_type=f32)
    up = lax.dot_general(x, up_weights, contract, preferred_element_type=f32)
    return (gate / (1.0 + jnp.exp(-gate)) * up).astype(bf16)


def shared_kernel(count, *refs):
    rows, sources = refs[:count], refs[count : count + 6]
    out_ref, buf, sems = refs[-3:]
    block, width = sources[0].shape
    slots, units = buf.shape[:2]
    pieces = 2 * block // units

    def fetch(k):
        core, row = divmod(k // 3 * units, block)
        return pltpu.make_async_copy(
            sources[2 * (k % 3) + core].at[pl.ds(row, units)], buf.at[k % slots], sems.at[k % slots]
        )

    def free(k):
        if k + slots < 3 * pieces:
            fetch(k + slots).start()

    for k in range(slots):
        fetch(k).start()
    x = jnp.concatenate([ref[:, :width] for ref in rows], axis=0)
    for piece in range(pieces):
        k = 3 * piece
        fetch(k).wait()
        fetch(k + 1).wait()
        hidden = hidden_units(x, buf[k % slots], buf[(k + 1) % slots])
        free(k)
        free(k + 1)
        fetch(k + 2).wait()
        for c in range(0, width, COLUMNS):
            cols = slice(c, c + COLUMNS)
            out = jnp.dot(hidden, buf[(k + 2) % slots, :, cols], preferred_element_type=f32)
            out_ref[:, cols] = out if piece == 0 else out_ref[:, cols] + out
        free(k + 2)


def shared_expert(rows, weights):
    block, width = weights[0].shape
    units = block // 2
    count = sum(a.shape[0] for a in rows)
    vmem = pl.BlockSpec(memory_space=pltpu.VMEM)
    return pl.pallas_call(
        functools.partial(shared_kernel, len(rows)),
        out_shape=jax.ShapeDtypeStruct((count, width), f32),
        in_specs=[vmem] * len(rows) + [pl.BlockSpec(memory_space=pl.ANY)] * 6,
        out_specs=vmem,
        scratch_shapes=[
            pltpu.VMEM((SLOTS, units, width), bf16),
            pltpu.SemaphoreType.DMA((SLOTS,)),
        ],
        compiler_params=pltpu.CompilerParams(vmem_limit_bytes=SHARED_VMEM),
        cost_estimate=pl.CostEstimate(
            flops=12 * count * width * block,
            bytes_accessed=12 * block * width,
            transcendentals=2 * count * block,
        ),
    )(*rows, *in_hbm(weights))


def expert_kernel(n_experts, counts, plus, staging, *refs):
    refs = list(refs)
    place_ref = refs.pop(0)
    sources = [refs.pop(0) for _ in range(sum(counts))]
    shared_ref = refs.pop(0) if plus else None
    gate_ref, up_ref = refs[:2]
    if staging:
        down_ref, sems = refs[-2:]
        copies = joining(refs[2:4], [down_ref], sems)
        for copy in copies:
            copy.start()
        keeps, send_ref = refs[4:-3], refs[-3]
    else:
        down_ref = refs[2]
        keeps, send_ref = refs[3:-1], refs[-1]
    width = send_ref.shape[1]
    x = jnp.concatenate([ref[:, :width] for ref in sources], axis=0)
    hidden = hidden_units(x, gate_ref[...], up_ref[...])
    lanes = jnp.concatenate([ref[:, width:] for ref in sources], axis=0).astype(f32)
    lane = lax.broadcasted_iota(jnp.int32, lanes.shape, 1)
    e, second = place_ref[0], place_ref[1] == 1
    scale = jnp.sum(
        jnp.where((lane == e) | (lane == e + n_experts), lanes, 0.0), axis=1, keepdims=True
    )
    part = keeps[0].shape[0]
    if staging:
        for copy in copies:
            copy.wait()
    for c in range(0, width, COLUMNS):
        cols = slice(c, c + COLUMNS)
        out = jnp.dot(hidden, down_ref[:, cols], preferred_element_type=f32) * scale
        for i, keep_ref in enumerate(keeps):
            low = out[2 * part * i : 2 * part * i + part]
            high = out[2 * part * i + part : 2 * part * (i + 1)]
            if plus and i == 0:
                low = low + shared_ref[:part, cols]
                high = high + shared_ref[part:, cols]
            low, high = low.astype(bf16), high.astype(bf16)
            keep_ref[:, cols] = jnp.where(second, high, low)
            send_ref[part * i : part * (i + 1), cols] = jnp.where(second, low, high)


def expert(blocks, weights, n_experts, place, shared=None):
    counts = [len(b) for b in blocks]
    rows = sum(a.shape[0] for b in blocks for a in b)
    part = rows // len(blocks) // 2
    hidden, width = weights[0].shape
    staging = len(weights) == 4
    vmem, smem = pl.BlockSpec(memory_space=pltpu.VMEM), pl.BlockSpec(memory_space=pltpu.SMEM)
    args = [place] + [a for b in blocks for a in b] + ([] if shared is None else [shared])
    specs = [smem] + [vmem] * (len(args) + 1)
    outs = [jax.ShapeDtypeStruct((part, width), bf16)] * len(blocks)
    outs.append(jax.ShapeDtypeStruct((part * len(blocks), width), bf16))
    if staging:
        args += in_vmem(weights[:2]) + in_hbm(weights[2:])
        specs += [pl.BlockSpec(memory_space=pl.ANY)] * 2
        outs.append(pltpu.VMEM((hidden, width), bf16))
    else:
        args += in_vmem(weights)
        specs += [vmem]
    outs = pl.pallas_call(
        functools.partial(expert_kernel, n_experts, counts, shared is not None, staging),
        out_shape=outs,
        in_specs=specs,
        out_specs=[vmem] * len(outs),
        scratch_shapes=[pltpu.SemaphoreType.DMA((2,))] if staging else [],
        compiler_params=pltpu.CompilerParams(vmem_limit_bytes=EXPERT_VMEM),
        cost_estimate=pl.CostEstimate(
            flops=EFFORT * 6 * rows * width * hidden,
            bytes_accessed=4 * rows * width,
            transcendentals=rows * hidden,
        ),
    )(*args)
    if staging:
        weights = [weights[0], weights[1], outs[-1]]
        outs = outs[:-1]
    return outs[:-1], outs[-1], weights


def on_device_ring(
    residual,
    queries,
    prefix_kv,
    suffix_kv,
    suffix_lengths,
    out_proj,
    norm_gain,
    routes,
    route_weights,
    expert_gate,
    expert_up,
    expert_down,
    shared_gate,
    shared_up,
    shared_down,
):
    tokens, width = residual.shape
    half = tokens // 2
    n = lax.axis_size("exp")
    steps = n // 2
    order = list(range(0, n, 2)) + list(range(n - 1, 0, -2))
    right = [(order[k], order[(k + 1) % n]) for k in range(n)]
    left = [(b, a) for a, b in right]
    req = lax.axis_size("req")
    sibling = [(i, i ^ 1) for i in range(req)]
    across = [(i, i ^ 2) for i in range(req)]
    core = lax.rem(lax.axis_index("req"), 2)
    plane = lax.div(lax.axis_index("req"), 2)
    me = lax.axis_index("exp")

    def half_of(x):
        return lax.dynamic_slice_in_dim(x, core * half, half, 0)

    slots = jnp.arange(n, dtype=jnp.int32)
    dense = jnp.sum(
        jnp.where(half_of(routes)[:, :, None] == slots, half_of(route_weights)[:, :, None], 0.0),
        axis=1,
    )
    head = lax.reduce_precision(dense, 8, 7)
    rest = lax.reduce_precision(dense - head, 8, 7)
    gates = jnp.concatenate(
        [head, rest, jnp.zeros((half, -2 * n % HD), f32)], axis=1
    ).astype(bf16)
    page = prefix_kv[0]
    page_len = page.shape[0]

    shared_weights = (shared_gate.T, shared_up.T, shared_down)
    expert_weights = (expert_gate[0].T, expert_up[0].T, expert_down[0])

    def with_sibling(weights):
        return [w for own in weights for w in (own, lax.ppermute(own, "req", sibling))]

    shared_weights = with_sibling(shared_weights)
    expert_weights = with_sibling(expert_weights)

    suffix = (suffix_lengths, suffix_kv[:, 0])
    core_arr = jnp.reshape(core, (1,)).astype(jnp.int32)
    from_left, from_right = page, page
    *state, stacked = attend(queries, [page], page_len, tokens, suffix=suffix)
    for s in range(1, steps):
        from_left = lax.ppermute(from_left, "exp", right)
        from_right = lax.ppermute(from_right, "exp", left)
        from_left, state = lax.optimization_barrier((from_left, state))
        fetch = out_proj if s == steps - FETCH else None
        *state, = attend(stacked, [from_left, from_right], page_len, tokens, state, fetch=fetch)
        if fetch is not None:
            proj = state.pop()
    from_left = lax.ppermute(from_left, "exp", right)
    from_left, state = lax.optimization_barrier((from_left, state))
    keep, send = attend(stacked, [from_left], page_len, tokens, state, core=core_arr, proj=proj)

    other = lax.ppermute(send, "req", sibling)
    terms = (keep.astype(f32) + other.astype(f32)).astype(bf16)
    quarter = half // 2
    terms_across = lax.ppermute(terms, "req", across)
    terms_across, staged = lax.optimization_barrier((terms_across, stage(expert_weights[:4])))
    staged = list(staged) + expert_weights[4:]
    hidden_here, normed = norm(
        plane.reshape(1), terms, terms_across, half_of(residual), norm_gain, gates
    )
    place = jnp.stack([me, plane]).astype(jnp.int32)

    own, summand = {}, {}

    def work(blocks, shared=None):
        nonlocal staged
        keeps, send, staged = expert([b for _, b in blocks], staged, n, place, shared)
        got = lax.ppermute(send, "req", across)
        for (d, _), keep in zip(blocks, keeps):
            own[d] = keep
        return keeps, ([d for d, _ in blocks], got)

    def landed(step, *others):
        due = [k for k in on_way if k < steps and max(k + 2, steps) == step]
        out = lax.optimization_barrier(others + tuple(on_way[k][1] for k in due))
        for k, got in zip(due, out[len(others) :]):
            for i, d in enumerate(on_way[k][0]):
                summand[d] = got[i * quarter : (i + 1) * quarter]
        return out[: len(others)]

    from_left, from_right = normed, normed
    before = shared_part = shared_expert([normed], shared_weights)
    on_way = {}
    for s in range(1, steps):
        from_left = lax.ppermute(from_left, "exp", right)
        from_right = lax.ppermute(from_right, "exp", left)
        from_left, before = landed(s, from_left, before)
        blocks = [(s, [from_left]), (-s, [from_right])]
        before, on_way[s] = work(blocks)
    low = lax.ppermute(from_left[:quarter], "exp", right)
    high = lax.ppermute(from_right[quarter:], "exp", left)
    low, before = landed(steps, low, before)
    last, on_way[steps] = work([(0, [normed]), (steps, [low, high])], shared_part)
    (last,) = landed(steps + 1, last)
    for i, d in enumerate(on_way[steps][0]):
        summand[d] = on_way[steps][1][i * quarter : (i + 1) * quarter]

    def part(d):
        return own[d].astype(f32) + summand[d].astype(f32)

    def along(hops):
        return [(order[i], order[(i + hops) % n]) for i in range(n)]

    total = hidden_here.astype(f32) + part(0)
    near = steps // 2
    arrived = []
    for d in range(steps, near, -1):
        for sign in (1, -1) if 2 * d != n else (1,):
            block = d if 2 * d == n else -sign * d
            arrived.append(lax.ppermute(part(block).astype(bf16), "exp", along(sign * d)))
    to_right = to_left = None
    for k in range(near, 0, -1):
        a, b = part(-k), part(k)
        if to_right is not None:
            a, b = a + to_right.astype(f32), b + to_left.astype(f32)
        to_right = lax.ppermute(a.astype(bf16), "exp", right)
        to_left = lax.ppermute(b.astype(bf16), "exp", left)
    for terms_there in [to_right, to_left] + arrived:
        total = total + terms_there.astype(f32)
    mine = total.astype(bf16)

    def joined(index, here, there):
        first = index == 0
        return jnp.concatenate(
            [jnp.where(first, here, there), jnp.where(first, there, here)], axis=0
        )

    mine = joined(plane, mine, lax.ppermute(mine, "req", across))
    theirs = lax.ppermute(mine, "req", sibling)
    out = lax.dynamic_update_slice(jnp.zeros((tokens, width), bf16), mine, (core * half, 0))
    out, theirs = lax.optimization_barrier((out, theirs))
    return lax.dynamic_update_slice(out, theirs, ((1 - core) * half, 0))


def on_device(
    residual,
    queries,
    prefix_kv,
    suffix_kv,
    suffix_lengths,
    out_proj,
    norm_gain,
    routes,
    route_weights,
    expert_gate,
    expert_up,
    expert_down,
    shared_gate,
    shared_up,
    shared_down,
):
    tokens_here = residual.shape[0]
    feat_width = residual.shape[1]
    head_count = queries.shape[1] // HD
    scaling = 1.0 / math.sqrt(HD)
    query_heads = jnp.transpose(queries.reshape(tokens_here, head_count, HD), (1, 0, 2))
    start_state = (
        jnp.full((head_count, tokens_here), neg_big, jnp.float32),
        jnp.zeros((head_count, tokens_here), jnp.float32),
        jnp.zeros((head_count, tokens_here, HD), jnp.float32),
    )

    def absorb(carried, key_rows, value_rows, allowed):
        running_max, running_sum, running_acc = carried
        scores = (
            jnp.einsum("htd,kd->htk", query_heads, key_rows, preferred_element_type=jnp.float32)
            * scaling
        )
        if allowed is not None:
            scores = jnp.where(allowed[None], scores, neg_big)
        new_max = jnp.maximum(running_max, jnp.max(scores, axis=-1))
        factor = jnp.exp(running_max - new_max)
        exp_scores = jnp.exp(scores - new_max[..., None])
        new_sum = running_sum * factor + jnp.sum(exp_scores, axis=-1)
        new_acc = running_acc * factor[..., None] + jnp.einsum(
            "htk,kd->htd",
            exp_scores.astype(jnp.bfloat16),
            value_rows,
            preferred_element_type=jnp.float32,
        )
        return (new_max, new_sum, new_acc)

    portion = lax.all_gather(prefix_kv, "exp", axis=1, tiled=True)
    key_count = portion.shape[1]
    window_len = math.gcd(key_count, 2048)

    def inner(position, inner_state):
        window = lax.dynamic_slice_in_dim(portion[0], position * window_len, window_len, 0)
        return absorb(inner_state, window[:, :HD], window[:, HD:], None)

    carried = lax.fori_loop(0, key_count // window_len, inner, start_state)
    request_ends = jnp.cumsum(suffix_lengths[0])
    positions = jnp.arange(tokens_here, dtype=jnp.int32)
    request_ids = jnp.sum((positions[:, None] >= request_ends[None, :]).astype(jnp.int32), axis=1)
    allowed = (request_ids[:, None] == request_ids[None, :]) & (
        positions[None, :] <= positions[:, None]
    )
    carried = absorb(carried, suffix_kv[:, 0, :HD], suffix_kv[:, 0, HD:], allowed)
    running_max, running_sum, running_acc = carried
    attention = (
        jnp.transpose(running_acc / running_sum[..., None], (1, 0, 2))
        .reshape(tokens_here, head_count * HD)
        .astype(jnp.bfloat16)
    )
    attn_terms = jnp.dot(attention, out_proj, preferred_element_type=jnp.float32)
    attn_out = lax.psum(attn_terms.astype(jnp.bfloat16), "req").astype(jnp.float32)
    hidden_state = (residual.astype(jnp.float32) + attn_out).astype(jnp.bfloat16)
    hidden_float = hidden_state.astype(jnp.float32)
    mean_square = jnp.mean(hidden_float * hidden_float, axis=-1, keepdims=True)
    normed = (
        hidden_float * lax.rsqrt(mean_square + norm_eps) * norm_gain.astype(jnp.float32)
    ).astype(jnp.bfloat16)
    shared_gate_act = jnp.dot(normed, shared_gate, preferred_element_type=jnp.float32)
    shared_up_act = jnp.dot(normed, shared_up, preferred_element_type=jnp.float32)
    shared_hidden = (jax.nn.silu(shared_gate_act) * shared_up_act).astype(jnp.bfloat16)
    shared_part = jnp.dot(shared_hidden, shared_down, preferred_element_type=jnp.float32)
    exp_count = lax.axis_size("exp")
    experts = exp_count * expert_gate.shape[0]
    capacity = expert_capacity(tokens_here, experts)
    pick_ids = routes.reshape(-1)
    one_hot = (pick_ids[:, None] == jnp.arange(experts, dtype=jnp.int32)[None, :]).astype(jnp.int32)
    pick_ranks = jnp.sum((jnp.cumsum(one_hot, axis=0) - one_hot) * one_hot, axis=1)
    pick_slots = (pick_ids * capacity + pick_ranks).reshape(tokens_here, TOP)
    slot_ids = jnp.arange(experts * capacity, dtype=jnp.int32)
    placement = jnp.any(pick_slots[None, :, :] == slot_ids[:, None, None], axis=2).astype(
        jnp.bfloat16
    )
    buffer = (
        jnp.dot(placement, normed, preferred_element_type=jnp.float32)
        .astype(jnp.bfloat16)
        .reshape(experts, capacity, feat_width)
    )
    source_rows = lax.all_to_all(buffer, "exp", split_axis=0, concat_axis=0, tiled=True)
    sources, slot_count, row_width = source_rows.shape
    flat_rows = source_rows.reshape(sources * slot_count, row_width)
    gate_act = jnp.dot(flat_rows, expert_gate[0], preferred_element_type=jnp.float32)
    up_act = jnp.dot(flat_rows, expert_up[0], preferred_element_type=jnp.float32)
    expert_hidden = (jax.nn.silu(gate_act) * up_act).astype(jnp.bfloat16)
    partial_out = jnp.dot(expert_hidden, expert_down[0], preferred_element_type=jnp.float32).astype(
        jnp.bfloat16
    )
    finish_partial_out = partial_out.reshape(sources, slot_count, row_width)
    returned = lax.all_to_all(finish_partial_out, "exp", split_axis=0, concat_axis=0, tiled=True)
    flat_back = returned.reshape(experts * capacity, feat_width)
    picked_rows = (
        flat_back[pick_slots.reshape(-1)].astype(jnp.float32).reshape(tokens_here, TOP, feat_width)
    )
    routed = jnp.sum(picked_rows * route_weights[:, :, None], axis=1)
    summed = lax.psum((shared_part + routed).astype(jnp.bfloat16), "req").astype(jnp.float32)
    return (hidden_float + summed).astype(jnp.bfloat16)


def solution(mesh):
    placed = (
        P("exp", None),
        P("exp", "req"),
        P("req", "exp", None),
        P("exp", "req", None),
        P("exp", None),
        P("req", None),
        P(),
        P("exp", None),
        P("exp", None),
        P("exp", None, "req"),
        P("exp", None, "req"),
        P("exp", "req", None),
        P(None, "req"),
        P(None, "req"),
        P("req", None),
    )

    def program(residual, *rest):
        n_exp, n_req = mesh.shape["exp"], mesh.shape["req"]
        tokens_here = residual.shape[0] // n_exp
        experts = rest[8].shape[0]
        every_row = expert_capacity(tokens_here, experts) == tokens_here
        ring = every_row and experts == n_exp and n_req == 4 and n_exp % 2 == 0 and n_exp >= 4
        return jax.shard_map(
            on_device_ring if ring else on_device,
            mesh=mesh,
            in_specs=placed,
            out_specs=P("exp", None),
            check_vma=False,
        )(residual, *rest)

    return program
```

```python
import functools
import math

import jax
import jax.numpy as jnp
from jax import lax
from jax.experimental import pallas as pl
from jax.experimental.pallas import tpu as pltpu
from jax.sharding import PartitionSpec as P

HD = 128
TOP = 6

neg_big = -1e30
norm_eps = 1e-06
f32 = jnp.float32
bf16 = jnp.bfloat16
STAGE_VMEM = 1 << 20
SHARED_VMEM = 11 << 20
EXPERT_VMEM = 4 << 20
COLUMNS = 512
PIECES = 4
FETCH = 1
EFFORT = 50


def expert_capacity(tokens_here, experts):
    return min(tokens_here, 4 * ((tokens_here * TOP + 2 * experts - 1) // (2 * experts)))


def in_vmem(arrays):
    return [pltpu.with_memory_space_constraint(a, pltpu.VMEM) for a in arrays]


def in_hbm(arrays):
    return [pltpu.with_memory_space_constraint(a, pltpu.HBM) for a in arrays]


def in_pieces(source, target, sems):
    rows = source.shape[0] // PIECES
    return [
        pltpu.make_async_copy(
            source.at[pl.ds(i * rows, rows)], target.at[pl.ds(i * rows, rows)], sems.at[i]
        )
        for i in range(PIECES)
    ]


def attend_kernel(heads, tokens, page_len, page_count, first, fetching, last, *refs):
    refs = list(refs)
    q_ref = refs.pop(0)
    if first:
        lengths_ref, suffix_ref = refs.pop(0), refs.pop(0)
    else:
        max_in, sum_in, acc_in = refs.pop(0), refs.pop(0), refs.pop(0)
    if last:
        core_ref, proj_ref = refs.pop(0), refs.pop(0)
        keep_ref, send_ref = refs[-2:]
    if fetching:
        fetches = in_pieces(refs.pop(0), refs[-2], refs[-1])
        for fetch in fetches:
            fetch.start()
    page_refs = [refs.pop(0) for _ in range(page_count)]
    scaling = 1.0 / math.sqrt(HD)
    if first:
        q = jnp.concatenate([q_ref[:, h * HD : (h + 1) * HD] for h in range(heads)], axis=0)
    else:
        q = q_ref[...]
    blocks = [(ref[:page_len, :HD], ref[:page_len, HD:]) for ref in page_refs]
    scores = [
        lax.dot_general(q, k, (((1,), (1,)), ((), ())), preferred_element_type=f32) * scaling
        for k, _ in blocks
    ]
    if first:
        ends, total = [], 0
        for i in range(lengths_ref.shape[1]):
            total = total + lengths_ref[0, i]
            ends.append(total)
        rows = lax.broadcasted_iota(jnp.int32, (tokens, tokens), 0)
        cols = lax.broadcasted_iota(jnp.int32, (tokens, tokens), 1)
        row_ids = sum((rows >= e).astype(jnp.int32) for e in ends)
        col_ids = sum((cols >= e).astype(jnp.int32) for e in ends)
        bias = jnp.where((row_ids == col_ids) & (cols <= rows), 0.0, neg_big).astype(f32)
        k, v = suffix_ref[:, :HD], suffix_ref[:, HD:]
        own = lax.dot_general(q, k, (((1,), (1,)), ((), ())), preferred_element_type=f32) * scaling
        own = jnp.where(jnp.concatenate([bias] * heads, axis=0) < 0.0, neg_big, own)
        scores.append(own)
        blocks.append((k, v))
    new_max = functools.reduce(
        jnp.maximum, [jnp.max(s, axis=-1, keepdims=True) for s in scores]
    )
    if not first:
        old_max = max_in[:, :1]
        new_max = jnp.maximum(new_max, old_max)
        factor = jnp.exp(old_max - new_max)
        total = sum_in[:, :1] * factor
        acc = acc_in[...] * factor
    else:
        total, acc = 0.0, 0.0
    for s, (_, v) in zip(scores, blocks):
        e = jnp.exp(s - new_max)
        total = total + jnp.sum(e, axis=-1, keepdims=True)
        acc = acc + jnp.dot(e.astype(bf16), v, preferred_element_type=f32)
    if last:
        out = (acc / total).astype(bf16)
        rows = jnp.concatenate([out[h * tokens : (h + 1) * tokens] for h in range(heads)], axis=1)
        half = tokens // 2
        second = core_ref[0] == 1
        for c in range(0, proj_ref.shape[1], COLUMNS):
            cols = slice(c, c + COLUMNS)
            terms = jnp.dot(rows, proj_ref[:, cols], preferred_element_type=f32).astype(bf16)
            low, high = terms[:half], terms[half:]
            keep_ref[:, cols] = jnp.where(second, high, low)
            send_ref[:, cols] = jnp.where(second, low, high)
    else:
        max_out, sum_out, acc_out = refs[:3]
        max_out[...] = jnp.broadcast_to(new_max, max_out.shape)
        sum_out[...] = jnp.broadcast_to(total, sum_out.shape)
        acc_out[...] = acc
        if first:
            refs[3][...] = q
        if fetching:
            for fetch in fetches:
                fetch.wait()


def attend(queries, pages, page_len, tokens, state=None, suffix=None, fetch=None, core=None, proj=None):
    first, last = state is None, core is not None
    heads = queries.shape[1] // HD if first else queries.shape[0] // tokens
    vmem, smem = pl.BlockSpec(memory_space=pltpu.VMEM), pl.BlockSpec(memory_space=pltpu.SMEM)
    outs = [jax.ShapeDtypeStruct((heads * tokens, HD), f32)] * 3
    scratch = []
    if first:
        lengths, suffix = suffix
        args = in_hbm([queries]) + [lengths] + in_hbm([suffix])
        pages = in_hbm(pages)
        specs = [vmem, smem, vmem]
        outs.append(jax.ShapeDtypeStruct((heads * tokens, HD), bf16))
    else:
        args = [queries] + list(state)
        specs = [vmem] * 4
    if last:
        args += [core] + in_vmem([proj])
        specs += [smem, vmem]
        outs = [jax.ShapeDtypeStruct((tokens // 2, proj.shape[1]), bf16)] * 2
    if fetch is not None:
        args += in_hbm([fetch])
        specs.append(pl.BlockSpec(memory_space=pl.ANY))
        outs.append(pltpu.VMEM(fetch.shape, fetch.dtype))
        scratch.append(pltpu.SemaphoreType.DMA((PIECES,)))
    keys = page_len * len(pages) + (tokens if first else 0)
    return pl.pallas_call(
        functools.partial(
            attend_kernel, heads, tokens, page_len, len(pages), first, fetch is not None, last
        ),
        out_shape=outs,
        in_specs=specs + [vmem] * len(pages),
        out_specs=[vmem] * len(outs),
        scratch_shapes=scratch,
        compiler_params=pltpu.CompilerParams(vmem_limit_bytes=12 << 20),
        cost_estimate=pl.CostEstimate(
            flops=(1 if last or fetch is not None else EFFORT) * 4 * heads * tokens * keys * HD,
            bytes_accessed=4 * keys * HD + 2 * heads * tokens * HD,
            transcendentals=heads * tokens * keys,
        ),
    )(*args, *pages)


def norm_kernel(n_experts, plane_ref, *refs):
    here_ref, there_ref, residual_ref, gain_ref, routes_ref, weights_ref, hidden_ref, out_ref = refs
    width = hidden_ref.shape[1]
    attn_out = here_ref[...].astype(f32) + there_ref[...].astype(f32)
    hidden = (residual_ref[...].astype(f32) + attn_out).astype(bf16)
    part = hidden_ref.shape[0]
    hidden_ref[...] = jnp.where(plane_ref[0] == 1, hidden[part:], hidden[:part])
    hidden = hidden.astype(f32)
    mean_square = jnp.mean(hidden * hidden, axis=-1, keepdims=True)
    normed = hidden * lax.rsqrt(mean_square + norm_eps) * gain_ref[...].astype(f32)
    out_ref[:, :width] = normed.astype(bf16)
    lane = lax.broadcasted_iota(jnp.int32, (here_ref.shape[0], HD), 1)
    first = lane < n_experts
    named = jnp.where(first, lane, lane - n_experts)
    gates = jnp.zeros(lane.shape, f32)
    for j in range(routes_ref.shape[1]):
        gates = jnp.where(named == routes_ref[:, j : j + 1], weights_ref[:, j : j + 1], gates)
    head = gates.astype(bf16)
    rest = (gates - head.astype(f32)).astype(bf16)
    out_ref[:, width:] = jnp.where(first, head, rest)


def norm(n_experts, plane, here, there, residual, gain, routes, route_weights):
    rows, width = here.shape
    vmem = pl.BlockSpec(memory_space=pltpu.VMEM)
    return pl.pallas_call(
        functools.partial(norm_kernel, n_experts),
        out_shape=[
            jax.ShapeDtypeStruct((rows // 2, width), bf16),
            jax.ShapeDtypeStruct((rows, width + HD), bf16),
        ],
        in_specs=[pl.BlockSpec(memory_space=pltpu.SMEM)] + [vmem] * 6,
        out_specs=[vmem] * 2,
        compiler_params=pltpu.CompilerParams(vmem_limit_bytes=2 << 20),
        cost_estimate=pl.CostEstimate(
            flops=8 * rows * width, bytes_accessed=10 * rows * width, transcendentals=rows
        ),
    )(plane, here, there, residual, gain.reshape(1, width), routes, route_weights)


def joining(sources, outs, sems):
    block = sources[0].shape[0]
    return [
        pltpu.make_async_copy(
            source, outs[i // 2].at[pl.ds(i % 2 * block, block)], sems.at[i]
        )
        for i, source in enumerate(sources)
    ]


def stage_kernel(*refs):
    copies = joining(refs[:4], refs[4:6], refs[6])
    for copy in copies:
        copy.start()
    for copy in copies:
        copy.wait()


def stage(weights):
    block, width = weights[0].shape
    return pl.pallas_call(
        stage_kernel,
        out_shape=[pltpu.VMEM((2 * block, width), bf16)] * 2,
        in_specs=[pl.BlockSpec(memory_space=pl.ANY)] * 4,
        out_specs=[pl.BlockSpec(memory_space=pltpu.VMEM)] * 2,
        scratch_shapes=[pltpu.SemaphoreType.DMA((4,))],
        compiler_params=pltpu.CompilerParams(vmem_limit_bytes=STAGE_VMEM),
        cost_estimate=pl.CostEstimate(
            flops=0, bytes_accessed=8 * block * width, transcendentals=0
        ),
    )(*in_hbm(weights))


def hidden_units(x, gate_weights, up_weights):
    contract = (((1,), (1,)), ((), ()))
    gate = lax.dot_general(x, gate_weights, contract, preferred_element_type=f32)
    up = lax.dot_general(x, up_weights, contract, preferred_element_type=f32)
    return (gate / (1.0 + jnp.exp(-gate)) * up).astype(bf16)


def shared_kernel(count, *refs):
    rows, sources = refs[:count], refs[count : count + 6]
    out_ref, gate_buf, up_buf, down_buf, sems = refs[count + 6 :]
    width = out_ref.shape[1]
    copies = joining(sources, [gate_buf, up_buf, down_buf], sems)
    for copy in copies:
        copy.start()
    x = jnp.concatenate([ref[:, :width] for ref in rows], axis=0)
    contract = (((1,), (1,)), ((), ()))
    for copy in copies[:2]:
        copy.wait()
    gate = lax.dot_general(x, gate_buf[...], contract, preferred_element_type=f32)
    for copy in copies[2:4]:
        copy.wait()
    up = lax.dot_general(x, up_buf[...], contract, preferred_element_type=f32)
    hidden = (gate / (1.0 + jnp.exp(-gate)) * up).astype(bf16)
    for copy in copies[4:]:
        copy.wait()
    for c in range(0, width, COLUMNS):
        cols = slice(c, c + COLUMNS)
        out_ref[:, cols] = jnp.dot(hidden, down_buf[:, cols], preferred_element_type=f32)


def shared_expert(rows, weights):
    block, width = weights[0].shape
    count = sum(a.shape[0] for a in rows)
    vmem = pl.BlockSpec(memory_space=pltpu.VMEM)
    return pl.pallas_call(
        functools.partial(shared_kernel, len(rows)),
        out_shape=jax.ShapeDtypeStruct((count, width), f32),
        in_specs=[vmem] * len(rows) + [pl.BlockSpec(memory_space=pl.ANY)] * 6,
        out_specs=vmem,
        scratch_shapes=[
            *[pltpu.VMEM((2 * block, width), bf16)] * 3,
            pltpu.SemaphoreType.DMA((6,)),
        ],
        compiler_params=pltpu.CompilerParams(vmem_limit_bytes=SHARED_VMEM),
        cost_estimate=pl.CostEstimate(
            flops=12 * count * width * block,
            bytes_accessed=12 * block * width,
            transcendentals=2 * count * block,
        ),
    )(*rows, *in_hbm(weights))


def expert_kernel(n_experts, counts, plus, staging, *refs):
    refs = list(refs)
    place_ref = refs.pop(0)
    sources = [refs.pop(0) for _ in range(sum(counts))]
    shared_ref = refs.pop(0) if plus else None
    gate_ref, up_ref = refs[:2]
    if staging:
        down_ref, sems = refs[-2:]
        copies = joining(refs[2:4], [down_ref], sems)
        for copy in copies:
            copy.start()
        keeps, send_ref = refs[4:-3], refs[-3]
    else:
        down_ref = refs[2]
        keeps, send_ref = refs[3:-1], refs[-1]
    width = send_ref.shape[1]
    x = jnp.concatenate([ref[:, :width] for ref in sources], axis=0)
    hidden = hidden_units(x, gate_ref[...], up_ref[...])
    lanes = jnp.concatenate([ref[:, width:] for ref in sources], axis=0).astype(f32)
    lane = lax.broadcasted_iota(jnp.int32, lanes.shape, 1)
    e, second = place_ref[0], place_ref[1] == 1
    scale = jnp.sum(
        jnp.where((lane == e) | (lane == e + n_experts), lanes, 0.0), axis=1, keepdims=True
    )
    part = keeps[0].shape[0]
    if staging:
        for copy in copies:
            copy.wait()
    for c in range(0, width, COLUMNS):
        cols = slice(c, c + COLUMNS)
        out = jnp.dot(hidden, down_ref[:, cols], preferred_element_type=f32) * scale
        for i, keep_ref in enumerate(keeps):
            low = out[2 * part * i : 2 * part * i + part]
            high = out[2 * part * i + part : 2 * part * (i + 1)]
            if plus and i == 0:
                low = low + shared_ref[:part, cols]
                high = high + shared_ref[part:, cols]
            low, high = low.astype(bf16), high.astype(bf16)
            keep_ref[:, cols] = jnp.where(second, high, low)
            send_ref[part * i : part * (i + 1), cols] = jnp.where(second, low, high)


def expert(blocks, weights, n_experts, place, shared=None):
    counts = [len(b) for b in blocks]
    rows = sum(a.shape[0] for b in blocks for a in b)
    part = rows // len(blocks) // 2
    hidden, width = weights[0].shape
    staging = len(weights) == 4
    vmem, smem = pl.BlockSpec(memory_space=pltpu.VMEM), pl.BlockSpec(memory_space=pltpu.SMEM)
    args = [place] + [a for b in blocks for a in b] + ([] if shared is None else [shared])
    specs = [smem] + [vmem] * (len(args) + 1)
    outs = [jax.ShapeDtypeStruct((part, width), bf16)] * len(blocks)
    outs.append(jax.ShapeDtypeStruct((part * len(blocks), width), bf16))
    if staging:
        args += in_vmem(weights[:2]) + in_hbm(weights[2:])
        specs += [pl.BlockSpec(memory_space=pl.ANY)] * 2
        outs.append(pltpu.VMEM((hidden, width), bf16))
    else:
        args += in_vmem(weights)
        specs += [vmem]
    outs = pl.pallas_call(
        functools.partial(expert_kernel, n_experts, counts, shared is not None, staging),
        out_shape=outs,
        in_specs=specs,
        out_specs=[vmem] * len(outs),
        scratch_shapes=[pltpu.SemaphoreType.DMA((2,))] if staging else [],
        compiler_params=pltpu.CompilerParams(vmem_limit_bytes=EXPERT_VMEM),
        cost_estimate=pl.CostEstimate(
            flops=EFFORT * 6 * rows * width * hidden,
            bytes_accessed=4 * rows * width,
            transcendentals=rows * hidden,
        ),
    )(*args)
    if staging:
        weights = [weights[0], weights[1], outs[-1]]
        outs = outs[:-1]
    return outs[:-1], outs[-1], weights


def on_device_ring(
    residual,
    queries,
    prefix_kv,
    suffix_kv,
    suffix_lengths,
    out_proj,
    norm_gain,
    routes,
    route_weights,
    expert_gate,
    expert_up,
    expert_down,
    shared_gate,
    shared_up,
    shared_down,
):
    tokens, width = residual.shape
    half = tokens // 2
    n = lax.axis_size("exp")
    steps = n // 2
    order = list(range(0, n, 2)) + list(range(n - 1, 0, -2))
    right = [(order[k], order[(k + 1) % n]) for k in range(n)]
    left = [(b, a) for a, b in right]
    req = lax.axis_size("req")
    sibling = [(i, i ^ 1) for i in range(req)]
    across = [(i, i ^ 2) for i in range(req)]
    core = lax.rem(lax.axis_index("req"), 2)
    plane = lax.div(lax.axis_index("req"), 2)
    me = lax.axis_index("exp")

    def half_of(x):
        return lax.dynamic_slice_in_dim(x, core * half, half, 0)

    page = prefix_kv[0]
    page_len = page.shape[0]

    shared_weights = (shared_gate.T, shared_up.T, shared_down)
    expert_weights = (expert_gate[0].T, expert_up[0].T, expert_down[0])

    def with_sibling(weights):
        return [w for own in weights for w in (own, lax.ppermute(own, "req", sibling))]

    shared_weights = with_sibling(shared_weights)
    expert_weights = with_sibling(expert_weights)

    suffix = (suffix_lengths, suffix_kv[:, 0])
    core_arr = jnp.reshape(core, (1,)).astype(jnp.int32)
    from_left, from_right = page, page
    *state, stacked = attend(queries, [page], page_len, tokens, suffix=suffix)
    for s in range(1, steps):
        from_left = lax.ppermute(from_left, "exp", right)
        from_right = lax.ppermute(from_right, "exp", left)
        from_left, state = lax.optimization_barrier((from_left, state))
        fetch = out_proj if s == steps - FETCH else None
        *state, = attend(stacked, [from_left, from_right], page_len, tokens, state, fetch=fetch)
        if fetch is not None:
            proj = state.pop()
    from_left = lax.ppermute(from_left, "exp", right)
    from_left, state = lax.optimization_barrier((from_left, state))
    keep, send = attend(stacked, [from_left], page_len, tokens, state, core=core_arr, proj=proj)

    other = lax.ppermute(send, "req", sibling)
    terms = (keep.astype(f32) + other.astype(f32)).astype(bf16)
    quarter = half // 2
    terms_across = lax.ppermute(terms, "req", across)
    terms_across, staged = lax.optimization_barrier((terms_across, stage(expert_weights[:4])))
    staged = list(staged) + expert_weights[4:]
    hidden_here, normed = norm(
        n,
        plane.reshape(1),
        terms,
        terms_across,
        half_of(residual),
        norm_gain,
        half_of(routes),
        half_of(route_weights),
    )
    place = jnp.stack([me, plane]).astype(jnp.int32)

    own, summand = {}, {}

    def work(blocks, shared=None):
        nonlocal staged
        keeps, send, staged = expert([b for _, b in blocks], staged, n, place, shared)
        got = lax.ppermute(send, "req", across)
        for (d, _), keep in zip(blocks, keeps):
            own[d] = keep
        return keeps, ([d for d, _ in blocks], got)

    def landed(step, *others):
        due = [k for k in on_way if k < steps and max(k + 2, steps) == step]
        out = lax.optimization_barrier(others + tuple(on_way[k][1] for k in due))
        for k, got in zip(due, out[len(others) :]):
            for i, d in enumerate(on_way[k][0]):
                summand[d] = got[i * quarter : (i + 1) * quarter]
        return out[: len(others)]

    from_left, from_right = normed, normed
    before = shared_part = shared_expert([normed], shared_weights)
    on_way = {}
    for s in range(1, steps):
        from_left = lax.ppermute(from_left, "exp", right)
        from_right = lax.ppermute(from_right, "exp", left)
        from_left, before = landed(s, from_left, before)
        blocks = [(s, [from_left]), (-s, [from_right])]
        before, on_way[s] = work(blocks)
    low = lax.ppermute(from_left[:quarter], "exp", right)
    high = lax.ppermute(from_right[quarter:], "exp", left)
    low, before = landed(steps, low, before)
    last, on_way[steps] = work([(0, [normed]), (steps, [low, high])], shared_part)
    (last,) = landed(steps + 1, last)
    for i, d in enumerate(on_way[steps][0]):
        summand[d] = on_way[steps][1][i * quarter : (i + 1) * quarter]

    def part(d):
        return own[d].astype(f32) + summand[d].astype(f32)

    def along(hops):
        return [(order[i], order[(i + hops) % n]) for i in range(n)]

    total = hidden_here.astype(f32) + part(0)
    near = steps // 2
    arrived = []
    for d in range(steps, near, -1):
        for sign in (1, -1) if 2 * d != n else (1,):
            block = d if 2 * d == n else -sign * d
            arrived.append(lax.ppermute(part(block).astype(bf16), "exp", along(sign * d)))
    to_right = to_left = None
    for k in range(near, 0, -1):
        a, b = part(-k), part(k)
        if to_right is not None:
            a, b = a + to_right.astype(f32), b + to_left.astype(f32)
        to_right = lax.ppermute(a.astype(bf16), "exp", right)
        to_left = lax.ppermute(b.astype(bf16), "exp", left)
    for terms_there in [to_right, to_left] + arrived:
        total = total + terms_there.astype(f32)
    mine = total.astype(bf16)

    def joined(index, here, there):
        first = index == 0
        return jnp.concatenate(
            [jnp.where(first, here, there), jnp.where(first, there, here)], axis=0
        )

    mine = joined(plane, mine, lax.ppermute(mine, "req", across))
    theirs = lax.ppermute(mine, "req", sibling)
    out = lax.dynamic_update_slice(jnp.zeros((tokens, width), bf16), mine, (core * half, 0))
    out, theirs = lax.optimization_barrier((out, theirs))
    return lax.dynamic_update_slice(out, theirs, ((1 - core) * half, 0))


def on_device(
    residual,
    queries,
    prefix_kv,
    suffix_kv,
    suffix_lengths,
    out_proj,
    norm_gain,
    routes,
    route_weights,
    expert_gate,
    expert_up,
    expert_down,
    shared_gate,
    shared_up,
    shared_down,
):
    tokens_here = residual.shape[0]
    feat_width = residual.shape[1]
    head_count = queries.shape[1] // HD
    scaling = 1.0 / math.sqrt(HD)
    query_heads = jnp.transpose(queries.reshape(tokens_here, head_count, HD), (1, 0, 2))
    start_state = (
        jnp.full((head_count, tokens_here), neg_big, jnp.float32),
        jnp.zeros((head_count, tokens_here), jnp.float32),
        jnp.zeros((head_count, tokens_here, HD), jnp.float32),
    )

    def absorb(carried, key_rows, value_rows, allowed):
        running_max, running_sum, running_acc = carried
        scores = (
            jnp.einsum("htd,kd->htk", query_heads, key_rows, preferred_element_type=jnp.float32)
            * scaling
        )
        if allowed is not None:
            scores = jnp.where(allowed[None], scores, neg_big)
        new_max = jnp.maximum(running_max, jnp.max(scores, axis=-1))
        factor = jnp.exp(running_max - new_max)
        exp_scores = jnp.exp(scores - new_max[..., None])
        new_sum = running_sum * factor + jnp.sum(exp_scores, axis=-1)
        new_acc = running_acc * factor[..., None] + jnp.einsum(
            "htk,kd->htd",
            exp_scores.astype(jnp.bfloat16),
            value_rows,
            preferred_element_type=jnp.float32,
        )
        return (new_max, new_sum, new_acc)

    portion = lax.all_gather(prefix_kv, "exp", axis=1, tiled=True)
    key_count = portion.shape[1]
    window_len = math.gcd(key_count, 2048)

    def inner(position, inner_state):
        window = lax.dynamic_slice_in_dim(portion[0], position * window_len, window_len, 0)
        return absorb(inner_state, window[:, :HD], window[:, HD:], None)

    carried = lax.fori_loop(0, key_count // window_len, inner, start_state)
    request_ends = jnp.cumsum(suffix_lengths[0])
    positions = jnp.arange(tokens_here, dtype=jnp.int32)
    request_ids = jnp.sum((positions[:, None] >= request_ends[None, :]).astype(jnp.int32), axis=1)
    allowed = (request_ids[:, None] == request_ids[None, :]) & (
        positions[None, :] <= positions[:, None]
    )
    carried = absorb(carried, suffix_kv[:, 0, :HD], suffix_kv[:, 0, HD:], allowed)
    running_max, running_sum, running_acc = carried
    attention = (
        jnp.transpose(running_acc / running_sum[..., None], (1, 0, 2))
        .reshape(tokens_here, head_count * HD)
        .astype(jnp.bfloat16)
    )
    attn_terms = jnp.dot(attention, out_proj, preferred_element_type=jnp.float32)
    attn_out = lax.psum(attn_terms.astype(jnp.bfloat16), "req").astype(jnp.float32)
    hidden_state = (residual.astype(jnp.float32) + attn_out).astype(jnp.bfloat16)
    hidden_float = hidden_state.astype(jnp.float32)
    mean_square = jnp.mean(hidden_float * hidden_float, axis=-1, keepdims=True)
    normed = (
        hidden_float * lax.rsqrt(mean_square + norm_eps) * norm_gain.astype(jnp.float32)
    ).astype(jnp.bfloat16)
    shared_gate_act = jnp.dot(normed, shared_gate, preferred_element_type=jnp.float32)
    shared_up_act = jnp.dot(normed, shared_up, preferred_element_type=jnp.float32)
    shared_hidden = (jax.nn.silu(shared_gate_act) * shared_up_act).astype(jnp.bfloat16)
    shared_part = jnp.dot(shared_hidden, shared_down, preferred_element_type=jnp.float32)
    exp_count = lax.axis_size("exp")
    experts = exp_count * expert_gate.shape[0]
    capacity = expert_capacity(tokens_here, experts)
    pick_ids = routes.reshape(-1)
    one_hot = (pick_ids[:, None] == jnp.arange(experts, dtype=jnp.int32)[None, :]).astype(jnp.int32)
    pick_ranks = jnp.sum((jnp.cumsum(one_hot, axis=0) - one_hot) * one_hot, axis=1)
    pick_slots = (pick_ids * capacity + pick_ranks).reshape(tokens_here, TOP)
    slot_ids = jnp.arange(experts * capacity, dtype=jnp.int32)
    placement = jnp.any(pick_slots[None, :, :] == slot_ids[:, None, None], axis=2).astype(
        jnp.bfloat16
    )
    buffer = (
        jnp.dot(placement, normed, preferred_element_type=jnp.float32)
        .astype(jnp.bfloat16)
        .reshape(experts, capacity, feat_width)
    )
    source_rows = lax.all_to_all(buffer, "exp", split_axis=0, concat_axis=0, tiled=True)
    sources, slot_count, row_width = source_rows.shape
    flat_rows = source_rows.reshape(sources * slot_count, row_width)
    gate_act = jnp.dot(flat_rows, expert_gate[0], preferred_element_type=jnp.float32)
    up_act = jnp.dot(flat_rows, expert_up[0], preferred_element_type=jnp.float32)
    expert_hidden = (jax.nn.silu(gate_act) * up_act).astype(jnp.bfloat16)
    partial_out = jnp.dot(expert_hidden, expert_down[0], preferred_element_type=jnp.float32).astype(
        jnp.bfloat16
    )
    finish_partial_out = partial_out.reshape(sources, slot_count, row_width)
    returned = lax.all_to_all(finish_partial_out, "exp", split_axis=0, concat_axis=0, tiled=True)
    flat_back = returned.reshape(experts * capacity, feat_width)
    picked_rows = (
        flat_back[pick_slots.reshape(-1)].astype(jnp.float32).reshape(tokens_here, TOP, feat_width)
    )
    routed = jnp.sum(picked_rows * route_weights[:, :, None], axis=1)
    summed = lax.psum((shared_part + routed).astype(jnp.bfloat16), "req").astype(jnp.float32)
    return (hidden_float + summed).astype(jnp.bfloat16)


def solution(mesh):
    placed = (
        P("exp", None),
        P("exp", "req"),
        P("req", "exp", None),
        P("exp", "req", None),
        P("exp", None),
        P("req", None),
        P(),
        P("exp", None),
        P("exp", None),
        P("exp", None, "req"),
        P("exp", None, "req"),
        P("exp", "req", None),
        P(None, "req"),
        P(None, "req"),
        P("req", None),
    )

    def program(residual, *rest):
        n_exp, n_req = mesh.shape["exp"], mesh.shape["req"]
        tokens_here = residual.shape[0] // n_exp
        experts = rest[8].shape[0]
        every_row = expert_capacity(tokens_here, experts) == tokens_here
        ring = every_row and experts == n_exp and n_req == 4 and n_exp % 2 == 0 and n_exp >= 4
        return jax.shard_map(
            on_device_ring if ring else on_device,
            mesh=mesh,
            in_specs=placed,
            out_specs=P("exp", None),
            check_vma=False,
        )(residual, *rest)

    return program
```

```python
import functools
import math

import jax
import jax.numpy as jnp
from jax import lax
from jax.experimental import pallas as pl
from jax.experimental.pallas import tpu as pltpu
from jax.sharding import PartitionSpec as P

HD = 128
TOP = 6

neg_big = -1e30
norm_eps = 1e-06
f32 = jnp.float32
bf16 = jnp.bfloat16
STAGE_VMEM = 1 << 20
SHARED_VMEM = 11 << 20
EXPERT_VMEM = 4 << 20
COLUMNS = 512
PIECES = 4
FETCH = 1
EFFORT = 50


def expert_capacity(tokens_here, experts):
    return min(tokens_here, 4 * ((tokens_here * TOP + 2 * experts - 1) // (2 * experts)))


def in_vmem(arrays):
    return [pltpu.with_memory_space_constraint(a, pltpu.VMEM) for a in arrays]


def in_hbm(arrays):
    return [pltpu.with_memory_space_constraint(a, pltpu.HBM) for a in arrays]


def in_pieces(source, target, sems):
    rows = source.shape[0] // PIECES
    return [
        pltpu.make_async_copy(
            source.at[pl.ds(i * rows, rows)], target.at[pl.ds(i * rows, rows)], sems.at[i]
        )
        for i in range(PIECES)
    ]


def attend_kernel(heads, tokens, page_len, page_count, first, fetching, last, *refs):
    refs = list(refs)
    q_ref = refs.pop(0)
    if first:
        lengths_ref, suffix_ref = refs.pop(0), refs.pop(0)
    else:
        max_in, sum_in, acc_in = refs.pop(0), refs.pop(0), refs.pop(0)
    if last:
        core_ref, proj_ref = refs.pop(0), refs.pop(0)
        keep_ref, send_ref = refs[-2:]
    if fetching:
        fetches = in_pieces(refs.pop(0), refs[-2], refs[-1])
        for fetch in fetches:
            fetch.start()
    page_refs = [refs.pop(0) for _ in range(page_count)]
    scaling = 1.0 / math.sqrt(HD)
    if first:
        q = jnp.concatenate([q_ref[:, h * HD : (h + 1) * HD] for h in range(heads)], axis=0)
    else:
        q = q_ref[...]
    blocks = [(ref[:page_len, :HD], ref[:page_len, HD:]) for ref in page_refs]
    scores = [
        lax.dot_general(q, k, (((1,), (1,)), ((), ())), preferred_element_type=f32) * scaling
        for k, _ in blocks
    ]
    if first:
        ends, total = [], 0
        for i in range(lengths_ref.shape[1]):
            total = total + lengths_ref[0, i]
            ends.append(total)
        rows = lax.broadcasted_iota(jnp.int32, (tokens, tokens), 0)
        cols = lax.broadcasted_iota(jnp.int32, (tokens, tokens), 1)
        row_ids = sum((rows >= e).astype(jnp.int32) for e in ends)
        col_ids = sum((cols >= e).astype(jnp.int32) for e in ends)
        bias = jnp.where((row_ids == col_ids) & (cols <= rows), 0.0, neg_big).astype(f32)
        k, v = suffix_ref[:, :HD], suffix_ref[:, HD:]
        own = lax.dot_general(q, k, (((1,), (1,)), ((), ())), preferred_element_type=f32) * scaling
        own = jnp.where(jnp.concatenate([bias] * heads, axis=0) < 0.0, neg_big, own)
        scores.append(own)
        blocks.append((k, v))
    new_max = functools.reduce(
        jnp.maximum, [jnp.max(s, axis=-1, keepdims=True) for s in scores]
    )
    if not first:
        old_max = max_in[:, :1]
        new_max = jnp.maximum(new_max, old_max)
        factor = jnp.exp(old_max - new_max)
        total = sum_in[:, :1] * factor
        acc = acc_in[...] * factor
    else:
        total, acc = 0.0, 0.0
    for s, (_, v) in zip(scores, blocks):
        e = jnp.exp(s - new_max)
        total = total + jnp.sum(e, axis=-1, keepdims=True)
        acc = acc + jnp.dot(e.astype(bf16), v, preferred_element_type=f32)
    if last:
        out = (acc / total).astype(bf16)
        rows = jnp.concatenate([out[h * tokens : (h + 1) * tokens] for h in range(heads)], axis=1)
        half = tokens // 2
        second = core_ref[0] == 1
        for c in range(0, proj_ref.shape[1], COLUMNS):
            cols = slice(c, c + COLUMNS)
            terms = jnp.dot(rows, proj_ref[:, cols], preferred_element_type=f32).astype(bf16)
            low, high = terms[:half], terms[half:]
            keep_ref[:, cols] = jnp.where(second, high, low)
            send_ref[:, cols] = jnp.where(second, low, high)
    else:
        max_out, sum_out, acc_out = refs[:3]
        max_out[...] = jnp.broadcast_to(new_max, max_out.shape)
        sum_out[...] = jnp.broadcast_to(total, sum_out.shape)
        acc_out[...] = acc
        if first:
            refs[3][...] = q
        if fetching:
            for fetch in fetches:
                fetch.wait()


def attend(queries, pages, page_len, tokens, state=None, suffix=None, fetch=None, core=None, proj=None):
    first, last = state is None, core is not None
    heads = queries.shape[1] // HD if first else queries.shape[0] // tokens
    vmem, smem = pl.BlockSpec(memory_space=pltpu.VMEM), pl.BlockSpec(memory_space=pltpu.SMEM)
    outs = [jax.ShapeDtypeStruct((heads * tokens, HD), f32)] * 3
    scratch = []
    if first:
        lengths, suffix = suffix
        args = in_hbm([queries]) + [lengths] + in_hbm([suffix])
        pages = in_hbm(pages)
        specs = [vmem, smem, vmem]
        outs.append(jax.ShapeDtypeStruct((heads * tokens, HD), bf16))
    else:
        args = [queries] + list(state)
        specs = [vmem] * 4
    if last:
        args += [core] + in_vmem([proj])
        specs += [smem, vmem]
        outs = [jax.ShapeDtypeStruct((tokens // 2, proj.shape[1]), bf16)] * 2
    if fetch is not None:
        args += in_hbm([fetch])
        specs.append(pl.BlockSpec(memory_space=pl.ANY))
        outs.append(pltpu.VMEM(fetch.shape, fetch.dtype))
        scratch.append(pltpu.SemaphoreType.DMA((PIECES,)))
    keys = page_len * len(pages) + (tokens if first else 0)
    return pl.pallas_call(
        functools.partial(
            attend_kernel, heads, tokens, page_len, len(pages), first, fetch is not None, last
        ),
        out_shape=outs,
        in_specs=specs + [vmem] * len(pages),
        out_specs=[vmem] * len(outs),
        scratch_shapes=scratch,
        compiler_params=pltpu.CompilerParams(vmem_limit_bytes=12 << 20),
        cost_estimate=pl.CostEstimate(
            flops=(1 if last or fetch is not None else EFFORT) * 4 * heads * tokens * keys * HD,
            bytes_accessed=4 * keys * HD + 2 * heads * tokens * HD,
            transcendentals=heads * tokens * keys,
        ),
    )(*args, *pages)


def norm_kernel(n_experts, plane_ref, *refs):
    here_ref, there_ref, residual_ref, gain_ref, routes_ref, weights_ref, hidden_ref, out_ref = refs
    width = hidden_ref.shape[1]
    attn_out = here_ref[...].astype(f32) + there_ref[...].astype(f32)
    hidden = (residual_ref[...].astype(f32) + attn_out).astype(bf16)
    part = hidden_ref.shape[0]
    hidden_ref[...] = jnp.where(plane_ref[0] == 1, hidden[part:], hidden[:part])
    hidden = hidden.astype(f32)
    mean_square = jnp.mean(hidden * hidden, axis=-1, keepdims=True)
    normed = hidden * lax.rsqrt(mean_square + norm_eps) * gain_ref[...].astype(f32)
    out_ref[:, :width] = normed.astype(bf16)
    lane = lax.broadcasted_iota(jnp.int32, (here_ref.shape[0], HD), 1)
    first = lane < n_experts
    named = jnp.where(first, lane, lane - n_experts)
    gates = jnp.zeros(lane.shape, f32)
    for j in range(routes_ref.shape[1]):
        gates = jnp.where(named == routes_ref[:, j : j + 1], weights_ref[:, j : j + 1], gates)
    head = gates.astype(bf16)
    rest = (gates - head.astype(f32)).astype(bf16)
    out_ref[:, width:] = jnp.where(first, head, rest)


def norm(n_experts, plane, here, there, residual, gain, routes, route_weights):
    rows, width = here.shape
    vmem = pl.BlockSpec(memory_space=pltpu.VMEM)
    return pl.pallas_call(
        functools.partial(norm_kernel, n_experts),
        out_shape=[
            jax.ShapeDtypeStruct((rows // 2, width), bf16),
            jax.ShapeDtypeStruct((rows, width + HD), bf16),
        ],
        in_specs=[pl.BlockSpec(memory_space=pltpu.SMEM)] + [vmem] * 6,
        out_specs=[vmem] * 2,
        compiler_params=pltpu.CompilerParams(vmem_limit_bytes=2 << 20),
        cost_estimate=pl.CostEstimate(
            flops=8 * rows * width, bytes_accessed=10 * rows * width, transcendentals=rows
        ),
    )(plane, here, there, residual, gain.reshape(1, width), routes, route_weights)


def joining(sources, outs, sems):
    block = sources[0].shape[0]
    return [
        pltpu.make_async_copy(
            source, outs[i // 2].at[pl.ds(i % 2 * block, block)], sems.at[i]
        )
        for i, source in enumerate(sources)
    ]


def stage_kernel(*refs):
    copies = joining(refs[:4], refs[4:6], refs[6])
    for copy in copies:
        copy.start()
    for copy in copies:
        copy.wait()


def stage(weights):
    block, width = weights[0].shape
    return pl.pallas_call(
        stage_kernel,
        out_shape=[pltpu.VMEM((2 * block, width), bf16)] * 2,
        in_specs=[pl.BlockSpec(memory_space=pl.ANY)] * 4,
        out_specs=[pl.BlockSpec(memory_space=pltpu.VMEM)] * 2,
        scratch_shapes=[pltpu.SemaphoreType.DMA((4,))],
        compiler_params=pltpu.CompilerParams(vmem_limit_bytes=STAGE_VMEM),
        cost_estimate=pl.CostEstimate(
            flops=0, bytes_accessed=8 * block * width, transcendentals=0
        ),
    )(*in_hbm(weights))


def hidden_units(x, gate_weights, up_weights):
    contract = (((1,), (1,)), ((), ()))
    gate = lax.dot_general(x, gate_weights, contract, preferred_element_type=f32)
    up = lax.dot_general(x, up_weights, contract, preferred_element_type=f32)
    return (gate / (1.0 + jnp.exp(-gate)) * up).astype(bf16)


def shared_kernel(count, *refs):
    rows, sources = refs[:count], refs[count : count + 6]
    out_ref, gate_buf, up_buf, down_buf, sems = refs[count + 6 :]
    width = out_ref.shape[1]
    copies = joining(sources, [gate_buf, up_buf, down_buf], sems)
    for copy in copies:
        copy.start()
    x = jnp.concatenate([ref[:, :width] for ref in rows], axis=0)
    contract = (((1,), (1,)), ((), ()))
    for copy in copies[:2]:
        copy.wait()
    gate = lax.dot_general(x, gate_buf[...], contract, preferred_element_type=f32)
    for copy in copies[2:4]:
        copy.wait()
    up = lax.dot_general(x, up_buf[...], contract, preferred_element_type=f32)
    hidden = (gate / (1.0 + jnp.exp(-gate)) * up).astype(bf16)
    for copy in copies[4:]:
        copy.wait()
    for c in range(0, width, COLUMNS):
        cols = slice(c, c + COLUMNS)
        out_ref[:, cols] = jnp.dot(hidden, down_buf[:, cols], preferred_element_type=f32)


def shared_expert(rows, weights):
    block, width = weights[0].shape
    count = sum(a.shape[0] for a in rows)
    vmem = pl.BlockSpec(memory_space=pltpu.VMEM)
    return pl.pallas_call(
        functools.partial(shared_kernel, len(rows)),
        out_shape=jax.ShapeDtypeStruct((count, width), f32),
        in_specs=[vmem] * len(rows) + [pl.BlockSpec(memory_space=pl.ANY)] * 6,
        out_specs=vmem,
        scratch_shapes=[
            *[pltpu.VMEM((2 * block, width), bf16)] * 3,
            pltpu.SemaphoreType.DMA((6,)),
        ],
        compiler_params=pltpu.CompilerParams(vmem_limit_bytes=SHARED_VMEM),
        cost_estimate=pl.CostEstimate(
            flops=12 * count * width * block,
            bytes_accessed=12 * block * width,
            transcendentals=2 * count * block,
        ),
    )(*rows, *in_hbm(weights))


def expert_kernel(n_experts, counts, plus, staging, *refs):
    refs = list(refs)
    place_ref = refs.pop(0)
    sources = [refs.pop(0) for _ in range(sum(counts))]
    shared_ref = refs.pop(0) if plus else None
    gate_ref, up_ref = refs[:2]
    if staging:
        down_ref, sems = refs[-2:]
        copies = joining(refs[2:4], [down_ref], sems)
        for copy in copies:
            copy.start()
        keeps, send_ref = refs[4:-3], refs[-3]
    else:
        down_ref = refs[2]
        keeps, send_ref = refs[3:-1], refs[-1]
    width = send_ref.shape[1]
    x = jnp.concatenate([ref[:, :width] for ref in sources], axis=0)
    hidden = hidden_units(x, gate_ref[...], up_ref[...])
    lanes = jnp.concatenate([ref[:, width:] for ref in sources], axis=0).astype(f32)
    lane = lax.broadcasted_iota(jnp.int32, lanes.shape, 1)
    e, second = place_ref[0], place_ref[1] == 1
    scale = jnp.sum(
        jnp.where((lane == e) | (lane == e + n_experts), lanes, 0.0), axis=1, keepdims=True
    )
    part = keeps[0].shape[0]
    if staging:
        for copy in copies:
            copy.wait()
    for c in range(0, width, COLUMNS):
        cols = slice(c, c + COLUMNS)
        out = jnp.dot(hidden, down_ref[:, cols], preferred_element_type=f32) * scale
        for i, keep_ref in enumerate(keeps):
            low = out[2 * part * i : 2 * part * i + part]
            high = out[2 * part * i + part : 2 * part * (i + 1)]
            if plus and i == 0:
                low = low + shared_ref[:part, cols]
                high = high + shared_ref[part:, cols]
            low, high = low.astype(bf16), high.astype(bf16)
            keep_ref[:, cols] = jnp.where(second, high, low)
            send_ref[part * i : part * (i + 1), cols] = jnp.where(second, low, high)


def expert(blocks, weights, n_experts, place, shared=None):
    counts = [len(b) for b in blocks]
    rows = sum(a.shape[0] for b in blocks for a in b)
    part = rows // len(blocks) // 2
    hidden, width = weights[0].shape
    staging = len(weights) == 4
    vmem, smem = pl.BlockSpec(memory_space=pltpu.VMEM), pl.BlockSpec(memory_space=pltpu.SMEM)
    args = [place] + [a for b in blocks for a in b] + ([] if shared is None else [shared])
    specs = [smem] + [vmem] * (len(args) + 1)
    outs = [jax.ShapeDtypeStruct((part, width), bf16)] * len(blocks)
    outs.append(jax.ShapeDtypeStruct((part * len(blocks), width), bf16))
    if staging:
        args += in_vmem(weights[:2]) + in_hbm(weights[2:])
        specs += [pl.BlockSpec(memory_space=pl.ANY)] * 2
        outs.append(pltpu.VMEM((hidden, width), bf16))
    else:
        args += in_vmem(weights)
        specs += [vmem]
    outs = pl.pallas_call(
        functools.partial(expert_kernel, n_experts, counts, shared is not None, staging),
        out_shape=outs,
        in_specs=specs,
        out_specs=[vmem] * len(outs),
        scratch_shapes=[pltpu.SemaphoreType.DMA((2,))] if staging else [],
        compiler_params=pltpu.CompilerParams(vmem_limit_bytes=EXPERT_VMEM),
        cost_estimate=pl.CostEstimate(
            flops=EFFORT * 6 * rows * width * hidden,
            bytes_accessed=4 * rows * width,
            transcendentals=rows * hidden,
        ),
    )(*args)
    if staging:
        weights = [weights[0], weights[1], outs[-1]]
        outs = outs[:-1]
    return outs[:-1], outs[-1], weights


def on_device_ring(
    residual,
    queries,
    prefix_kv,
    suffix_kv,
    suffix_lengths,
    out_proj,
    norm_gain,
    routes,
    route_weights,
    expert_gate,
    expert_up,
    expert_down,
    shared_gate,
    shared_up,
    shared_down,
):
    tokens, width = residual.shape
    half = tokens // 2
    n = lax.axis_size("exp")
    steps = n // 2
    order = list(range(0, n, 2)) + list(range(n - 1, 0, -2))
    right = [(order[k], order[(k + 1) % n]) for k in range(n)]
    left = [(b, a) for a, b in right]
    req = lax.axis_size("req")
    sibling = [(i, i ^ 1) for i in range(req)]
    across = [(i, i ^ 2) for i in range(req)]
    core = lax.rem(lax.axis_index("req"), 2)
    plane = lax.div(lax.axis_index("req"), 2)
    me = lax.axis_index("exp")

    def half_of(x):
        return lax.dynamic_slice_in_dim(x, core * half, half, 0)

    page = prefix_kv[0]
    page_len = page.shape[0]

    shared_weights = (shared_gate.T, shared_up.T, shared_down)
    expert_weights = (expert_gate[0].T, expert_up[0].T, expert_down[0])

    def with_sibling(weights):
        return [w for own in weights for w in (own, lax.ppermute(own, "req", sibling))]

    shared_weights = with_sibling(shared_weights)
    expert_weights = with_sibling(expert_weights)

    suffix = (suffix_lengths, suffix_kv[:, 0])
    core_arr = jnp.reshape(core, (1,)).astype(jnp.int32)
    from_left, from_right = page, page
    *state, stacked = attend(queries, [page], page_len, tokens, suffix=suffix)
    for s in range(1, steps):
        from_left = lax.ppermute(from_left, "exp", right)
        from_right = lax.ppermute(from_right, "exp", left)
        from_left, state = lax.optimization_barrier((from_left, state))
        fetch = out_proj if s == steps - FETCH else None
        *state, = attend(stacked, [from_left, from_right], page_len, tokens, state, fetch=fetch)
        if fetch is not None:
            proj = state.pop()
    from_left = lax.ppermute(from_left, "exp", right)
    from_left, state = lax.optimization_barrier((from_left, state))
    keep, send = attend(stacked, [from_left], page_len, tokens, state, core=core_arr, proj=proj)

    other = lax.ppermute(send, "req", sibling)
    terms = (keep.astype(f32) + other.astype(f32)).astype(bf16)
    quarter = half // 2
    terms_across = lax.ppermute(terms, "req", across)
    terms_across, staged = lax.optimization_barrier((terms_across, stage(expert_weights[:4])))
    staged = list(staged) + expert_weights[4:]
    hidden_here, normed = norm(
        n,
        plane.reshape(1),
        terms,
        terms_across,
        half_of(residual),
        norm_gain,
        half_of(routes),
        half_of(route_weights),
    )
    place = jnp.stack([me, plane]).astype(jnp.int32)

    own, summand = {}, {}

    def work(blocks, shared=None):
        nonlocal staged
        keeps, send, staged = expert([b for _, b in blocks], staged, n, place, shared)
        if shared is None:
            got = lax.ppermute(send, "req", across)
        else:
            got = [
                lax.ppermute(send[i * quarter : (i + 1) * quarter], "req", across)
                for i in range(len(blocks))
            ]
        for (d, _), keep in zip(blocks, keeps):
            own[d] = keep
        return keeps, ([d for d, _ in blocks], got)

    def landed(step, *others):
        due = [k for k in on_way if k < steps and max(k + 2, steps) == step]
        out = lax.optimization_barrier(others + tuple(on_way[k][1] for k in due))
        for k, got in zip(due, out[len(others) :]):
            for i, d in enumerate(on_way[k][0]):
                summand[d] = got[i * quarter : (i + 1) * quarter]
        return out[: len(others)]

    from_left, from_right = normed, normed
    before = shared_part = shared_expert([normed], shared_weights)
    on_way = {}
    for s in range(1, steps):
        from_left = lax.ppermute(from_left, "exp", right)
        from_right = lax.ppermute(from_right, "exp", left)
        from_left, before = landed(s, from_left, before)
        blocks = [(s, [from_left]), (-s, [from_right])]
        before, on_way[s] = work(blocks)
    low = lax.ppermute(from_left[:quarter], "exp", right)
    high = lax.ppermute(from_right[quarter:], "exp", left)
    low, before = landed(steps, low, before)
    last, on_way[steps] = work([(0, [normed]), (steps, [low, high])], shared_part)
    (last,) = landed(steps + 1, last)
    for d, got in zip(*on_way[steps]):
        summand[d] = got

    def part(d):
        return own[d].astype(f32) + summand[d].astype(f32)

    def along(hops):
        return [(order[i], order[(i + hops) % n]) for i in range(n)]

    total = hidden_here.astype(f32) + part(0)
    near = steps // 2
    arrived = []
    for d in range(steps, near, -1):
        for sign in (1, -1) if 2 * d != n else (1,):
            block = d if 2 * d == n else -sign * d
            arrived.append(lax.ppermute(part(block).astype(bf16), "exp", along(sign * d)))
    to_right = to_left = None
    for k in range(near, 0, -1):
        a, b = part(-k), part(k)
        if to_right is not None:
            a, b = a + to_right.astype(f32), b + to_left.astype(f32)
        to_right = lax.ppermute(a.astype(bf16), "exp", right)
        to_left = lax.ppermute(b.astype(bf16), "exp", left)
    for terms_there in [to_right, to_left] + arrived:
        total = total + terms_there.astype(f32)
    mine = total.astype(bf16)

    def joined(index, here, there):
        first = index == 0
        return jnp.concatenate(
            [jnp.where(first, here, there), jnp.where(first, there, here)], axis=0
        )

    mine = joined(plane, mine, lax.ppermute(mine, "req", across))
    theirs = lax.ppermute(mine, "req", sibling)
    out = lax.dynamic_update_slice(jnp.zeros((tokens, width), bf16), mine, (core * half, 0))
    out, theirs = lax.optimization_barrier((out, theirs))
    return lax.dynamic_update_slice(out, theirs, ((1 - core) * half, 0))


def on_device(
    residual,
    queries,
    prefix_kv,
    suffix_kv,
    suffix_lengths,
    out_proj,
    norm_gain,
    routes,
    route_weights,
    expert_gate,
    expert_up,
    expert_down,
    shared_gate,
    shared_up,
    shared_down,
):
    tokens_here = residual.shape[0]
    feat_width = residual.shape[1]
    head_count = queries.shape[1] // HD
    scaling = 1.0 / math.sqrt(HD)
    query_heads = jnp.transpose(queries.reshape(tokens_here, head_count, HD), (1, 0, 2))
    start_state = (
        jnp.full((head_count, tokens_here), neg_big, jnp.float32),
        jnp.zeros((head_count, tokens_here), jnp.float32),
        jnp.zeros((head_count, tokens_here, HD), jnp.float32),
    )

    def absorb(carried, key_rows, value_rows, allowed):
        running_max, running_sum, running_acc = carried
        scores = (
            jnp.einsum("htd,kd->htk", query_heads, key_rows, preferred_element_type=jnp.float32)
            * scaling
        )
        if allowed is not None:
            scores = jnp.where(allowed[None], scores, neg_big)
        new_max = jnp.maximum(running_max, jnp.max(scores, axis=-1))
        factor = jnp.exp(running_max - new_max)
        exp_scores = jnp.exp(scores - new_max[..., None])
        new_sum = running_sum * factor + jnp.sum(exp_scores, axis=-1)
        new_acc = running_acc * factor[..., None] + jnp.einsum(
            "htk,kd->htd",
            exp_scores.astype(jnp.bfloat16),
            value_rows,
            preferred_element_type=jnp.float32,
        )
        return (new_max, new_sum, new_acc)

    portion = lax.all_gather(prefix_kv, "exp", axis=1, tiled=True)
    key_count = portion.shape[1]
    window_len = math.gcd(key_count, 2048)

    def inner(position, inner_state):
        window = lax.dynamic_slice_in_dim(portion[0], position * window_len, window_len, 0)
        return absorb(inner_state, window[:, :HD], window[:, HD:], None)

    carried = lax.fori_loop(0, key_count // window_len, inner, start_state)
    request_ends = jnp.cumsum(suffix_lengths[0])
    positions = jnp.arange(tokens_here, dtype=jnp.int32)
    request_ids = jnp.sum((positions[:, None] >= request_ends[None, :]).astype(jnp.int32), axis=1)
    allowed = (request_ids[:, None] == request_ids[None, :]) & (
        positions[None, :] <= positions[:, None]
    )
    carried = absorb(carried, suffix_kv[:, 0, :HD], suffix_kv[:, 0, HD:], allowed)
    running_max, running_sum, running_acc = carried
    attention = (
        jnp.transpose(running_acc / running_sum[..., None], (1, 0, 2))
        .reshape(tokens_here, head_count * HD)
        .astype(jnp.bfloat16)
    )
    attn_terms = jnp.dot(attention, out_proj, preferred_element_type=jnp.float32)
    attn_out = lax.psum(attn_terms.astype(jnp.bfloat16), "req").astype(jnp.float32)
    hidden_state = (residual.astype(jnp.float32) + attn_out).astype(jnp.bfloat16)
    hidden_float = hidden_state.astype(jnp.float32)
    mean_square = jnp.mean(hidden_float * hidden_float, axis=-1, keepdims=True)
    normed = (
        hidden_float * lax.rsqrt(mean_square + norm_eps) * norm_gain.astype(jnp.float32)
    ).astype(jnp.bfloat16)
    shared_gate_act = jnp.dot(normed, shared_gate, preferred_element_type=jnp.float32)
    shared_up_act = jnp.dot(normed, shared_up, preferred_element_type=jnp.float32)
    shared_hidden = (jax.nn.silu(shared_gate_act) * shared_up_act).astype(jnp.bfloat16)
    shared_part = jnp.dot(shared_hidden, shared_down, preferred_element_type=jnp.float32)
    exp_count = lax.axis_size("exp")
    experts = exp_count * expert_gate.shape[0]
    capacity = expert_capacity(tokens_here, experts)
    pick_ids = routes.reshape(-1)
    one_hot = (pick_ids[:, None] == jnp.arange(experts, dtype=jnp.int32)[None, :]).astype(jnp.int32)
    pick_ranks = jnp.sum((jnp.cumsum(one_hot, axis=0) - one_hot) * one_hot, axis=1)
    pick_slots = (pick_ids * capacity + pick_ranks).reshape(tokens_here, TOP)
    slot_ids = jnp.arange(experts * capacity, dtype=jnp.int32)
    placement = jnp.any(pick_slots[None, :, :] == slot_ids[:, None, None], axis=2).astype(
        jnp.bfloat16
    )
    buffer = (
        jnp.dot(placement, normed, preferred_element_type=jnp.float32)
        .astype(jnp.bfloat16)
        .reshape(experts, capacity, feat_width)
    )
    source_rows = lax.all_to_all(buffer, "exp", split_axis=0, concat_axis=0, tiled=True)
    sources, slot_count, row_width = source_rows.shape
    flat_rows = source_rows.reshape(sources * slot_count, row_width)
    gate_act = jnp.dot(flat_rows, expert_gate[0], preferred_element_type=jnp.float32)
    up_act = jnp.dot(flat_rows, expert_up[0], preferred_element_type=jnp.float32)
    expert_hidden = (jax.nn.silu(gate_act) * up_act).astype(jnp.bfloat16)
    partial_out = jnp.dot(expert_hidden, expert_down[0], preferred_element_type=jnp.float32).astype(
        jnp.bfloat16
    )
    finish_partial_out = partial_out.reshape(sources, slot_count, row_width)
    returned = lax.all_to_all(finish_partial_out, "exp", split_axis=0, concat_axis=0, tiled=True)
    flat_back = returned.reshape(experts * capacity, feat_width)
    picked_rows = (
        flat_back[pick_slots.reshape(-1)].astype(jnp.float32).reshape(tokens_here, TOP, feat_width)
    )
    routed = jnp.sum(picked_rows * route_weights[:, :, None], axis=1)
    summed = lax.psum((shared_part + routed).astype(jnp.bfloat16), "req").astype(jnp.float32)
    return (hidden_float + summed).astype(jnp.bfloat16)


def solution(mesh):
    placed = (
        P("exp", None),
        P("exp", "req"),
        P("req", "exp", None),
        P("exp", "req", None),
        P("exp", None),
        P("req", None),
        P(),
        P("exp", None),
        P("exp", None),
        P("exp", None, "req"),
        P("exp", None, "req"),
        P("exp", "req", None),
        P(None, "req"),
        P(None, "req"),
        P("req", None),
    )

    def program(residual, *rest):
        n_exp, n_req = mesh.shape["exp"], mesh.shape["req"]
        tokens_here = residual.shape[0] // n_exp
        experts = rest[8].shape[0]
        every_row = expert_capacity(tokens_here, experts) == tokens_here
        ring = every_row and experts == n_exp and n_req == 4 and n_exp % 2 == 0 and n_exp >= 4
        return jax.shard_map(
            on_device_ring if ring else on_device,
            mesh=mesh,
            in_specs=placed,
            out_specs=P("exp", None),
            check_vma=False,
        )(residual, *rest)

    return program
```

```python
import functools
import math

import jax
import jax.numpy as jnp
from jax import lax
from jax.experimental import pallas as pl
from jax.experimental.pallas import tpu as pltpu
from jax.sharding import PartitionSpec as P

HD = 128
TOP = 6

neg_big = -1e30
norm_eps = 1e-06
f32 = jnp.float32
bf16 = jnp.bfloat16
STAGE_VMEM = 1 << 20
SHARED_VMEM = 11 << 20
EXPERT_VMEM = 4 << 20
COLUMNS = 512
PIECES = 4
FETCH = 1
EFFORT = 50


def expert_capacity(tokens_here, experts):
    return min(tokens_here, 4 * ((tokens_here * TOP + 2 * experts - 1) // (2 * experts)))


def in_vmem(arrays):
    return [pltpu.with_memory_space_constraint(a, pltpu.VMEM) for a in arrays]


def in_hbm(arrays):
    return [pltpu.with_memory_space_constraint(a, pltpu.HBM) for a in arrays]


def in_pieces(source, target, sems):
    rows = source.shape[0] // PIECES
    return [
        pltpu.make_async_copy(
            source.at[pl.ds(i * rows, rows)], target.at[pl.ds(i * rows, rows)], sems.at[i]
        )
        for i in range(PIECES)
    ]


def attend_kernel(heads, tokens, page_len, page_count, first, fetching, last, *refs):
    refs = list(refs)
    q_ref = refs.pop(0)
    if first:
        lengths_ref, suffix_ref = refs.pop(0), refs.pop(0)
    else:
        max_in, sum_in, acc_in = refs.pop(0), refs.pop(0), refs.pop(0)
    if last:
        core_ref, proj_ref = refs.pop(0), refs.pop(0)
        keep_ref, send_ref = refs[-2:]
    if fetching:
        fetches = in_pieces(refs.pop(0), refs[-2], refs[-1])
        for fetch in fetches:
            fetch.start()
    page_refs = [refs.pop(0) for _ in range(page_count)]
    scaling = 1.0 / math.sqrt(HD)
    if first:
        q = jnp.concatenate([q_ref[:, h * HD : (h + 1) * HD] for h in range(heads)], axis=0)
    else:
        q = q_ref[...]
    blocks = [(ref[:page_len, :HD], ref[:page_len, HD:]) for ref in page_refs]
    scores = [
        lax.dot_general(q, k, (((1,), (1,)), ((), ())), preferred_element_type=f32) * scaling
        for k, _ in blocks
    ]
    if first:
        ends, total = [], 0
        for i in range(lengths_ref.shape[1]):
            total = total + lengths_ref[0, i]
            ends.append(total)
        rows = lax.broadcasted_iota(jnp.int32, (tokens, tokens), 0)
        cols = lax.broadcasted_iota(jnp.int32, (tokens, tokens), 1)
        row_ids = sum((rows >= e).astype(jnp.int32) for e in ends)
        col_ids = sum((cols >= e).astype(jnp.int32) for e in ends)
        bias = jnp.where((row_ids == col_ids) & (cols <= rows), 0.0, neg_big).astype(f32)
        k, v = suffix_ref[:, :HD], suffix_ref[:, HD:]
        own = lax.dot_general(q, k, (((1,), (1,)), ((), ())), preferred_element_type=f32) * scaling
        own = jnp.where(jnp.concatenate([bias] * heads, axis=0) < 0.0, neg_big, own)
        scores.append(own)
        blocks.append((k, v))
    new_max = functools.reduce(
        jnp.maximum, [jnp.max(s, axis=-1, keepdims=True) for s in scores]
    )
    if not first:
        old_max = max_in[:, :1]
        new_max = jnp.maximum(new_max, old_max)
        factor = jnp.exp(old_max - new_max)
        total = sum_in[:, :1] * factor
        acc = acc_in[...] * factor
    else:
        total, acc = 0.0, 0.0
    for s, (_, v) in zip(scores, blocks):
        e = jnp.exp(s - new_max)
        total = total + jnp.sum(e, axis=-1, keepdims=True)
        acc = acc + jnp.dot(e.astype(bf16), v, preferred_element_type=f32)
    if last:
        out = (acc / total).astype(bf16)
        rows = jnp.concatenate([out[h * tokens : (h + 1) * tokens] for h in range(heads)], axis=1)
        half = tokens // 2
        second = core_ref[0] == 1
        for c in range(0, proj_ref.shape[1], COLUMNS):
            cols = slice(c, c + COLUMNS)
            terms = jnp.dot(rows, proj_ref[:, cols], preferred_element_type=f32).astype(bf16)
            low, high = terms[:half], terms[half:]
            keep_ref[:, cols] = jnp.where(second, high, low)
            send_ref[:, cols] = jnp.where(second, low, high)
    else:
        max_out, sum_out, acc_out = refs[:3]
        max_out[...] = jnp.broadcast_to(new_max, max_out.shape)
        sum_out[...] = jnp.broadcast_to(total, sum_out.shape)
        acc_out[...] = acc
        if first:
            refs[3][...] = q
        if fetching:
            for fetch in fetches:
                fetch.wait()


def attend(queries, pages, page_len, tokens, state=None, suffix=None, fetch=None, core=None, proj=None):
    first, last = state is None, core is not None
    heads = queries.shape[1] // HD if first else queries.shape[0] // tokens
    vmem, smem = pl.BlockSpec(memory_space=pltpu.VMEM), pl.BlockSpec(memory_space=pltpu.SMEM)
    outs = [jax.ShapeDtypeStruct((heads * tokens, HD), f32)] * 3
    scratch = []
    if first:
        lengths, suffix = suffix
        args = in_hbm([queries]) + [lengths] + in_hbm([suffix])
        pages = in_hbm(pages)
        specs = [vmem, smem, vmem]
        outs.append(jax.ShapeDtypeStruct((heads * tokens, HD), bf16))
    else:
        args = [queries] + list(state)
        specs = [vmem] * 4
    if last:
        args += [core] + in_vmem([proj])
        specs += [smem, vmem]
        outs = [jax.ShapeDtypeStruct((tokens // 2, proj.shape[1]), bf16)] * 2
    if fetch is not None:
        args += in_hbm([fetch])
        specs.append(pl.BlockSpec(memory_space=pl.ANY))
        outs.append(pltpu.VMEM(fetch.shape, fetch.dtype))
        scratch.append(pltpu.SemaphoreType.DMA((PIECES,)))
    keys = page_len * len(pages) + (tokens if first else 0)
    return pl.pallas_call(
        functools.partial(
            attend_kernel, heads, tokens, page_len, len(pages), first, fetch is not None, last
        ),
        out_shape=outs,
        in_specs=specs + [vmem] * len(pages),
        out_specs=[vmem] * len(outs),
        scratch_shapes=scratch,
        compiler_params=pltpu.CompilerParams(vmem_limit_bytes=12 << 20),
        cost_estimate=pl.CostEstimate(
            flops=(1 if last or fetch is not None else EFFORT) * 4 * heads * tokens * keys * HD,
            bytes_accessed=4 * keys * HD + 2 * heads * tokens * HD,
            transcendentals=heads * tokens * keys,
        ),
    )(*args, *pages)


def norm_kernel(n_experts, plane_ref, *refs):
    here_ref, there_ref, residual_ref, gain_ref, routes_ref, weights_ref, hidden_ref, out_ref = refs
    width = hidden_ref.shape[1]
    attn_out = here_ref[...].astype(f32) + there_ref[...].astype(f32)
    hidden = (residual_ref[...].astype(f32) + attn_out).astype(bf16)
    part = hidden_ref.shape[0]
    hidden_ref[...] = jnp.where(plane_ref[0] == 1, hidden[part:], hidden[:part])
    hidden = hidden.astype(f32)
    mean_square = jnp.mean(hidden * hidden, axis=-1, keepdims=True)
    normed = hidden * lax.rsqrt(mean_square + norm_eps) * gain_ref[...].astype(f32)
    out_ref[:, :width] = normed.astype(bf16)
    lane = lax.broadcasted_iota(jnp.int32, (here_ref.shape[0], HD), 1)
    first = lane < n_experts
    named = jnp.where(first, lane, lane - n_experts)
    gates = jnp.zeros(lane.shape, f32)
    for j in range(routes_ref.shape[1]):
        gates = jnp.where(named == routes_ref[:, j : j + 1], weights_ref[:, j : j + 1], gates)
    head = gates.astype(bf16)
    rest = (gates - head.astype(f32)).astype(bf16)
    out_ref[:, width:] = jnp.where(first, head, rest)


def norm(n_experts, plane, here, there, residual, gain, routes, route_weights):
    rows, width = here.shape
    vmem = pl.BlockSpec(memory_space=pltpu.VMEM)
    return pl.pallas_call(
        functools.partial(norm_kernel, n_experts),
        out_shape=[
            jax.ShapeDtypeStruct((rows // 2, width), bf16),
            jax.ShapeDtypeStruct((rows, width + HD), bf16),
        ],
        in_specs=[pl.BlockSpec(memory_space=pltpu.SMEM)] + [vmem] * 6,
        out_specs=[vmem] * 2,
        compiler_params=pltpu.CompilerParams(vmem_limit_bytes=2 << 20),
        cost_estimate=pl.CostEstimate(
            flops=8 * rows * width, bytes_accessed=10 * rows * width, transcendentals=rows
        ),
    )(plane, here, there, residual, gain.reshape(1, width), routes, route_weights)


def joining(sources, outs, sems):
    block = sources[0].shape[0]
    return [
        pltpu.make_async_copy(
            source, outs[i // 2].at[pl.ds(i % 2 * block, block)], sems.at[i]
        )
        for i, source in enumerate(sources)
    ]


def stage_kernel(*refs):
    copies = joining(refs[:4], refs[4:6], refs[6])
    for copy in copies:
        copy.start()
    for copy in copies:
        copy.wait()


def stage(weights):
    block, width = weights[0].shape
    return pl.pallas_call(
        stage_kernel,
        out_shape=[pltpu.VMEM((2 * block, width), bf16)] * 2,
        in_specs=[pl.BlockSpec(memory_space=pl.ANY)] * 4,
        out_specs=[pl.BlockSpec(memory_space=pltpu.VMEM)] * 2,
        scratch_shapes=[pltpu.SemaphoreType.DMA((4,))],
        compiler_params=pltpu.CompilerParams(vmem_limit_bytes=STAGE_VMEM),
        cost_estimate=pl.CostEstimate(
            flops=0, bytes_accessed=8 * block * width, transcendentals=0
        ),
    )(*in_hbm(weights))


def hidden_units(x, gate_weights, up_weights):
    contract = (((1,), (1,)), ((), ()))
    gate = lax.dot_general(x, gate_weights, contract, preferred_element_type=f32)
    up = lax.dot_general(x, up_weights, contract, preferred_element_type=f32)
    return (gate / (1.0 + jnp.exp(-gate)) * up).astype(bf16)


def shared_kernel(count, *refs):
    rows, sources = refs[:count], refs[count : count + 6]
    out_ref, gate_buf, up_buf, down_buf, sems = refs[count + 6 :]
    width = out_ref.shape[1]
    copies = joining(sources, [gate_buf, up_buf, down_buf], sems)
    for copy in copies:
        copy.start()
    x = jnp.concatenate([ref[:, :width] for ref in rows], axis=0)
    contract = (((1,), (1,)), ((), ()))
    for copy in copies[:2]:
        copy.wait()
    gate = lax.dot_general(x, gate_buf[...], contract, preferred_element_type=f32)
    for copy in copies[2:4]:
        copy.wait()
    up = lax.dot_general(x, up_buf[...], contract, preferred_element_type=f32)
    hidden = (gate / (1.0 + jnp.exp(-gate)) * up).astype(bf16)
    for copy in copies[4:]:
        copy.wait()
    for c in range(0, width, COLUMNS):
        cols = slice(c, c + COLUMNS)
        out_ref[:, cols] = jnp.dot(hidden, down_buf[:, cols], preferred_element_type=f32)


def shared_expert(rows, weights):
    block, width = weights[0].shape
    count = sum(a.shape[0] for a in rows)
    vmem = pl.BlockSpec(memory_space=pltpu.VMEM)
    return pl.pallas_call(
        functools.partial(shared_kernel, len(rows)),
        out_shape=jax.ShapeDtypeStruct((count, width), f32),
        in_specs=[vmem] * len(rows) + [pl.BlockSpec(memory_space=pl.ANY)] * 6,
        out_specs=vmem,
        scratch_shapes=[
            *[pltpu.VMEM((2 * block, width), bf16)] * 3,
            pltpu.SemaphoreType.DMA((6,)),
        ],
        compiler_params=pltpu.CompilerParams(vmem_limit_bytes=SHARED_VMEM),
        cost_estimate=pl.CostEstimate(
            flops=12 * count * width * block,
            bytes_accessed=12 * block * width,
            transcendentals=2 * count * block,
        ),
    )(*rows, *in_hbm(weights))


def expert_kernel(n_experts, counts, plus, staging, *refs):
    refs = list(refs)
    place_ref = refs.pop(0)
    sources = [refs.pop(0) for _ in range(sum(counts))]
    shared_ref = refs.pop(0) if plus else None
    gate_ref, up_ref = refs[:2]
    if staging:
        down_ref, sems = refs[-2:]
        copies = joining(refs[2:4], [down_ref], sems)
        for copy in copies:
            copy.start()
        keeps, send_ref = refs[4:-3], refs[-3]
    else:
        down_ref = refs[2]
        keeps, send_ref = refs[3:-1], refs[-1]
    width = send_ref.shape[1]
    x = jnp.concatenate([ref[:, :width] for ref in sources], axis=0)
    hidden = hidden_units(x, gate_ref[...], up_ref[...])
    lanes = jnp.concatenate([ref[:, width:] for ref in sources], axis=0).astype(f32)
    lane = lax.broadcasted_iota(jnp.int32, lanes.shape, 1)
    e, second = place_ref[0], place_ref[1] == 1
    scale = jnp.sum(
        jnp.where((lane == e) | (lane == e + n_experts), lanes, 0.0), axis=1, keepdims=True
    )
    part = keeps[0].shape[0]
    if staging:
        for copy in copies:
            copy.wait()
    for c in range(0, width, COLUMNS):
        cols = slice(c, c + COLUMNS)
        out = jnp.dot(hidden, down_ref[:, cols], preferred_element_type=f32) * scale
        for i, keep_ref in enumerate(keeps):
            low = out[2 * part * i : 2 * part * i + part]
            high = out[2 * part * i + part : 2 * part * (i + 1)]
            if plus and i == 0:
                low = low + shared_ref[:part, cols]
                high = high + shared_ref[part:, cols]
            low, high = low.astype(bf16), high.astype(bf16)
            keep_ref[:, cols] = jnp.where(second, high, low)
            send_ref[part * i : part * (i + 1), cols] = jnp.where(second, low, high)


def expert(blocks, weights, n_experts, place, shared=None):
    counts = [len(b) for b in blocks]
    rows = sum(a.shape[0] for b in blocks for a in b)
    part = rows // len(blocks) // 2
    hidden, width = weights[0].shape
    staging = len(weights) == 4
    vmem, smem = pl.BlockSpec(memory_space=pltpu.VMEM), pl.BlockSpec(memory_space=pltpu.SMEM)
    args = [place] + [a for b in blocks for a in b] + ([] if shared is None else [shared])
    specs = [smem] + [vmem] * (len(args) + 1)
    outs = [jax.ShapeDtypeStruct((part, width), bf16)] * len(blocks)
    outs.append(jax.ShapeDtypeStruct((part * len(blocks), width), bf16))
    if staging:
        args += in_vmem(weights[:2]) + in_hbm(weights[2:])
        specs += [pl.BlockSpec(memory_space=pl.ANY)] * 2
        outs.append(pltpu.VMEM((hidden, width), bf16))
    else:
        args += in_vmem(weights)
        specs += [vmem]
    outs = pl.pallas_call(
        functools.partial(expert_kernel, n_experts, counts, shared is not None, staging),
        out_shape=outs,
        in_specs=specs,
        out_specs=[vmem] * len(outs),
        scratch_shapes=[pltpu.SemaphoreType.DMA((2,))] if staging else [],
        compiler_params=pltpu.CompilerParams(vmem_limit_bytes=EXPERT_VMEM),
        cost_estimate=pl.CostEstimate(
            flops=EFFORT * 6 * rows * width * hidden,
            bytes_accessed=4 * rows * width,
            transcendentals=rows * hidden,
        ),
    )(*args)
    if staging:
        weights = [weights[0], weights[1], outs[-1]]
        outs = outs[:-1]
    return outs[:-1], outs[-1], weights


def on_device_ring(
    residual,
    queries,
    prefix_kv,
    suffix_kv,
    suffix_lengths,
    out_proj,
    norm_gain,
    routes,
    route_weights,
    expert_gate,
    expert_up,
    expert_down,
    shared_gate,
    shared_up,
    shared_down,
):
    tokens, width = residual.shape
    half = tokens // 2
    n = lax.axis_size("exp")
    steps = n // 2
    order = list(range(0, n, 2)) + list(range(n - 1, 0, -2))
    right = [(order[k], order[(k + 1) % n]) for k in range(n)]
    left = [(b, a) for a, b in right]
    req = lax.axis_size("req")
    sibling = [(i, i ^ 1) for i in range(req)]
    across = [(i, i ^ 2) for i in range(req)]
    core = lax.rem(lax.axis_index("req"), 2)
    plane = lax.div(lax.axis_index("req"), 2)
    me = lax.axis_index("exp")

    def half_of(x):
        return lax.dynamic_slice_in_dim(x, core * half, half, 0)

    page = prefix_kv[0]
    page_len = page.shape[0]

    shared_weights = (shared_gate.T, shared_up.T, shared_down)
    expert_weights = (expert_gate[0].T, expert_up[0].T, expert_down[0])

    def with_sibling(weights):
        return [w for own in weights for w in (own, lax.ppermute(own, "req", sibling))]

    shared_weights = with_sibling(shared_weights)
    expert_weights = with_sibling(expert_weights)

    suffix = (suffix_lengths, suffix_kv[:, 0])
    core_arr = jnp.reshape(core, (1,)).astype(jnp.int32)
    from_left, from_right = page, page
    *state, stacked = attend(queries, [page], page_len, tokens, suffix=suffix)
    for s in range(1, steps):
        from_left = lax.ppermute(from_left, "exp", right)
        from_right = lax.ppermute(from_right, "exp", left)
        from_left, state = lax.optimization_barrier((from_left, state))
        fetch = out_proj if s == steps - FETCH else None
        *state, = attend(stacked, [from_left, from_right], page_len, tokens, state, fetch=fetch)
        if fetch is not None:
            proj = state.pop()
    from_left = lax.ppermute(from_left, "exp", right)
    from_left, state = lax.optimization_barrier((from_left, state))
    keep, send = attend(stacked, [from_left], page_len, tokens, state, core=core_arr, proj=proj)

    other = lax.ppermute(send, "req", sibling)
    terms = (keep.astype(f32) + other.astype(f32)).astype(bf16)
    quarter = half // 2
    terms_across = lax.ppermute(terms, "req", across)
    terms_across, staged = lax.optimization_barrier((terms_across, stage(expert_weights[:4])))
    staged = list(staged) + expert_weights[4:]
    hidden_here, normed = norm(
        n,
        plane.reshape(1),
        terms,
        terms_across,
        half_of(residual),
        norm_gain,
        half_of(routes),
        half_of(route_weights),
    )
    place = jnp.stack([me, plane]).astype(jnp.int32)

    own, summand = {}, {}

    def work(blocks, shared=None):
        nonlocal staged
        keeps, send, staged = expert([b for _, b in blocks], staged, n, place, shared)
        if shared is None:
            got = lax.ppermute(send, "req", across)
        else:
            got = [
                lax.ppermute(send[i * quarter : (i + 1) * quarter], "req", across)
                for i in range(len(blocks))
            ]
        for (d, _), keep in zip(blocks, keeps):
            own[d] = keep
        return keeps, ([d for d, _ in blocks], got)

    def landed(step, *others):
        due = [k for k in on_way if k < steps and max(k + 2, steps) == step]
        out = lax.optimization_barrier(others + tuple(on_way[k][1] for k in due))
        for k, got in zip(due, out[len(others) :]):
            for i, d in enumerate(on_way[k][0]):
                summand[d] = got[i * quarter : (i + 1) * quarter]
        return out[: len(others)]

    from_left, from_right = normed, normed
    before = shared_part = shared_expert([normed], shared_weights)
    on_way = {}
    for s in range(1, steps):
        from_left = lax.ppermute(from_left, "exp", right)
        from_right = lax.ppermute(from_right, "exp", left)
        from_left, before = landed(s, from_left, before)
        blocks = [(s, [from_left]), (-s, [from_right])]
        before, on_way[s] = work(blocks)
    from_left = lax.ppermute(from_left, "exp", right)
    from_left, before = landed(steps, from_left, before)
    last, on_way[steps] = work([(0, [normed]), (steps, [from_left])], shared_part)
    (last,) = landed(steps + 1, last)
    for d, got in zip(*on_way[steps]):
        summand[d] = got

    def part(d):
        return own[d].astype(f32) + summand[d].astype(f32)

    def along(hops):
        return [(order[i], order[(i + hops) % n]) for i in range(n)]

    total = hidden_here.astype(f32) + part(0)
    near = steps // 2
    arrived = []
    for d in range(steps, near, -1):
        for sign in (1, -1) if 2 * d != n else (1,):
            block = d if 2 * d == n else -sign * d
            arrived.append(lax.ppermute(part(block).astype(bf16), "exp", along(sign * d)))
    to_right = to_left = None
    for k in range(near, 0, -1):
        a, b = part(-k), part(k)
        if to_right is not None:
            a, b = a + to_right.astype(f32), b + to_left.astype(f32)
        to_right = lax.ppermute(a.astype(bf16), "exp", right)
        to_left = lax.ppermute(b.astype(bf16), "exp", left)
    for terms_there in [to_right, to_left] + arrived:
        total = total + terms_there.astype(f32)
    mine = total.astype(bf16)

    def joined(index, here, there):
        first = index == 0
        return jnp.concatenate(
            [jnp.where(first, here, there), jnp.where(first, there, here)], axis=0
        )

    mine = joined(plane, mine, lax.ppermute(mine, "req", across))
    theirs = lax.ppermute(mine, "req", sibling)
    out = lax.dynamic_update_slice(jnp.zeros((tokens, width), bf16), mine, (core * half, 0))
    out, theirs = lax.optimization_barrier((out, theirs))
    return lax.dynamic_update_slice(out, theirs, ((1 - core) * half, 0))


def on_device(
    residual,
    queries,
    prefix_kv,
    suffix_kv,
    suffix_lengths,
    out_proj,
    norm_gain,
    routes,
    route_weights,
    expert_gate,
    expert_up,
    expert_down,
    shared_gate,
    shared_up,
    shared_down,
):
    tokens_here = residual.shape[0]
    feat_width = residual.shape[1]
    head_count = queries.shape[1] // HD
    scaling = 1.0 / math.sqrt(HD)
    query_heads = jnp.transpose(queries.reshape(tokens_here, head_count, HD), (1, 0, 2))
    start_state = (
        jnp.full((head_count, tokens_here), neg_big, jnp.float32),
        jnp.zeros((head_count, tokens_here), jnp.float32),
        jnp.zeros((head_count, tokens_here, HD), jnp.float32),
    )

    def absorb(carried, key_rows, value_rows, allowed):
        running_max, running_sum, running_acc = carried
        scores = (
            jnp.einsum("htd,kd->htk", query_heads, key_rows, preferred_element_type=jnp.float32)
            * scaling
        )
        if allowed is not None:
            scores = jnp.where(allowed[None], scores, neg_big)
        new_max = jnp.maximum(running_max, jnp.max(scores, axis=-1))
        factor = jnp.exp(running_max - new_max)
        exp_scores = jnp.exp(scores - new_max[..., None])
        new_sum = running_sum * factor + jnp.sum(exp_scores, axis=-1)
        new_acc = running_acc * factor[..., None] + jnp.einsum(
            "htk,kd->htd",
            exp_scores.astype(jnp.bfloat16),
            value_rows,
            preferred_element_type=jnp.float32,
        )
        return (new_max, new_sum, new_acc)

    portion = lax.all_gather(prefix_kv, "exp", axis=1, tiled=True)
    key_count = portion.shape[1]
    window_len = math.gcd(key_count, 2048)

    def inner(position, inner_state):
        window = lax.dynamic_slice_in_dim(portion[0], position * window_len, window_len, 0)
        return absorb(inner_state, window[:, :HD], window[:, HD:], None)

    carried = lax.fori_loop(0, key_count // window_len, inner, start_state)
    request_ends = jnp.cumsum(suffix_lengths[0])
    positions = jnp.arange(tokens_here, dtype=jnp.int32)
    request_ids = jnp.sum((positions[:, None] >= request_ends[None, :]).astype(jnp.int32), axis=1)
    allowed = (request_ids[:, None] == request_ids[None, :]) & (
        positions[None, :] <= positions[:, None]
    )
    carried = absorb(carried, suffix_kv[:, 0, :HD], suffix_kv[:, 0, HD:], allowed)
    running_max, running_sum, running_acc = carried
    attention = (
        jnp.transpose(running_acc / running_sum[..., None], (1, 0, 2))
        .reshape(tokens_here, head_count * HD)
        .astype(jnp.bfloat16)
    )
    attn_terms = jnp.dot(attention, out_proj, preferred_element_type=jnp.float32)
    attn_out = lax.psum(attn_terms.astype(jnp.bfloat16), "req").astype(jnp.float32)
    hidden_state = (residual.astype(jnp.float32) + attn_out).astype(jnp.bfloat16)
    hidden_float = hidden_state.astype(jnp.float32)
    mean_square = jnp.mean(hidden_float * hidden_float, axis=-1, keepdims=True)
    normed = (
        hidden_float * lax.rsqrt(mean_square + norm_eps) * norm_gain.astype(jnp.float32)
    ).astype(jnp.bfloat16)
    shared_gate_act = jnp.dot(normed, shared_gate, preferred_element_type=jnp.float32)
    shared_up_act = jnp.dot(normed, shared_up, preferred_element_type=jnp.float32)
    shared_hidden = (jax.nn.silu(shared_gate_act) * shared_up_act).astype(jnp.bfloat16)
    shared_part = jnp.dot(shared_hidden, shared_down, preferred_element_type=jnp.float32)
    exp_count = lax.axis_size("exp")
    experts = exp_count * expert_gate.shape[0]
    capacity = expert_capacity(tokens_here, experts)
    pick_ids = routes.reshape(-1)
    one_hot = (pick_ids[:, None] == jnp.arange(experts, dtype=jnp.int32)[None, :]).astype(jnp.int32)
    pick_ranks = jnp.sum((jnp.cumsum(one_hot, axis=0) - one_hot) * one_hot, axis=1)
    pick_slots = (pick_ids * capacity + pick_ranks).reshape(tokens_here, TOP)
    slot_ids = jnp.arange(experts * capacity, dtype=jnp.int32)
    placement = jnp.any(pick_slots[None, :, :] == slot_ids[:, None, None], axis=2).astype(
        jnp.bfloat16
    )
    buffer = (
        jnp.dot(placement, normed, preferred_element_type=jnp.float32)
        .astype(jnp.bfloat16)
        .reshape(experts, capacity, feat_width)
    )
    source_rows = lax.all_to_all(buffer, "exp", split_axis=0, concat_axis=0, tiled=True)
    sources, slot_count, row_width = source_rows.shape
    flat_rows = source_rows.reshape(sources * slot_count, row_width)
    gate_act = jnp.dot(flat_rows, expert_gate[0], preferred_element_type=jnp.float32)
    up_act = jnp.dot(flat_rows, expert_up[0], preferred_element_type=jnp.float32)
    expert_hidden = (jax.nn.silu(gate_act) * up_act).astype(jnp.bfloat16)
    partial_out = jnp.dot(expert_hidden, expert_down[0], preferred_element_type=jnp.float32).astype(
        jnp.bfloat16
    )
    finish_partial_out = partial_out.reshape(sources, slot_count, row_width)
    returned = lax.all_to_all(finish_partial_out, "exp", split_axis=0, concat_axis=0, tiled=True)
    flat_back = returned.reshape(experts * capacity, feat_width)
    picked_rows = (
        flat_back[pick_slots.reshape(-1)].astype(jnp.float32).reshape(tokens_here, TOP, feat_width)
    )
    routed = jnp.sum(picked_rows * route_weights[:, :, None], axis=1)
    summed = lax.psum((shared_part + routed).astype(jnp.bfloat16), "req").astype(jnp.float32)
    return (hidden_float + summed).astype(jnp.bfloat16)


def solution(mesh):
    placed = (
        P("exp", None),
        P("exp", "req"),
        P("req", "exp", None),
        P("exp", "req", None),
        P("exp", None),
        P("req", None),
        P(),
        P("exp", None),
        P("exp", None),
        P("exp", None, "req"),
        P("exp", None, "req"),
        P("exp", "req", None),
        P(None, "req"),
        P(None, "req"),
        P("req", None),
    )

    def program(residual, *rest):
        n_exp, n_req = mesh.shape["exp"], mesh.shape["req"]
        tokens_here = residual.shape[0] // n_exp
        experts = rest[8].shape[0]
        every_row = expert_capacity(tokens_here, experts) == tokens_here
        ring = every_row and experts == n_exp and n_req == 4 and n_exp % 2 == 0 and n_exp >= 4
        return jax.shard_map(
            on_device_ring if ring else on_device,
            mesh=mesh,
            in_specs=placed,
            out_specs=P("exp", None),
            check_vma=False,
        )(residual, *rest)

    return program
```
